128 devices in a mesh: seq: 32 (over y, x_lo, z), fsdp: 4 (over x_hi, core).
Axes of the slice: x: 4 (x_hi: 2, x_lo: 2; x = x_hi * 2 + x_lo), y: 4, z: 4, core: 2. Of those that a mesh axis runs over, the one named last changes fastest.
Arguments:
- tokens: float32 [4, 8192, 1024], P('fsdp', 'seq'), may hold values from -6 to 6
- cotangent: float32 [4, 8192, 1024], P('fsdp', 'seq'), may hold values from -6 to 6
- norm1_gain: bfloat16 [1024], P(('seq', 'fsdp')), may hold values from 0.099609375 to 1.8984375
- in_weight: bfloat16 [1024, 3072], P(('seq', 'fsdp')), may hold values from -0.1875 to 0.1875
- conv_taps: bfloat16 [3, 1024], P(None, ('seq', 'fsdp')), may hold values from -3.5 to 3.5
- out_weight: bfloat16 [1024, 1024], P(('seq', 'fsdp')), may hold values from -0.1875 to 0.1875
- norm2_gain: bfloat16 [1024], P(('seq', 'fsdp')), may hold values from 0.099609375 to 1.8984375
- gate_weight: bfloat16 [1024, 4608], P(('seq', 'fsdp')), may hold values from -0.1875 to 0.1875
- up_weight: bfloat16 [1024, 4608], P(('seq', 'fsdp')), may hold values from -0.1875 to 0.1875
- down_weight: bfloat16 [4608, 1024], P(('seq', 'fsdp')), may hold values from -0.09375 to 0.09375
Outputs:
- block_out: float32 [4, 8192, 1024], P('fsdp', 'seq')
- input_grad: float32 [4, 8192, 1024], P('fsdp', 'seq')
- norm1_gain_grad: float32 [1024], P(('seq', 'fsdp'))
- in_weight_grad: float32 [1024, 3072], P(('seq', 'fsdp'))
- conv_taps_grad: float32 [3, 1024], P(None, ('seq', 'fsdp'))
- out_weight_grad: float32 [1024, 1024], P(('seq', 'fsdp'))
- norm2_gain_grad: float32 [1024], P(('seq', 'fsdp'))
- gate_weight_grad: float32 [1024, 4608], P(('seq', 'fsdp'))
- up_weight_grad: float32 [1024, 4608], P(('seq', 'fsdp'))
- down_weight_grad: float32 [4608, 1024], P(('seq', 'fsdp'))
The draws below stay inside these ranges and needn't reach their ends.
All inputs are finite; a program needn't handle non-finite values.
Results may differ from the reference program's by a relative error of at most 0.0097.
Values may be sent and summed in bfloat16 or wider, within the bound.
A program may use at most 128 MiB of HBM per device.

```python
import math
import jax
import jax.numpy as jnp
from jax import lax

D = 1024
FF = 4608
KERNEL = 3
LEN = 8192
SEQS = 4


def strengthened(entries, stream_key, source, target, parts, factor):
    def block_of(dim):
        return (jnp.arange(entries.shape[dim]) // (entries.shape[dim] // parts)).reshape((-1,) + (1,) * (entries.ndim - 1 - dim))

    near = jax.random.permutation(stream_key, parts)[block_of(target)]
    second = (block_of(target) + parts // 2) % parts
    return jnp.where((block_of(source) == near) | (block_of(source) == second), factor * entries, entries)


def block_scale(own_key, extent, cuts, low, top_value):
    factor_of, own = 1.0, jax.random.fold_in(own_key, 6)
    for dim, blocks in cuts:
        heights = jnp.exp(jax.random.uniform(jax.random.fold_in(own, dim), (blocks,), jnp.float32, low / len(cuts), top_value / len(cuts)))
        factor_of = factor_of * jnp.repeat(heights, extent[dim] // blocks).reshape([-1 if axis == dim else 1 for axis in range(len(extent))])
    return factor_of


def scatter_about(stream_key, extent, scale, limit, shards=(), kind=jnp.bfloat16):
    array = jax.random.normal(stream_key, extent, jnp.float32) * scale
    if len(shards) > 0:
        array = block_scale(stream_key, extent, shards, -0.22, 0.18) * array
    return jnp.clip(array, min=-limit, max=limit).astype(kind)


def gaussian_with(key, extent, deviation, bound, pieces, heavy, held_as=jnp.bfloat16):
    entries = deviation * jax.random.normal(key, extent, jnp.float32)
    if pieces:
        entries = entries * block_scale(key, extent, pieces, -0.22, 0.18)
    return jnp.clip(strengthened(entries, jax.random.fold_in(key, 3), *heavy), -bound, bound).astype(held_as)


def setup_inputs(seed: int = 0) -> dict:
    arg_keys = jax.random.split(jax.random.key(seed), 11)
    return {
        "tokens": gaussian_with(arg_keys[0], (SEQS, LEN, D), 1.0, 6.0, ((0, 4), (1, 32)), (1, 2, 32, 2.75), jnp.float32),
        "cotangent": scatter_about(arg_keys[1], (SEQS, LEN, D), 1.0, 6.0, ((0, 4), (1, 32)), jnp.float32),
        "norm1_gain": jnp.clip(1.0 + 0.18 * jax.random.normal(arg_keys[2], (D,), jnp.float32), 0.099609375, 1.8984375).astype(jnp.bfloat16),
        "in_weight": scatter_about(arg_keys[3], (D, 3 * D), D ** -0.5, 0.1875, ((0, 128),)),
        "conv_taps": scatter_about(arg_keys[4], (KERNEL, D), KERNEL ** -0.5, 3.5, ((1, 128),)),
        "out_weight": scatter_about(arg_keys[5], (D, D), D ** -0.5, 0.1875, ((0, 128),)),
        "norm2_gain": jnp.clip(1.0 + 0.18 * jax.random.normal(arg_keys[6], (D,), jnp.float32), 0.099609375, 1.8984375).astype(jnp.bfloat16),
        "gate_weight": scatter_about(arg_keys[7], (D, FF), D ** -0.5, 0.1875, ((0, 128),)),
        "up_weight": scatter_about(arg_keys[8], (D, FF), D ** -0.5, 0.1875, ((0, 128),)),
        "down_weight": scatter_about(arg_keys[9], (FF, D), FF ** -0.5, 0.09375, ((0, 128),)),
    }


norm_eps = 1e-05

def rms_inverse(values):
    return lax.rsqrt(lax.optimization_barrier(jnp.mean(values * values, axis=-1, keepdims=True)) + norm_eps)

def one_sequence(weights, inputs, upstream):
    gain_one, w_inproj, taps, w_outproj, gain_two, w_gate, w_upproj, w_down = weights
    width = inputs.shape[-1]
    inv_one = rms_inverse(inputs)
    normed_one = inputs * inv_one
    hidden_one = (normed_one * gain_one).astype(jnp.bfloat16)
    projected = jnp.dot(hidden_one, w_inproj, preferred_element_type=jnp.float32)
    b_mat = projected[:, :width]
    c_mat = projected[:, width:2 * width]
    x_mat = projected[:, 2 * width:]
    gated_in = b_mat * x_mat
    padded = jnp.concatenate([jnp.zeros((2, width), jnp.float32), gated_in], axis=0)
    convolved = taps[0] * padded[:-2] + taps[1] * padded[1:-1] + taps[2] * padded[2:]
    y_mat = (c_mat * convolved).astype(jnp.bfloat16)
    resid = inputs + jnp.dot(y_mat, w_outproj, preferred_element_type=jnp.float32)
    inv_two = rms_inverse(resid)
    normed_two = resid * inv_two
    hidden_two = (normed_two * gain_two).astype(jnp.bfloat16)
    gate = jnp.dot(hidden_two, w_gate, preferred_element_type=jnp.float32)
    up_vals = jnp.dot(hidden_two, w_upproj, preferred_element_type=jnp.float32)
    sigma_gate = jax.nn.sigmoid(gate)
    activated = (gate * sigma_gate * up_vals).astype(jnp.bfloat16)
    block_out = resid + jnp.dot(activated, w_down, preferred_element_type=jnp.float32)
    cot_half = upstream.astype(jnp.bfloat16)
    grad_down = jnp.dot(activated.T, cot_half, preferred_element_type=jnp.float32)
    d_act = jnp.dot(cot_half, w_down.T, preferred_element_type=jnp.float32)
    d_gate = (d_act * up_vals * sigma_gate * (1.0 + gate * (1.0 - sigma_gate))).astype(jnp.bfloat16)
    d_upvals = (d_act * gate * sigma_gate).astype(jnp.bfloat16)
    grad_gate = jnp.dot(hidden_two.T, d_gate, preferred_element_type=jnp.float32)
    grad_up = jnp.dot(hidden_two.T, d_upvals, preferred_element_type=jnp.float32)
    d_hidden_two = jnp.dot(d_gate, w_gate.T, preferred_element_type=jnp.float32) + jnp.dot(d_upvals, w_upproj.T, preferred_element_type=jnp.float32)
    grad_gain_two = lax.optimization_barrier(jnp.sum(d_hidden_two * normed_two, axis=0))
    scaled_two = d_hidden_two * gain_two
    d_resid = upstream + inv_two * (scaled_two - normed_two * lax.optimization_barrier(jnp.mean(scaled_two * normed_two, axis=-1, keepdims=True)))
    dres_half = d_resid.astype(jnp.bfloat16)
    grad_out = jnp.dot(y_mat.T, dres_half, preferred_element_type=jnp.float32)
    d_ymat = jnp.dot(dres_half, w_outproj.T, preferred_element_type=jnp.float32)
    d_cmat = d_ymat * convolved
    d_conv = d_ymat * c_mat
    grad_taps = jnp.stack([lax.optimization_barrier(jnp.sum(d_conv * padded[:-2], axis=0)), lax.optimization_barrier(jnp.sum(d_conv * padded[1:-1], axis=0)), lax.optimization_barrier(jnp.sum(d_conv * padded[2:], axis=0))])
    dconv_pad = jnp.concatenate([d_conv, jnp.zeros((2, width), jnp.float32)], axis=0)
    d_gated = taps[0] * dconv_pad[2:] + taps[1] * dconv_pad[1:-1] + taps[2] * dconv_pad[:-2]
    d_proj = jnp.concatenate([d_gated * x_mat, d_cmat, d_gated * b_mat], axis=1).astype(jnp.bfloat16)
    grad_in = jnp.dot(hidden_one.T, d_proj, preferred_element_type=jnp.float32)
    d_hidden_one = jnp.dot(d_proj, w_inproj.T, preferred_element_type=jnp.float32)
    grad_gain_one = lax.optimization_barrier(jnp.sum(d_hidden_one * normed_one, axis=0))
    scaled_one = d_hidden_one * gain_one
    input_grad = d_resid + inv_one * (scaled_one - normed_one * lax.optimization_barrier(jnp.mean(scaled_one * normed_one, axis=-1, keepdims=True)))
    grads = (grad_gain_one, grad_in, grad_taps, grad_out, grad_gain_two, grad_gate, grad_up, grad_down)
    return (block_out, input_grad, grads)

def reference(tokens, cotangent, norm1_gain, in_weight, conv_taps, out_weight, norm2_gain, gate_weight, up_weight, down_weight):
    weights = (norm1_gain.astype(jnp.float32), in_weight, conv_taps.astype(jnp.float32), out_weight, norm2_gain.astype(jnp.float32), gate_weight, up_weight, down_weight)
    zeros = (jnp.zeros(norm1_gain.shape, jnp.float32), jnp.zeros(in_weight.shape, jnp.float32), jnp.zeros(conv_taps.shape, jnp.float32), jnp.zeros(out_weight.shape, jnp.float32), jnp.zeros(norm2_gain.shape, jnp.float32), jnp.zeros(gate_weight.shape, jnp.float32), jnp.zeros(up_weight.shape, jnp.float32), jnp.zeros(down_weight.shape, jnp.float32))

    def step_fn(carry, pair):
        block_out, input_grad, grads = one_sequence(weights, pair[0], pair[1])
        carry = tuple((total + part for total, part in zip(carry, grads)))
        return (carry, (block_out, input_grad))
    totals, outputs = lax.scan(step_fn, zeros, (tokens, cotangent))
    factor = 1.0 / math.sqrt(tokens.shape[0] * tokens.shape[1])
    totals = tuple((total * factor for total in totals))
    return (outputs[0], outputs[1], totals[0], totals[1], totals[2], totals[3], totals[4], totals[5], totals[6], totals[7])
```

```python
import math

import jax
import jax.numpy as jnp
from jax import lax
from jax.experimental import pallas as pl
from jax.experimental.pallas import tpu as pltpu
from jax.sharding import PartitionSpec as P

norm_eps = 1e-05
MESH = pl.DeviceIdType.MESH
F32, BF16 = jnp.float32, jnp.bfloat16

CHIPS = (4, 2, 4, 2)
ARRAYS = (
    ((16, 640), "xyz"),
    ((16, 512), "yzx"),
    ((16, 1024), "zxy"),
    ((16, 2304), "xyz"),
    ((16, 2304), "yzx"),
    ((72, 512), "zxy"),
)


def position():
    s, f = lax.axis_index("seq"), lax.axis_index("fsdp")
    y, x_lo, z = lax.div(s, 8), lax.rem(lax.div(s, 4), 2), lax.rem(s, 4)
    x_hi, core = lax.div(f, 2), lax.rem(f, 2)
    return {"x": x_hi * 2 + x_lo, "y": y, "z": z}, core


def device(at, core):
    x_lo, x_hi = lax.rem(at["x"], 2), lax.div(at["x"], 2)
    return ((at["y"] * 2 + x_lo) * 4 + at["z"], x_hi * 2 + core)


def moved(at, axis, by):
    return {**at, axis: lax.rem(at[axis] + by, 4)}


def chip_index(at, whole):
    y = slice(None) if "y" in whole else pl.ds(at["y"], 1)
    z = slice(None) if "z" in whole else pl.ds(at["z"], 1)
    if "x" in whole:
        x_lo = x_hi = slice(None)
    else:
        x_lo, x_hi = pl.ds(lax.rem(at["x"], 2), 1), pl.ds(lax.div(at["x"], 2), 1)
    return (y, x_lo, z, x_hi)


def halves(columns):
    first = (columns // 128 + 1) // 2 * 128
    return slice(0, first), slice(first, columns)


def enter(at, core):
    barrier = pltpu.get_barrier_semaphore()
    for axis in "xyz":
        for by in (1, 3):
            pl.semaphore_signal(
                barrier, inc=1, device_id=device(moved(at, axis, by), core), device_id_type=MESH
            )
    pl.semaphore_signal(barrier, inc=1, device_id=device(at, 1 - core), device_id_type=MESH)
    pl.semaphore_wait(barrier, 7)


def remote(src, dst, sends, recvs, target, sem):
    return pltpu.make_async_remote_copy(
        src_ref=src,
        dst_ref=dst,
        send_sem=sends.at[sem],
        recv_sem=recvs.at[sem],
        device_id=target,
        device_id_type=MESH,
    )


def gather_kernel(*refs):
    count = len(ARRAYS)
    shards, (tok, cot) = refs[:count], refs[count : count + 2]
    full = refs[count + 2 : 2 * count + 2]
    out_half, down_half, tok_pair, cot_pair = refs[2 * count + 2 : 2 * count + 6]
    theirs = refs[2 * count + 6 : 3 * count + 6]
    block = refs[3 * count + 6 : 4 * count + 6]
    sends, recvs, local = refs[4 * count + 6 :]
    at, core = position()
    sibling = device(at, 1 - core)
    enter(at, core)
    sent, kept = [], []

    swaps = []
    for k in range(count):
        copy = remote(shards[k].at[1 - core], theirs[k], sends, recvs, sibling, 12 * count + k)
        copy.start()
        swaps.append(copy)
    pairs = []
    for k, (src, dst) in enumerate(((tok, tok_pair), (cot, cot_pair))):
        copy = remote(src, dst.at[core], sends, recvs, sibling, 13 * count + k)
        copy.start()
        pairs.append(copy)
        own = pltpu.make_async_copy(src, dst.at[core], local.at[count + k])
        own.start()
        kept.append(own)

    def send(k, src, dst, target, sem):
        copy = remote(src, dst, sends, recvs, target, sem)
        copy.start()
        sent.append(copy)

    def arrived(ref, sem):
        remote(ref, ref, sends, recvs, sibling, sem).wait_recv()

    own_copies = []
    for k in range(count):
        swaps[k].wait_recv()
        block[k][...] = shards_value(shards[k], core) + theirs[k][...]
        own = pltpu.make_async_copy(
            block[k], full[k].at[lax.div(lax.rem(at["y"], 4), 1), lax.rem(at["x"], 2), at["z"], lax.div(at["x"], 2)], local.at[k]
        )
        own.start()
        own_copies.append(own)
        axis = ARRAYS[k][1][0]
        here = (at["y"], lax.rem(at["x"], 2), at["z"], lax.div(at["x"], 2))
        base = 12 * k
        send(k, block[k], full[k].at[here], device(moved(at, axis, 1), core), base)
        send(k, block[k], full[k].at[here], device(moved(at, axis, 3), core), base + 1)

    for phase in range(3):
        for k, ((_, columns), order) in enumerate(ARRAYS):
            axis, whole, base = order[phase], order[:phase], 12 * k + 4 * phase
            first, second = halves(columns)
            right, left = moved(at, axis, 1), moved(at, axis, 3)
            from_left = full[k].at[chip_index(left, whole)]
            arrived(from_left, base)
            part = full[k].at[(*chip_index(left, whole), slice(None), first)]
            send(k, part, part, device(right, core), base + 2)
            from_right = full[k].at[chip_index(right, whole)]
            arrived(from_right, base + 1)
            part = full[k].at[(*chip_index(right, whole), slice(None), second)]
            send(k, part, part, device(left, core), base + 3)
        for k, ((_, columns), order) in enumerate(ARRAYS):
            axis, whole, base = order[phase], order[:phase], 12 * k + 4 * phase
            first, second = halves(columns)
            across = moved(at, axis, 2)
            arrived(full[k].at[(*chip_index(across, whole), slice(None), first)], base + 2)
            arrived(full[k].at[(*chip_index(across, whole), slice(None), second)], base + 3)
            if phase == 0:
                own_copies[k].wait()
            if phase < 2:
                axis, whole, base = order[phase + 1], order[: phase + 1], base + 4
                mine = full[k].at[chip_index(at, whole)]
                send(k, mine, mine, device(moved(at, axis, 1), core), base)
                send(k, mine, mine, device(moved(at, axis, 3), core), base + 1)
            elif k in (2, 5):
                columns = slice(512, 1024) if k == 2 else slice(0, 512)
                dst = out_half if k == 2 else down_half
                rest = (slice(None),) * 4
                mine = full[k].at[(pl.ds(2 * core, 2), *rest, columns)]
                other = full[k].at[(pl.ds(2 - 2 * core, 2), *rest, columns)]
                copy = remote(other, dst.at[core], sends, recvs, sibling, 13 * count + k)
                copy.start()
                pairs.append(copy)
                own = pltpu.make_async_copy(mine, dst.at[core], local.at[count + k])
                own.start()
                kept.append(own)

    for copy in sent:
        copy.wait_send()
    for copy in swaps:
        copy.wait_send()
    for copy in pairs:
        copy.wait()
    for copy in kept:
        copy.wait()


def shards_value(ref, core):
    return jnp.where(core == 0, ref[0], ref[1])


def gather(shards, tok, cot):
    count = len(ARRAYS)
    hbm, vmem = pl.BlockSpec(memory_space=pl.ANY), pl.BlockSpec(memory_space=pltpu.VMEM)
    outs = [jax.ShapeDtypeStruct((*CHIPS, *shape), BF16) for shape, _ in ARRAYS]
    outs += [
        jax.ShapeDtypeStruct((2, 2, 2, 4, 2, 16, 512), BF16),
        jax.ShapeDtypeStruct((2, 2, 2, 4, 2, 72, 512), BF16),
        jax.ShapeDtypeStruct((2, *tok.shape), F32),
        jax.ShapeDtypeStruct((2, *cot.shape), F32),
    ]
    blocks = [pltpu.VMEM(shape, BF16) for shape, _ in ARRAYS]
    return pl.pallas_call(
        gather_kernel,
        out_shape=outs,
        in_specs=[vmem] * count + [hbm] * 2,
        out_specs=[hbm] * len(outs),
        scratch_shapes=[
            *blocks,
            *blocks,
            pltpu.SemaphoreType.DMA((14 * count,)),
            pltpu.SemaphoreType.DMA((14 * count,)),
            pltpu.SemaphoreType.DMA((2 * count,)),
        ],
        compiler_params=pltpu.CompilerParams(
            collective_id=0, has_side_effects=True, vmem_limit_bytes=24 * 2**20
        ),
        name="gather_weights",
    )(*shards, tok, cot)


def reduce_kernel(*refs):
    count = len(ARRAYS)
    grads, (out_grad, down_grad) = refs[: count - 1], refs[count - 1 : count + 1]
    totals = refs[count + 1 : 2 * count + 1]
    data = refs[2 * count + 1 : 3 * count + 1]
    arriving = refs[3 * count + 1 : 15 * count + 1]
    sends, recvs, local = refs[15 * count + 1 :]
    at, core = position()
    sibling = device(at, 1 - core)
    enter(at, core)
    sent = []
    rest = (slice(None),) * 4

    def buffer(k, phase, which):
        return arriving[12 * k + 4 * phase + which]

    def send(src, dst, target, sem):
        copy = remote(src, dst, sends, recvs, target, sem)
        copy.start()
        sent.append(copy)

    def arrived(ref, sem):
        remote(ref, ref, sends, recvs, sibling, sem).wait_recv()

    loads = [[] for _ in range(count)]
    for k in range(count):
        if k < count - 1:
            dst = data[k].at[(*rest, slice(None), slice(0, 512))] if k == 2 else data[k]
            copy = pltpu.make_async_copy(grads[k], dst, local.at[k])
            copy.start()
            loads[k].append(copy)
        if k in (2, 5):
            columns = slice(512, 1024) if k == 2 else slice(0, 512)
            src = out_grad if k == 2 else down_grad
            dst = data[k].at[(pl.ds(2 * core, 2), *rest, columns)]
            copy = pltpu.make_async_copy(src.at[core], dst, local.at[count + k])
            copy.start()
            loads[k].append(copy)
            send(src.at[1 - core], dst, sibling, 12 * count + k)

    def add_part(k, into, source, where, leads, columns):
        sizes = source.shape[:4]

        def body(t, carry):
            i3 = lax.rem(t, sizes[3])
            t3 = lax.div(t, sizes[3])
            i2 = lax.rem(t3, sizes[2])
            t2 = lax.div(t3, sizes[2])
            i1 = lax.rem(t2, sizes[1])
            i0 = lax.div(t2, sizes[1])
            spot = tuple(i + b for i, b in zip((i0, i1, i2, i3), where))
            value = into[(*spot, slice(None), columns)].astype(F32)
            value = value + source[i0, i1, i2, i3].astype(F32)
            into[(*spot, slice(None), columns)] = value.astype(BF16)
            return carry

        lax.fori_loop(0, math.prod(sizes), body, 0)

    def add_both(k, into, one, two, where, total):
        sizes = one.shape[:4]

        def body(t, carry):
            i3 = lax.rem(t, sizes[3])
            t3 = lax.div(t, sizes[3])
            i2 = lax.rem(t3, sizes[2])
            t2 = lax.div(t3, sizes[2])
            i1 = lax.rem(t2, sizes[1])
            i0 = lax.div(t2, sizes[1])
            spot = tuple(i + b for i, b in zip((i0, i1, i2, i3), where))
            value = into[spot].astype(F32) + one[i0, i1, i2, i3].astype(F32)
            value = value + two[i0, i1, i2, i3].astype(F32)
            if total is None:
                into[spot] = value.astype(BF16)
            else:
                total[...] = value
            return carry

        lax.fori_loop(0, math.prod(sizes), body, 0)

    def start_of(position_, whole):
        y = 0 if "y" in whole else position_["y"]
        z = 0 if "z" in whole else position_["z"]
        if "x" in whole:
            return (y, 0, z, 0)
        return (y, lax.rem(position_["x"], 2), z, lax.div(position_["x"], 2))

    def first_sends(k, phase):
        (_, columns), order = ARRAYS[k]
        axis, whole = order[2 - phase], order[: 2 - phase]
        first, second = halves(columns)
        across = chip_index(moved(at, axis, 2), whole)
        base = 12 * k + 4 * phase
        for part, which, by in ((first, 0, 1), (second, 1, 3)):
            send(
                data[k].at[(*across, slice(None), part)],
                buffer(k, phase, which),
                device(moved(at, axis, by), core),
                base + which,
            )

    for k in range(count):
        for copy in loads[k]:
            copy.wait()
        if k in (2, 5):
            columns = slice(512, 1024) if k == 2 else slice(0, 512)
            arrived(data[k].at[(pl.ds(2 - 2 * core, 2), *rest, columns)], 12 * count + k)
        first_sends(k, 0)

    for phase in range(3):
        for k, ((_, columns), order) in enumerate(ARRAYS):
            axis, whole = order[2 - phase], order[: 2 - phase]
            base = 12 * k + 4 * phase
            for part, which, by in zip(halves(columns), (0, 1), (1, 3)):
                near = moved(at, axis, by)
                arrived(buffer(k, phase, which), base + which)
                add_part(k, data[k], buffer(k, phase, which), start_of(near, whole), None, part)
                send(
                    data[k].at[chip_index(near, whole)],
                    buffer(k, phase, 2 + which),
                    device(near, core),
                    base + 2 + which,
                )
        for k, ((_, columns), order) in enumerate(ARRAYS):
            axis, whole = order[2 - phase], order[: 2 - phase]
            base = 12 * k + 4 * phase
            arrived(buffer(k, phase, 2), base + 2)
            arrived(buffer(k, phase, 3), base + 3)
            last = phase == 2
            mine = totals[k].at[core] if last else None
            add_both(k, data[k], buffer(k, phase, 2), buffer(k, phase, 3), start_of(at, whole), mine)
            if not last:
                first_sends(k, phase + 1)
            else:
                send(mine, mine, sibling, 13 * count + k)
    for k in range(count):
        arrived(totals[k].at[1 - core], 13 * count + k)
    for copy in sent:
        copy.wait_send()


def reduce(grads, out_grad, down_grad):
    count = len(ARRAYS)
    hbm, vmem = pl.BlockSpec(memory_space=pl.ANY), pl.BlockSpec(memory_space=pltpu.VMEM)
    buffers = []
    for (rows, columns), order in ARRAYS:
        for phase in range(3):
            whole = order[: 2 - phase]
            lead = (
                4 if "y" in whole else 1,
                2 if "x" in whole else 1,
                4 if "z" in whole else 1,
                2 if "x" in whole else 1,
            )
            for part in halves(columns):
                buffers.append(pltpu.VMEM((*lead, rows, part.stop - part.start), BF16))
            buffers += [pltpu.VMEM((*lead, rows, columns), BF16)] * 2
    return pl.pallas_call(
        reduce_kernel,
        out_shape=[jax.ShapeDtypeStruct((2, *shape), F32) for shape, _ in ARRAYS],
        in_specs=[hbm] * (count + 1),
        out_specs=[vmem] * count,
        scratch_shapes=[
            *[pltpu.VMEM((*CHIPS, *shape), BF16) for shape, _ in ARRAYS],
            *buffers,
            pltpu.SemaphoreType.DMA((14 * count,)),
            pltpu.SemaphoreType.DMA((14 * count,)),
            pltpu.SemaphoreType.DMA((2 * count,)),
        ],
        compiler_params=pltpu.CompilerParams(
            collective_id=1, has_side_effects=True, vmem_limit_bytes=52 * 2**20
        ),
        name="sum_gradients",
    )(*grads, out_grad, down_grad)


def rms_inverse(values):
    return lax.rsqrt(jnp.mean(values * values, axis=-1, keepdims=True) + norm_eps)


def dot(a, b):
    return jnp.dot(a, b, preferred_element_type=F32)


def dot_t(a, b):
    return lax.dot_general(a, b, (((1,), (1,)), ((), ())), preferred_element_type=F32)


def t_dot(a, b):
    return lax.dot_general(a, b, (((0,), (0,)), ((), ())), preferred_element_type=F32)


def swap_pair(value):
    return lax.ppermute(value, "fsdp", [(0, 1), (1, 0), (2, 3), (3, 2)])


def shifted(value, by):
    peers = lax.axis_size("seq")
    return lax.ppermute(
        value, "seq", [(i, i + by) for i in range(peers) if 0 <= i + by < peers]
    )


def rows_for_pair(shard, core):
    rows = shard.shape[0]
    both = jnp.concatenate([shard, shard], axis=0)
    mine = lax.broadcasted_iota(jnp.int32, both.shape, 0) // rows == core
    return jnp.where(mine, both, jnp.zeros_like(both))


def shards(
    tokens,
    cotangent,
    norm1_gain,
    in_weight,
    conv_taps,
    out_weight,
    norm2_gain,
    gate_weight,
    up_weight,
    down_weight,
):
    width = tokens.shape[-1]
    inputs = tokens.reshape(-1, width)
    upstream = cotangent.reshape(-1, width)
    rows = inputs.shape[0]
    total_rows = rows * lax.axis_size("seq") * lax.axis_size("fsdp")
    factor = 1.0 / math.sqrt(total_rows)
    core = lax.rem(lax.axis_index("fsdp"), 2)

    small = jnp.concatenate(
        [norm1_gain[:, None], norm2_gain[:, None], conv_taps.T, jnp.zeros((8, 123), BF16)], axis=1
    )

    def by_half(*columns):
        return jnp.stack(
            [
                rows_for_pair(
                    jnp.concatenate(
                        [
                            c if c.shape[1] == 128 else c[:, h * c.shape[1] // 2 : (h + 1) * c.shape[1] // 2]
                            for c in columns
                        ],
                        axis=1,
                    ),
                    core,
                )
                for h in range(2)
            ]
        )

    b_w, c_w, x_w = in_weight[:, :width], in_weight[:, width : 2 * width], in_weight[:, 2 * width :]
    pieces = (
        by_half(b_w, small),
        by_half(c_w),
        by_half(x_w, out_weight),
        by_half(gate_weight),
        by_half(up_weight),
        by_half(down_weight),
    )
    full0, full1, full2, w_gate, w_up, _, w_out, w_down, tok, cot = gather(pieces, inputs, upstream)
    full0 = full0.reshape(width, -1)
    w_b, small = full0[:, :512], full0[:, 512:].T.astype(F32)
    w_c = full1.reshape(width, -1)
    w_x = full2.reshape(width, -1)[:, :512]
    w_gate = w_gate.reshape(width, -1)
    w_up = w_up.reshape(width, -1)
    w_out = w_out.reshape(2, 512, 512)
    w_down = w_down.reshape(2, 2304, 512)
    gain_one, gain_two = small[0], small[1]
    taps = lax.dynamic_slice_in_dim(small[2:5], core * 512, 512, axis=1)
    tok, cot = tok.reshape(-1, width), cot.reshape(-1, width)

    inv_one = rms_inverse(tok)
    normed_one = tok * inv_one
    hidden_one = (normed_one * gain_one).astype(BF16)
    b_mat, c_mat, x_mat = dot(hidden_one, w_b), dot(hidden_one, w_c), dot(hidden_one, w_x)
    gated = (b_mat * x_mat).reshape(2, rows, 512)
    padded = jnp.concatenate([shifted(gated[:, -2:], 1), gated], axis=1)
    convolved = taps[0] * padded[:, :-2] + taps[1] * padded[:, 1:-1] + taps[2] * padded[:, 2:]
    convolved = convolved.reshape(-1, 512)
    y_mat = (c_mat * convolved).astype(BF16)

    mixed = jnp.concatenate([dot(y_mat, w_out[0]), dot(y_mat, w_out[1])], axis=1)
    resid = tok + (mixed + swap_pair(mixed))
    inv_two = rms_inverse(resid)
    normed_two = resid * inv_two
    hidden_two = (normed_two * gain_two).astype(BF16)
    gate, up_vals = dot(hidden_two, w_gate), dot(hidden_two, w_up)
    sigma = jax.nn.sigmoid(gate)
    act = (gate * sigma * up_vals).astype(BF16)
    out_part = jnp.concatenate([dot(act, w_down[0]), dot(act, w_down[1])], axis=1)

    def own(value):
        return lax.dynamic_slice_in_dim(value, core * rows, rows, axis=0)

    def others(value):
        return lax.dynamic_slice_in_dim(value, (1 - core) * rows, rows, axis=0)

    block_out = own(resid) + (own(out_part) + swap_pair(others(out_part)))

    cot_half = cot.astype(BF16)
    g_down = jnp.stack([t_dot(act, cot_half[:, :512]), t_dot(act, cot_half[:, 512:])]).astype(BF16)
    d_act = dot_t(cot_half[:, :512], w_down[0]) + dot_t(cot_half[:, 512:], w_down[1])
    d_gate = (d_act * up_vals * sigma * (1.0 + gate * (1.0 - sigma))).astype(BF16)
    d_up = (d_act * gate * sigma).astype(BF16)
    g_gate = t_dot(hidden_two, d_gate).astype(BF16)
    g_up = t_dot(hidden_two, d_up).astype(BF16)
    d_hid2 = dot_t(d_gate, w_gate) + dot_t(d_up, w_up)
    d_hid2 = d_hid2 + swap_pair(d_hid2)

    g_norm2 = jnp.sum(d_hid2 * normed_two, axis=0)
    scaled = d_hid2 * gain_two
    d_resid = cot + inv_two * (
        scaled - normed_two * jnp.mean(scaled * normed_two, axis=-1, keepdims=True)
    )
    dres = d_resid.astype(BF16)
    g_out = jnp.stack([t_dot(y_mat, dres[:, :512]), t_dot(y_mat, dres[:, 512:])]).astype(BF16)
    d_y = dot_t(dres[:, :512], w_out[0]) + dot_t(dres[:, 512:], w_out[1])
    d_c = d_y * convolved
    d_conv = (d_y * c_mat).reshape(2, rows, 512)
    g_taps = [
        jnp.sum(d_conv * padded[:, :-2], axis=(0, 1)),
        jnp.sum(d_conv * padded[:, 1:-1], axis=(0, 1)),
        jnp.sum(d_conv * padded[:, 2:], axis=(0, 1)),
    ]
    after = jnp.concatenate([d_conv, shifted(d_conv[:, :2], -1)], axis=1)
    d_gated = taps[0] * after[:, 2:] + taps[1] * after[:, 1:-1] + taps[2] * after[:, :-2]
    d_gated = d_gated.reshape(-1, 512)
    d_b, d_c, d_x = (
        (d_gated * x_mat).astype(BF16),
        d_c.astype(BF16),
        (d_gated * b_mat).astype(BF16),
    )
    g_b, g_c, g_x = (t_dot(hidden_one, d).astype(BF16) for d in (d_b, d_c, d_x))
    d_hid1_part = dot_t(d_b, w_b) + dot_t(d_c, w_c) + dot_t(d_x, w_x)
    g_norm1 = jnp.sum(d_hid1_part * normed_one, axis=0)
    d_hid1 = own(d_hid1_part) + swap_pair(others(d_hid1_part))
    scaled = d_hid1 * gain_one
    own_normed = own(normed_one)
    input_grad = own(d_resid) + own(inv_one) * (
        scaled - own_normed * jnp.mean(scaled * own_normed, axis=-1, keepdims=True)
    )

    tap_rows = lax.dynamic_update_slice(
        jnp.zeros((3, width), F32), jnp.stack(g_taps), (0, core * 512)
    )
    g_small = jnp.concatenate(
        [g_norm1[None], g_norm2[None] * 0.5, tap_rows, jnp.zeros((123, width), F32)], axis=0
    )
    grads = (
        jnp.concatenate([g_b, g_small.T.astype(BF16)], axis=1).reshape(*CHIPS, 16, 640),
        g_c.reshape(*CHIPS, 16, 512),
        g_x.reshape(*CHIPS, 16, 512),
        g_gate.reshape(*CHIPS, 16, 2304),
        g_up.reshape(*CHIPS, 16, 2304),
    )
    totals = reduce(
        grads, g_out.reshape(2, 2, 2, 4, 2, 16, 512), g_down.reshape(2, 2, 2, 4, 2, 72, 512)
    )

    def whole(total, columns=slice(None)):
        count = total.shape[1] // 2
        mine = lax.dynamic_slice_in_dim(total, core * count, count, axis=1)[:, :, columns]
        return jnp.concatenate([mine[0], mine[1]], axis=1) * factor

    t_b, t_c, t_x, t_gate, t_up, t_down = totals
    count = 8
    t_small = lax.dynamic_slice_in_dim(t_b[0] + t_b[1], core * count, count, axis=0)[:, 512:] * factor
    left = slice(0, 512)
    return (
        block_out.reshape(tokens.shape),
        input_grad.reshape(tokens.shape),
        t_small[:, 0],
        jnp.concatenate([whole(t_b, left), whole(t_c), whole(t_x, left)], axis=1),
        t_small[:, 2:5].T,
        whole(t_x, slice(512, 1024)),
        t_small[:, 1],
        whole(t_gate),
        whole(t_up),
        whole(t_down),
    )


def solution(mesh):
    tokens = P("fsdp", "seq", None)
    vector, matrix, taps = P(("seq", "fsdp")), P(("seq", "fsdp"), None), P(None, ("seq", "fsdp"))
    weights = (vector, matrix, taps, matrix, vector, matrix, matrix, matrix)
    return jax.shard_map(
        shards,
        mesh=mesh,
        in_specs=(tokens, tokens, *weights),
        out_specs=(tokens, tokens, *weights),
        check_vma=False,
    )
```

```python
import math

import jax
import jax.numpy as jnp
from jax import lax
from jax.experimental import pallas as pl
from jax.experimental.pallas import tpu as pltpu
from jax.sharding import PartitionSpec as P

norm_eps = 1e-05
MESH = pl.DeviceIdType.MESH
F32, BF16 = jnp.float32, jnp.bfloat16

CHIPS = (4, 2, 4, 2)
ARRAYS = (
    ((16, 640), "xyz"),
    ((16, 512), "yzx"),
    ((16, 1024), "zxy"),
    ((16, 2304), "xyz"),
    ((16, 2304), "yzx"),
    ((72, 512), "zxy"),
)


def position():
    s, f = lax.axis_index("seq"), lax.axis_index("fsdp")
    y, x_lo, z = lax.div(s, 8), lax.rem(lax.div(s, 4), 2), lax.rem(s, 4)
    x_hi, core = lax.div(f, 2), lax.rem(f, 2)
    return {"x": x_hi * 2 + x_lo, "y": y, "z": z}, core


def device(at, core):
    x_lo, x_hi = lax.rem(at["x"], 2), lax.div(at["x"], 2)
    return ((at["y"] * 2 + x_lo) * 4 + at["z"], x_hi * 2 + core)


def moved(at, axis, by):
    return {**at, axis: lax.rem(at[axis] + by, 4)}


def chip_index(at, whole):
    y = slice(None) if "y" in whole else pl.ds(at["y"], 1)
    z = slice(None) if "z" in whole else pl.ds(at["z"], 1)
    if "x" in whole:
        x_lo = x_hi = slice(None)
    else:
        x_lo, x_hi = pl.ds(lax.rem(at["x"], 2), 1), pl.ds(lax.div(at["x"], 2), 1)
    return (y, x_lo, z, x_hi)


def halves(columns):
    first = (columns // 128 + 1) // 2 * 128
    return slice(0, first), slice(first, columns)


def enter(at, core):
    barrier = pltpu.get_barrier_semaphore()
    for axis in "xyz":
        for by in (1, 3):
            pl.semaphore_signal(
                barrier, inc=1, device_id=device(moved(at, axis, by), core), device_id_type=MESH
            )
    for other in (device(at, 1 - core), next_block(1), next_block(31)):
        pl.semaphore_signal(barrier, inc=1, device_id=other, device_id_type=MESH)
    pl.semaphore_wait(barrier, 9)


def next_block(by):
    return (lax.rem(lax.axis_index("seq") + by, 32), lax.axis_index("fsdp"))


def remote(src, dst, sends, recvs, target, sem):
    return pltpu.make_async_remote_copy(
        src_ref=src,
        dst_ref=dst,
        send_sem=sends.at[sem],
        recv_sem=recvs.at[sem],
        device_id=target,
        device_id_type=MESH,
    )


def dot(a, b):
    return jnp.dot(a, b, preferred_element_type=F32)


def dot_t(a, b):
    return lax.dot_general(a, b, (((1,), (1,)), ((), ())), preferred_element_type=F32)


def t_dot(a, b):
    return lax.dot_general(a, b, (((0,), (0,)), ((), ())), preferred_element_type=F32)


def flat(value):
    return value.reshape(-1, value.shape[-1])


def tile(j, size=256):
    return pl.ds(pl.multiple_of(j * size, size), size)


def rms_inverse(values):
    return lax.rsqrt(jnp.mean(values * values, axis=-1, keepdims=True) + norm_eps)


def steps(count, body):
    def run(i, carry):
        body(i)
        return carry

    lax.fori_loop(0, count, run, 0)


REST = (slice(None),) * 4
MIXER, FEED = (0, 1, 2), (3, 4, 5)
ROWS, WIDTH, HALF = 256, 1024, 512


def row_blocks(body, size=32):
    per = ROWS // size

    def run(i):
        body(lax.div(i, per), tile(lax.rem(i, per), size))

    steps(2 * per, run)


def picker():
    shape = (16, 128)
    same = lax.broadcasted_iota(jnp.int32, shape, 0) == lax.broadcasted_iota(jnp.int32, shape, 1)
    return jnp.where(same, 1.0, 0.0).astype(BF16)


def gather_kernel(*refs):
    count = len(ARRAYS)
    refs = list(refs)

    def take(n):
        taken = refs[:n]
        del refs[:n]
        return taken

    shards = take(count)
    tok, cot = take(2)
    w_b, w_c, w_x, out_half = take(4)
    feed_full = take(3)
    down_half, tok_pair, cot_pair = take(3)
    res, hid1, hid2, b_mat, c_mat, x_mat, gated, y_mat, small = take(9)
    theirs, block = take(count), take(count)
    full = take(3) + feed_full
    toks, mix, mix2, outw, halo = take(5)
    sends, recvs, local = refs
    at, core = position()
    sibling = device(at, 1 - core)
    enter(at, core)
    sent, kept = [], []

    def start(copy):
        copy.start()
        return copy

    def send(src, dst, target, sem):
        sent.append(start(remote(src, dst, sends, recvs, target, sem)))

    def arrived(ref, sem):
        remote(ref, ref, sends, recvs, sibling, sem).wait_recv()

    def keep(src, dst, sem):
        kept.append(start(pltpu.make_async_copy(src, dst, local.at[sem])))
        return kept[-1]

    for k in range(count):
        send(shards[k].at[1 - core], theirs[k], sibling, 12 * count + k)
    own_copies = []
    here = (at["y"], lax.rem(at["x"], 2), at["z"], lax.div(at["x"], 2))
    for k in range(count):
        arrived(theirs[k], 12 * count + k)
        block[k][...] = jnp.where(core == 0, shards[k][0], shards[k][1]) + theirs[k][...]
        own_copies.append(
            start(pltpu.make_async_copy(block[k], full[k].at[here], local.at[k]))
        )
        for by, sem in ((1, 0), (3, 1)):
            send(
                block[k],
                full[k].at[here],
                device(moved(at, ARRAYS[k][1][0], by), core),
                12 * k + sem,
            )
    send(tok, toks.at[core], sibling, 13 * count)
    own_tok = start(pltpu.make_async_copy(tok, toks.at[core], local.at[count]))
    send(cot, cot_pair.at[core], sibling, 13 * count + 1)
    keep(cot, cot_pair.at[core], count + 1)

    def pass_on(k, phase):
        (_, columns), order = ARRAYS[k]
        axis, whole, base = order[phase], order[:phase], 12 * k + 4 * phase
        right, left = moved(at, axis, 1), moved(at, axis, 3)
        for source, part, target, sem in zip((left, right), halves(columns), (right, left), (0, 1)):
            arrived(full[k].at[chip_index(source, whole)], base + sem)
            piece = full[k].at[(*chip_index(source, whole), slice(None), part)]
            send(piece, piece, device(target, core), base + 2 + sem)

    def complete(k, phase):
        (_, columns), order = ARRAYS[k]
        whole, base = order[:phase], 12 * k + 4 * phase
        across = moved(at, order[phase], 2)
        for part, sem in zip(halves(columns), (2, 3)):
            arrived(full[k].at[(*chip_index(across, whole), slice(None), part)], base + sem)
        if phase == 0:
            own_copies[k].wait()

    def begin(k, phase):
        order = ARRAYS[k][1]
        mine = full[k].at[chip_index(at, order[:phase])]
        for by, sem in ((1, 0), (3, 1)):
            send(mine, mine, device(moved(at, order[phase], by), core), 12 * k + 4 * phase + sem)

    def give_half(k, dst, columns):
        mine = full[k].at[(pl.ds(2 * core, 2), *REST, columns)]
        other = full[k].at[(pl.ds(2 - 2 * core, 2), *REST, columns)]
        send(other, dst.at[core], sibling, 13 * count + k)
        return start(pltpu.make_async_copy(mine, dst.at[core], local.at[count + k]))

    def each(step, arrays, phase):
        for k in arrays:
            step(k, phase)

    each(pass_on, MIXER, 0)
    each(pass_on, FEED, 0)
    each(complete, MIXER, 0)
    each(begin, MIXER, 1)
    each(complete, FEED, 0)
    each(begin, FEED, 1)
    each(pass_on, MIXER, 1)
    each(complete, MIXER, 1)
    each(begin, MIXER, 2)
    each(pass_on, FEED, 1)
    each(complete, FEED, 1)
    each(pass_on, MIXER, 2)
    each(begin, FEED, 2)
    each(complete, MIXER, 2)
    own_out = give_half(2, outw, slice(512, 1024))
    left = slice(0, 512)
    keep(full[0].at[(*REST, slice(None), left)], w_b, 18)
    keep(full[1], w_c, 19)
    keep(full[2].at[(*REST, slice(None), left)], w_x, 20)

    small[...] = dot_t(picker(), flat(full[0][:, :, :, :, :, 512:640]))
    own_tok.wait()
    arrived(toks.at[1 - core], 13 * count)
    keep(toks, tok_pair, 21)

    def norm_one(c, rows):
        t = toks[c, rows, :]
        hid1[c, rows, :] = (t * rms_inverse(t) * small[0:1, :]).astype(BF16)

    row_blocks(norm_one)

    def project(i):
        c, j = lax.div(i, 2), tile(lax.rem(i, 2))
        h = hid1[c]
        b = dot(h, flat(full[0][:, :, :, :, :, j]))
        x = dot(h, flat(full[2][:, :, :, :, :, j]))
        b_mat[c, :, j] = b
        x_mat[c, :, j] = x
        gated[c, pl.ds(8, ROWS), j] = b * x
        c_mat[c, pl.ds(0, ROWS), j] = dot(h, flat(full[1][:, :, :, :, :, j]))

    steps(4, project)
    send(gated.at[:, pl.ds(ROWS, 8), :], halo, next_block(1), 13 * count + 4)
    own_out.wait()
    arrived(outw.at[1 - core], 13 * count + 2)
    keep(outw, out_half, 22)
    arrived(halo, 13 * count + 4)
    starts = lax.axis_index("seq") == 0
    taps = [small[2 + i : 3 + i, tile(core, HALF)] for i in range(3)]
    for c in range(2):
        gated[c, 0:8, :] = jnp.where(starts, 0.0, halo[c])
        for r in range(0, ROWS, 64):
            conv = taps[0] * gated[c, r + 6 : r + 70, :]
            conv = conv + taps[1] * gated[c, r + 7 : r + 71, :]
            conv = conv + taps[2] * gated[c, r + 8 : r + 72, :]
            y_mat[c, r : r + 64, :] = (c_mat[c, r : r + 64, :] * conv).astype(BF16)

    def mixing(i):
        c, h, j = lax.div(i, 4), lax.rem(lax.div(i, 2), 2), lax.rem(i, 2)
        weight = outw[h, :, :, :, :, :, tile(j)]
        mix[c, :, tile(2 * h + j)] = dot(y_mat[c], flat(weight))

    steps(8, mixing)
    send(mix, mix2, sibling, 13 * count + 3)
    each(pass_on, FEED, 2)
    arrived(mix2, 13 * count + 3)

    def norm_two(c, rows):
        r = toks[c, rows, :] + (mix[c, rows, :] + mix2[c, rows, :])
        res[c, rows, :] = r
        hid2[c, rows, :] = (r * rms_inverse(r) * small[1:2, :]).astype(BF16)

    row_blocks(norm_two)
    each(complete, FEED, 2)
    give_half(5, down_half, slice(0, 512)).wait()
    arrived(down_half.at[1 - core], 13 * count + 5)
    arrived(cot_pair.at[1 - core], 13 * count + 1)
    for copy in sent:
        copy.wait_send()
    for copy in kept:
        copy.wait()


def gather(shards, tok, cot):
    count = len(ARRAYS)
    hbm, vmem = pl.BlockSpec(memory_space=pl.ANY), pl.BlockSpec(memory_space=pltpu.VMEM)
    shape = jax.ShapeDtypeStruct
    pair = (2, ROWS, WIDTH)
    outs = [shape((*CHIPS, 16, HALF), BF16)] * 3 + [shape((2, 2, 2, 4, 2, 16, HALF), BF16)]
    outs += [shape((*CHIPS, *ARRAYS[k][0]), BF16) for k in FEED]
    outs += [shape((2, 2, 2, 4, 2, 72, HALF), BF16), shape(pair, F32), shape(pair, F32)]
    in_hbm = len(outs)
    outs += [
        shape(pair, F32),
        shape(pair, BF16),
        shape(pair, BF16),
        shape((2, ROWS, HALF), F32),
        shape((2, ROWS + 8, HALF), F32),
        shape((2, ROWS, HALF), F32),
        shape((2, ROWS + 8, HALF), F32),
        shape((2, ROWS, HALF), BF16),
        shape((16, WIDTH), F32),
    ]
    blocks = [pltpu.VMEM(array, BF16) for array, _ in ARRAYS]
    return pl.pallas_call(
        gather_kernel,
        out_shape=outs,
        in_specs=[vmem] * count + [hbm] * 2,
        out_specs=[hbm] * 4 + [vmem] * 3 + [hbm] * (in_hbm - 7) + [vmem] * (len(outs) - in_hbm),
        scratch_shapes=[
            *blocks,
            *blocks,
            *[pltpu.VMEM((*CHIPS, *ARRAYS[k][0]), BF16) for k in MIXER],
            *[pltpu.VMEM(pair, F32)] * 3,
            pltpu.VMEM((2, 2, 2, 4, 2, 16, HALF), BF16),
            pltpu.VMEM((2, 8, HALF), F32),
            pltpu.SemaphoreType.DMA((14 * count,)),
            pltpu.SemaphoreType.DMA((14 * count,)),
            pltpu.SemaphoreType.DMA((24,)),
        ],
        compiler_params=pltpu.CompilerParams(
            collective_id=0, has_side_effects=True, vmem_limit_bytes=60 * 2**20
        ),
        name="gather_and_mix",
    )(*shards, tok, cot)


def reduce_kernel(*refs):
    count = len(ARRAYS)
    refs = list(refs)

    def take(n):
        taken = refs[:n]
        del refs[:n]
        return taken

    g_gate, g_up, g_down, d_hid2, in_hbm = *take(4), take(14)
    totals, (input_grad,) = take(count), take(1)
    data, arriving = take(count), take(12 * count)
    cot, res, hid1, b_mat, c_mat, x_mat, gated, y_mat, outw, small = held = take(10)
    dh, dh2, d1r, dres, g_out, halo = take(6)
    d_proj, (g_small,) = take(3), take(1)
    sends, recvs, local = refs
    at, core = position()
    sibling = device(at, 1 - core)
    enter(at, core)
    sent = []

    def send(src, dst, target, sem):
        copy = remote(src, dst, sends, recvs, target, sem)
        copy.start()
        sent.append(copy)

    def arrived(ref, sem):
        remote(ref, ref, sends, recvs, sibling, sem).wait_recv()

    def load(src, dst, sem):
        copy = pltpu.make_async_copy(src, dst, local.at[sem])
        copy.start()
        return copy

    def buffer(k, phase, which):
        return arriving[12 * k + 4 * phase + which]

    def add(k, phase, where, sources, columns, total=None):
        sizes = sources[0].shape[:4]

        def body(t):
            i3 = lax.rem(t, sizes[3])
            t3 = lax.div(t, sizes[3])
            i2 = lax.rem(t3, sizes[2])
            t2 = lax.div(t3, sizes[2])
            i1 = lax.rem(t2, sizes[1])
            i0 = lax.div(t2, sizes[1])
            spot = tuple(i + b for i, b in zip((i0, i1, i2, i3), where))
            value = data[k][(*spot, slice(None), columns)].astype(F32)
            for source in sources:
                value = value + source[i0, i1, i2, i3].astype(F32)
            if total is None:
                data[k][(*spot, slice(None), columns)] = value.astype(BF16)
            else:
                total[...] = value

        steps(math.prod(sizes), body)

    def start_of(place, whole):
        y = 0 if "y" in whole else place["y"]
        z = 0 if "z" in whole else place["z"]
        if "x" in whole:
            return (y, 0, z, 0)
        return (y, lax.rem(place["x"], 2), z, lax.div(place["x"], 2))

    def begin(k, phase):
        (_, columns), order = ARRAYS[k]
        axis, whole = order[2 - phase], order[: 2 - phase]
        across = chip_index(moved(at, axis, 2), whole)
        for part, which, by in zip(halves(columns), (0, 1), (1, 3)):
            send(
                data[k].at[(*across, slice(None), part)],
                buffer(k, phase, which),
                device(moved(at, axis, by), core),
                12 * k + 4 * phase + which,
            )

    def pass_on(k, phase):
        (_, columns), order = ARRAYS[k]
        axis, whole = order[2 - phase], order[: 2 - phase]
        base = 12 * k + 4 * phase
        for part, which, by in zip(halves(columns), (0, 1), (1, 3)):
            near = moved(at, axis, by)
            arrived(buffer(k, phase, which), base + which)
            add(k, phase, start_of(near, whole), [buffer(k, phase, which)], part)
            send(
                data[k].at[chip_index(near, whole)],
                buffer(k, phase, 2 + which),
                device(near, core),
                base + 2 + which,
            )

    def complete(k, phase):
        whole = ARRAYS[k][1][: 2 - phase]
        base = 12 * k + 4 * phase
        both = [buffer(k, phase, 2), buffer(k, phase, 3)]
        arrived(both[0], base + 2)
        arrived(both[1], base + 3)
        total = totals[k].at[core] if phase == 2 else None
        add(k, phase, start_of(at, whole), both, slice(None), total)
        if phase < 2:
            begin(k, phase + 1)
        else:
            send(total, total, sibling, 13 * count + k)

    def each(step, arrays, phase):
        for k in arrays:
            step(k, phase)

    mine = data[5].at[pl.ds(2 * core, 2)]
    send(g_down.at[1 - core], mine, sibling, 12 * count + 5)
    send(d_hid2, dh2, sibling, 12 * count)
    feed_loads = [
        load(g_gate, data[3], 3),
        load(g_up, data[4], 4),
        load(g_down.at[core], mine, 5),
    ]
    first_loads = [load(d_hid2, dh, 6)]
    first_loads += [load(in_hbm[i], held[i], 7 + i) for i in (0, 1, 9)]
    rest_loads = [load(in_hbm[i], held[i], 7 + i) for i in range(2, 9)]
    left = slice(0, HALF)
    for k in MIXER:
        dst = data[k] if k == 1 else data[k].at[(*REST, slice(None), left)]
        rest_loads.append(load(in_hbm[10 + k], dst, 17 + k))
    for k in FEED:
        feed_loads[k - 3].wait()
        if k == 5:
            arrived(data[5].at[pl.ds(2 - 2 * core, 2)], 12 * count + 5)
        begin(k, 0)
    for copy in first_loads:
        copy.wait()
    arrived(dh2, 12 * count)
    g_small[...] = jnp.zeros_like(g_small)

    def norm_two(c, rows):
        r = res[c, rows, :]
        inv = rms_inverse(r)
        normed = r * inv
        d = dh[c, rows, :] + dh2[c, rows, :]
        g_small[1:2, :] += 0.5 * jnp.sum(d * normed, axis=0, keepdims=True)
        scaled = d * small[1:2, :]
        mean = jnp.mean(scaled * normed, axis=-1, keepdims=True)
        out = cot[c, rows, :] + inv * (scaled - normed * mean)
        cot[c, rows, :] = out
        dres[c, rows, :] = out.astype(BF16)

    row_blocks(norm_two)
    tok_load = load(in_hbm[13], res, 20)
    each(pass_on, FEED, 0)
    for copy in rest_loads:
        copy.wait()

    taps = [small[2 + i : 3 + i, tile(core, HALF)] for i in range(3)]
    for c in range(2):
        for j in range(2):
            cols = slice(256 * j, 256 * j + 256)
            d_y = dot_t(dres[c, :, 0:HALF], flat(outw[0, j]))
            d_y = d_y + dot_t(dres[c, :, HALF:WIDTH], flat(outw[1, j]))
            conv = sum(taps[i][:, cols] * gated[c, 6 + i : 6 + i + ROWS, cols] for i in range(3))
            d_proj[1][c, :, cols] = (d_y * conv).astype(BF16)
            c_mat[c, 0:ROWS, cols] = d_y * c_mat[c, 0:ROWS, cols]
    send(c_mat.at[:, pl.ds(0, 8), :], halo, next_block(31), 12 * count + 3)

    def out_grad(i):
        f, j = lax.div(i, 2), lax.rem(i, 2)
        other = sum(
            t_dot(y_mat[c, :, tile(f)], dres[c, :, tile(2 - 2 * core + j)]) for c in range(2)
        )
        g_out[f, :, :, :, :, tile(j)] = other.astype(BF16).reshape(2, 4, 2, 16, 256)
        own = sum(t_dot(y_mat[c, :, tile(f)], dres[c, :, tile(2 * core + j)]) for c in range(2))
        data[2][2 * core + f, :, :, :, :, tile(2 + j)] = own.astype(BF16).reshape(2, 4, 2, 16, 256)

    steps(4, out_grad)
    right = slice(HALF, WIDTH)
    send(g_out, data[2].at[(pl.ds(2 * core, 2), *REST, right)], sibling, 12 * count + 2)
    arrived(halo, 12 * count + 3)
    ends = lax.axis_index("seq") == 31
    for c in range(2):
        c_mat[c, ROWS : ROWS + 8, :] = jnp.where(ends, 0.0, halo[c])
        for r in range(0, ROWS, 64):
            d_conv = c_mat[c, r : r + 64, :]
            for i in range(3):
                part = jnp.sum(
                    d_conv * gated[c, r + 6 + i : r + 70 + i, :], axis=0, keepdims=True
                )
                g_small[2 + i : 3 + i, tile(core, HALF)] += part
            d_gated = taps[0] * c_mat[c, r + 2 : r + 66, :]
            d_gated = d_gated + taps[1] * c_mat[c, r + 1 : r + 65, :] + taps[2] * d_conv
            d_proj[0][c, r : r + 64, :] = (d_gated * x_mat[c, r : r + 64, :]).astype(BF16)
            d_proj[2][c, r : r + 64, :] = (d_gated * b_mat[c, r : r + 64, :]).astype(BF16)

    def back(i):
        c, y = lax.div(i, 4), lax.rem(i, 4)
        value = None
        for k in MIXER:
            part = dot_t(d_proj[k][c], flat(data[k][y, :, :, :, :, 0:HALF]))
            value = part if value is None else value + part
        dh[c, :, tile(y)] = value

    steps(8, back)
    send(dh.at[1 - core], d1r, sibling, 12 * count + 1)

    def in_grad(i):
        y, j = lax.div(i, 2), tile(lax.rem(i, 2))
        for k in MIXER:
            value = sum(t_dot(hid1[c, :, tile(y)], d_proj[k][c, :, j]) for c in range(2))
            data[k][y, :, :, :, :, j] = value.astype(BF16).reshape(2, 4, 2, 16, 256)

    steps(8, in_grad)
    tok_load.wait()

    def gain_one(c, rows):
        t = res[c, rows, :]
        g_small[0:1, :] += jnp.sum(dh[c, rows, :] * (t * rms_inverse(t)), axis=0, keepdims=True)

    row_blocks(gain_one)
    turned = t_dot(g_small[...].astype(BF16), picker()).astype(BF16)
    data[0][:, :, :, :, :, HALF : HALF + 128] = turned.reshape(*CHIPS, 16, 128)
    arrived(data[2].at[(pl.ds(2 - 2 * core, 2), *REST, right)], 12 * count + 2)
    each(begin, MIXER, 0)
    each(complete, FEED, 0)
    each(pass_on, MIXER, 0)
    each(pass_on, FEED, 1)
    arrived(d1r, 12 * count + 1)

    def norm_one(i):
        rows = tile(i, 32)
        t = res[core, rows, :]
        inv = rms_inverse(t)
        normed = t * inv
        scaled = (dh[core, rows, :] + d1r[rows, :]) * small[0:1, :]
        mean = jnp.mean(scaled * normed, axis=-1, keepdims=True)
        input_grad[rows, :] = cot[core, rows, :] + inv * (scaled - normed * mean)

    steps(ROWS // 32, norm_one)
    each(complete, MIXER, 0)
    each(complete, FEED, 1)
    each(pass_on, MIXER, 1)
    each(pass_on, FEED, 2)
    each(complete, MIXER, 1)
    each(complete, FEED, 2)
    each(pass_on, MIXER, 2)
    each(complete, MIXER, 2)
    for k in range(count):
        arrived(totals[k].at[1 - core], 13 * count + k)
    for copy in sent:
        copy.wait_send()


def reduce(g_gate, g_up, g_down, d_hid2, *rest):
    count = len(ARRAYS)
    hbm, vmem = pl.BlockSpec(memory_space=pl.ANY), pl.BlockSpec(memory_space=pltpu.VMEM)
    buffers = []
    for (rows, columns), order in ARRAYS:
        for phase in range(3):
            whole = order[: 2 - phase]
            lead = (
                4 if "y" in whole else 1,
                2 if "x" in whole else 1,
                4 if "z" in whole else 1,
                2 if "x" in whole else 1,
            )
            for part in halves(columns):
                buffers.append(pltpu.VMEM((*lead, rows, part.stop - part.start), BF16))
            buffers += [pltpu.VMEM((*lead, rows, columns), BF16)] * 2
    pair = pltpu.VMEM((2, ROWS, WIDTH), F32)
    operands = (g_gate, g_up, g_down, d_hid2, *rest)
    return pl.pallas_call(
        reduce_kernel,
        out_shape=[jax.ShapeDtypeStruct((2, *shape), F32) for shape, _ in ARRAYS]
        + [jax.ShapeDtypeStruct((ROWS, WIDTH), F32)],
        in_specs=[hbm] * len(operands),
        out_specs=[vmem] * (count + 1),
        scratch_shapes=[
            *[pltpu.VMEM((*CHIPS, *shape), BF16) for shape, _ in ARRAYS],
            *buffers,
            *[pltpu.VMEM(value.shape, value.dtype) for value in rest[:10]],
            pair,
            pair,
            pltpu.VMEM((ROWS, WIDTH), F32),
            pltpu.VMEM((2, ROWS, WIDTH), BF16),
            pltpu.VMEM((2, 2, 4, 2, 16, HALF), BF16),
            pltpu.VMEM((2, 8, HALF), F32),
            *[pltpu.VMEM((2, ROWS, HALF), BF16)] * 3,
            pltpu.VMEM((16, WIDTH), F32),
            pltpu.SemaphoreType.DMA((14 * count,)),
            pltpu.SemaphoreType.DMA((14 * count,)),
            pltpu.SemaphoreType.DMA((24,)),
        ],
        compiler_params=pltpu.CompilerParams(
            collective_id=1, has_side_effects=True, vmem_limit_bytes=63 * 2**20
        ),
        name="sum_gradients",
    )(*operands)


def swap_pair(value):
    return lax.ppermute(value, "fsdp", [(0, 1), (1, 0), (2, 3), (3, 2)])


def rows_for_pair(shard, core):
    rows = shard.shape[0]
    both = jnp.concatenate([shard, shard], axis=0)
    mine = lax.broadcasted_iota(jnp.int32, both.shape, 0) // rows == core
    return jnp.where(mine, both, jnp.zeros_like(both))


def shards(
    tokens,
    cotangent,
    norm1_gain,
    in_weight,
    conv_taps,
    out_weight,
    norm2_gain,
    gate_weight,
    up_weight,
    down_weight,
):
    width = tokens.shape[-1]
    inputs = tokens.reshape(-1, width)
    upstream = cotangent.reshape(-1, width)
    rows = inputs.shape[0]
    total_rows = rows * lax.axis_size("seq") * lax.axis_size("fsdp")
    factor = 1.0 / math.sqrt(total_rows)
    core = lax.rem(lax.axis_index("fsdp"), 2)

    small = jnp.concatenate(
        [norm1_gain[:, None], norm2_gain[:, None], conv_taps.T, jnp.zeros((8, 123), BF16)], axis=1
    )

    def by_half(*columns):
        return jnp.stack(
            [
                rows_for_pair(
                    jnp.concatenate(
                        [
                            c if c.shape[1] == 128 else c[:, h * c.shape[1] // 2 : (h + 1) * c.shape[1] // 2]
                            for c in columns
                        ],
                        axis=1,
                    ),
                    core,
                )
                for h in range(2)
            ]
        )

    b_w, c_w, x_w = in_weight[:, :width], in_weight[:, width : 2 * width], in_weight[:, 2 * width :]
    pieces = (
        by_half(b_w, small),
        by_half(c_w),
        by_half(x_w, out_weight),
        by_half(gate_weight),
        by_half(up_weight),
        by_half(down_weight),
    )
    w_b, w_c, w_x, w_out, w_gate, w_up, _, w_down, tok, cot, *kept = gather(pieces, inputs, upstream)
    resid, hidden_one, hidden_two, b_mat, c_mat, x_mat, gated, y_mat, small = kept
    w_gate = w_gate.reshape(width, -1)
    w_up = w_up.reshape(width, -1)
    w_down = w_down.reshape(2, 2304, 512)
    hid2 = hidden_two.reshape(-1, width)
    gate, up_vals = dot(hid2, w_gate), dot(hid2, w_up)
    sigma = jax.nn.sigmoid(gate)
    act = (gate * sigma * up_vals).astype(BF16)
    out_part = jnp.concatenate([dot(act, w_down[0]), dot(act, w_down[1])], axis=1)

    def own(value):
        return lax.dynamic_slice_in_dim(value, core * rows, rows, axis=0)

    def others(value):
        return lax.dynamic_slice_in_dim(value, (1 - core) * rows, rows, axis=0)

    block_out = own(resid.reshape(-1, width)) + (own(out_part) + swap_pair(others(out_part)))

    cot_half = cot.reshape(-1, width).astype(BF16)
    g_down = jnp.stack([t_dot(act, cot_half[:, :512]), t_dot(act, cot_half[:, 512:])]).astype(BF16)
    d_act = dot_t(cot_half[:, :512], w_down[0]) + dot_t(cot_half[:, 512:], w_down[1])
    d_gate = (d_act * up_vals * sigma * (1.0 + gate * (1.0 - sigma))).astype(BF16)
    d_up = (d_act * gate * sigma).astype(BF16)
    g_gate = t_dot(hid2, d_gate).astype(BF16)
    g_up = t_dot(hid2, d_up).astype(BF16)
    d_hid2 = dot_t(d_gate, w_gate) + dot_t(d_up, w_up)
    *totals, input_grad = reduce(
        g_gate.reshape(*CHIPS, 16, 2304),
        g_up.reshape(*CHIPS, 16, 2304),
        g_down.reshape(2, 2, 2, 4, 2, 72, 512),
        d_hid2.reshape(2, rows, width),
        cot,
        resid,
        hidden_one,
        b_mat,
        c_mat,
        x_mat,
        gated,
        y_mat,
        w_out,
        small,
        w_b,
        w_c,
        w_x,
        tok,
    )

    def whole(total, columns=slice(None)):
        count = total.shape[1] // 2
        mine = lax.dynamic_slice_in_dim(total, core * count, count, axis=1)[:, :, columns]
        return jnp.concatenate([mine[0], mine[1]], axis=1) * factor

    t_b, t_c, t_x, t_gate, t_up, t_down = totals
    count = 8
    t_small = lax.dynamic_slice_in_dim(t_b[0] + t_b[1], core * count, count, axis=0)[:, 512:] * factor
    left = slice(0, 512)
    return (
        block_out.reshape(tokens.shape),
        input_grad.reshape(tokens.shape),
        t_small[:, 0],
        jnp.concatenate([whole(t_b, left), whole(t_c), whole(t_x, left)], axis=1),
        t_small[:, 2:5].T,
        whole(t_x, slice(512, 1024)),
        t_small[:, 1],
        whole(t_gate),
        whole(t_up),
        whole(t_down),
    )


def solution(mesh):
    tokens = P("fsdp", "seq", None)
    vector, matrix, taps = P(("seq", "fsdp")), P(("seq", "fsdp"), None), P(None, ("seq", "fsdp"))
    weights = (vector, matrix, taps, matrix, vector, matrix, matrix, matrix)
    return jax.shard_map(
        shards,
        mesh=mesh,
        in_specs=(tokens, tokens, *weights),
        out_specs=(tokens, tokens, *weights),
        check_vma=False,
    )
```

```python
import functools
import math

import jax
import jax.numpy as jnp
from jax import lax
from jax.experimental import pallas as pl
from jax.experimental.pallas import tpu as pltpu
from jax.sharding import PartitionSpec as P

norm_eps = 1e-05
MESH = pl.DeviceIdType.MESH
F32, BF16 = jnp.float32, jnp.bfloat16

CHIPS = (4, 2, 4, 2)
ARRAYS = (
    ((16, 640), "xyz"),
    ((16, 768), "yzx"),
    ((16, 768), "zxy"),
    ((16, 2304), "xyz"),
    ((16, 2304), "yzx"),
    ((72, 512), "zxy"),
)


def position():
    s, f = lax.axis_index("seq"), lax.axis_index("fsdp")
    y, x_lo, z = lax.div(s, 8), lax.rem(lax.div(s, 4), 2), lax.rem(s, 4)
    x_hi, core = lax.div(f, 2), lax.rem(f, 2)
    return {"x": x_hi * 2 + x_lo, "y": y, "z": z}, core


def device(at, core):
    x_lo, x_hi = lax.rem(at["x"], 2), lax.div(at["x"], 2)
    return ((at["y"] * 2 + x_lo) * 4 + at["z"], x_hi * 2 + core)


def moved(at, axis, by):
    return {**at, axis: lax.rem(at[axis] + by, 4)}


def chip_index(at, whole):
    y = slice(None) if "y" in whole else pl.ds(at["y"], 1)
    z = slice(None) if "z" in whole else pl.ds(at["z"], 1)
    if "x" in whole:
        x_lo = x_hi = slice(None)
    else:
        x_lo, x_hi = pl.ds(lax.rem(at["x"], 2), 1), pl.ds(lax.div(at["x"], 2), 1)
    return (y, x_lo, z, x_hi)


def halves(columns):
    first = (columns // 128 + 1) // 2 * 128
    return slice(0, first), slice(first, columns)


def enter(at, core):
    barrier = pltpu.get_barrier_semaphore()
    for axis in "xyz":
        for by in (1, 3):
            pl.semaphore_signal(
                barrier, inc=1, device_id=device(moved(at, axis, by), core), device_id_type=MESH
            )
    for other in (device(at, 1 - core), next_block(1), next_block(31)):
        pl.semaphore_signal(barrier, inc=1, device_id=other, device_id_type=MESH)
    pl.semaphore_wait(barrier, 9)


def next_block(by):
    return (lax.rem(lax.axis_index("seq") + by, 32), lax.axis_index("fsdp"))


def remote(src, dst, sends, recvs, target, sem):
    return pltpu.make_async_remote_copy(
        src_ref=src,
        dst_ref=dst,
        send_sem=sends.at[sem],
        recv_sem=recvs.at[sem],
        device_id=target,
        device_id_type=MESH,
    )


def dot(a, b):
    return jnp.dot(a, b, preferred_element_type=F32)


def dot_t(a, b):
    return lax.dot_general(a, b, (((1,), (1,)), ((), ())), preferred_element_type=F32)


def t_dot(a, b):
    return lax.dot_general(a, b, (((0,), (0,)), ((), ())), preferred_element_type=F32)


def flat(value):
    return value.reshape(-1, value.shape[-1])


def tile(j, size=256):
    return pl.ds(pl.multiple_of(j * size, size), size)


def rms_inverse(values):
    return lax.rsqrt(jnp.mean(values * values, axis=-1, keepdims=True) + norm_eps)


def steps(count, body):
    def run(i, carry):
        body(i)
        return carry

    lax.fori_loop(0, count, run, 0)


REST = (slice(None),) * 4
MIXER, FEED = (0, 1, 2), (3, 4, 5)
ROWS, WIDTH, HALF = 256, 1024, 512


def row_blocks(body, size=32):
    per = ROWS // size

    def run(i):
        body(lax.div(i, per), tile(lax.rem(i, per), size))

    steps(2 * per, run)


def picker():
    shape = (16, 128)
    same = lax.broadcasted_iota(jnp.int32, shape, 0) == lax.broadcasted_iota(jnp.int32, shape, 1)
    return jnp.where(same, 1.0, 0.0).astype(BF16)


def gather_kernel(*refs):
    count = len(ARRAYS)
    refs = list(refs)

    def take(n):
        taken = refs[:n]
        del refs[:n]
        return taken

    small_rows, in_rows, out_rows, gate_rows, up_rows, down_rows, tok, cot = take(8)
    w_b, w_c, w_x, out_half, gate_full, up_full, down_half, tok_pair, cot_pair = take(9)
    results = take(9)
    (small,) = take(1)
    given, theirs, block, (down32,) = take(count), take(count), take(count), take(1)
    full = take(count)
    toks, mix, mix2, outw, halo, cots, landed = take(7)
    res, hid1, hid2, b_mat, c_mat, x_mat, gated, y_mat, cot16 = held = take(9)
    sends, recvs, local = refs
    at, core = position()
    sibling = device(at, 1 - core)
    enter(at, core)
    sent, kept = [], []

    def start(copy):
        copy.start()
        return copy

    def send(src, dst, target, sem):
        sent.append(start(remote(src, dst, sends, recvs, target, sem)))

    def arrived(ref, sem):
        remote(ref, ref, sends, recvs, sibling, sem).wait_recv()

    def keep(src, dst, sem):
        kept.append(start(pltpu.make_async_copy(src, dst, local.at[sem])))
        return kept[-1]

    down32[...] = jnp.zeros_like(down32)
    for c in range(2):

        @pl.when(core == c)
        def _():
            down32[36 * c : 36 * c + 36, :] = down_rows[...].astype(F32)

    def spread(rows):
        both = jnp.concatenate([rows.astype(F32)] * 2, axis=0)
        mine = lax.broadcasted_iota(jnp.int32, both.shape, 0) // 8 == core
        return jnp.where(mine, both, 0.0).astype(BF16)

    def fill(k, half, dst):
        def columns(ref, first, size):
            return ref[:, pl.ds(pl.multiple_of(first, 128), size)]

        if k < 3:
            dst[:, 0:HALF] = spread(columns(in_rows, k * WIDTH + half * HALF, HALF))
        if k == 0:
            dst[:, HALF : HALF + 128] = spread(small_rows[...])
        elif k < 3:
            dst[:, HALF : HALF + 256] = spread(
                columns(out_rows, half * HALF + 256 * (k - 1), 256)
            )
        elif k < 5:
            dst[...] = spread(columns(gate_rows if k == 3 else up_rows, half * 2304, 2304))
        else:
            dst[...] = columns(down32, half * HALF, HALF).astype(BF16)

    for k in range(count):
        fill(k, 1 - core, given[k])
        send(given[k], theirs[k], sibling, 12 * count + k)
    for k in range(count):
        fill(k, core, block[k])
    own_copies = []
    here = (at["y"], lax.rem(at["x"], 2), at["z"], lax.div(at["x"], 2))
    for k in range(count):
        arrived(theirs[k], 12 * count + k)
        block[k][...] = block[k][...] + theirs[k][...]
        own_copies.append(
            start(pltpu.make_async_copy(block[k], full[k].at[here], local.at[k]))
        )
        for by, sem in ((1, 0), (3, 1)):
            send(
                block[k],
                full[k].at[here],
                device(moved(at, ARRAYS[k][1][0], by), core),
                12 * k + sem,
            )
    send(tok, toks.at[core], sibling, 13 * count)
    own_tok = start(pltpu.make_async_copy(tok, toks.at[core], local.at[count]))
    send(cot, cots.at[core], sibling, 13 * count + 1)
    own_cot = start(pltpu.make_async_copy(cot, cots.at[core], local.at[count + 1]))

    def pass_on(k, phase):
        (_, columns), order = ARRAYS[k]
        axis, whole, base = order[phase], order[:phase], 12 * k + 4 * phase
        right, left = moved(at, axis, 1), moved(at, axis, 3)
        for source, part, target, sem in zip((left, right), halves(columns), (right, left), (0, 1)):
            arrived(full[k].at[chip_index(source, whole)], base + sem)
            piece = full[k].at[(*chip_index(source, whole), slice(None), part)]
            send(piece, piece, device(target, core), base + 2 + sem)

    def complete(k, phase):
        (_, columns), order = ARRAYS[k]
        whole, base = order[:phase], 12 * k + 4 * phase
        across = moved(at, order[phase], 2)
        for part, sem in zip(halves(columns), (2, 3)):
            arrived(full[k].at[(*chip_index(across, whole), slice(None), part)], base + sem)
        if phase == 0:
            own_copies[k].wait()

    def begin(k, phase):
        order = ARRAYS[k][1]
        mine = full[k].at[chip_index(at, order[:phase])]
        for by, sem in ((1, 0), (3, 1)):
            send(mine, mine, device(moved(at, order[phase], by), core), 12 * k + 4 * phase + sem)

    def give_half(k, dst, columns, sem):
        mine = full[k].at[(pl.ds(2 * core, 2), *REST, columns)]
        other = full[k].at[(pl.ds(2 - 2 * core, 2), *REST, columns)]
        send(other, dst, sibling, sem)
        return start(pltpu.make_async_copy(mine, dst, local.at[10 + k]))

    def each(step, arrays, phase):
        for k in arrays:
            step(k, phase)

    each(pass_on, MIXER, 0)
    each(pass_on, FEED, 0)
    each(complete, MIXER, 0)
    each(begin, MIXER, 1)
    each(complete, FEED, 0)
    each(begin, FEED, 1)
    each(pass_on, MIXER, 1)
    each(complete, MIXER, 1)
    each(begin, MIXER, 2)
    each(pass_on, FEED, 1)
    each(complete, FEED, 1)
    each(pass_on, MIXER, 2)
    each(begin, FEED, 2)
    each(complete, MIXER, 2)
    own_out = [
        give_half(
            k,
            outw.at[(core, *REST, slice(None), slice(256 * k - 256, 256 * k))],
            slice(HALF, HALF + 256),
            14 * count + k,
        )
        for k in (1, 2)
    ]
    own_cot.wait()
    arrived(cots.at[1 - core], 13 * count + 1)
    keep(cots, cot_pair, 23)

    def round_cot(c, rows):
        cot16[c, rows, :] = cots[c, rows, :].astype(BF16)

    row_blocks(round_cot)
    left = slice(0, 512)

    def hand_over(*which):
        for i in which:
            keep(held[i], results[i], 24 + i)

    hand_over(8)
    keep(full[0].at[(*REST, slice(None), left)], w_b, 18)
    keep(full[1].at[(*REST, slice(None), left)], w_c, 19)
    keep(full[2].at[(*REST, slice(None), left)], w_x, 20)

    small[...] = dot_t(picker(), flat(full[0][:, :, :, :, :, 512:640]))
    own_tok.wait()
    arrived(toks.at[1 - core], 13 * count)
    keep(toks, tok_pair, 21)

    def norm_one(c, rows):
        t = toks[c, rows, :]
        hid1[c, rows, :] = (t * rms_inverse(t) * small[0:1, :]).astype(BF16)

    row_blocks(norm_one)

    def project(i):
        c, j = lax.div(i, 2), tile(lax.rem(i, 2))
        h = hid1[c]
        b = dot(h, flat(full[0][:, :, :, :, :, j]))
        x = dot(h, flat(full[2][:, :, :, :, :, j]))
        b_mat[c, :, j] = b
        x_mat[c, :, j] = x
        gated[c, pl.ds(8, ROWS), j] = b * x
        c_mat[c, pl.ds(0, ROWS), j] = dot(h, flat(full[1][:, :, :, :, :, j]))

    steps(4, project)
    send(gated.at[:, pl.ds(ROWS, 8), :], halo, next_block(1), 13 * count + 4)
    hand_over(1, 3, 4, 5)
    for k in (1, 2):
        own_out[k - 1].wait()
        part = (1 - core, *REST, slice(None), slice(256 * k - 256, 256 * k))
        arrived(outw.at[part], 14 * count + k)
    keep(outw, out_half, 22)
    arrived(halo, 13 * count + 4)
    starts = lax.axis_index("seq") == 0
    taps = [small[2 + i : 3 + i, tile(core, HALF)] for i in range(3)]
    for c in range(2):
        gated[c, 0:8, :] = jnp.where(starts, 0.0, halo[c])
        for r in range(0, ROWS, 64):
            conv = taps[0] * gated[c, r + 6 : r + 70, :]
            conv = conv + taps[1] * gated[c, r + 7 : r + 71, :]
            conv = conv + taps[2] * gated[c, r + 8 : r + 72, :]
            y_mat[c, r : r + 64, :] = (c_mat[c, r : r + 64, :] * conv).astype(BF16)

    hand_over(6, 7)

    def mixing(i):
        c, h, j = lax.div(i, 4), lax.rem(lax.div(i, 2), 2), lax.rem(i, 2)
        weight = outw[h, :, :, :, :, :, tile(j)]
        mix[c, :, tile(2 * h + j)] = dot(y_mat[c], flat(weight))

    steps(8, mixing)
    send(mix, mix2, sibling, 13 * count + 3)
    each(pass_on, FEED, 2)

    def columns(half):
        return tile(half, HALF)

    def feed_out(step):
        for k, dst in ((3, gate_full), (4, up_full)):
            order = ARRAYS[k][1]
            spot = chip_index(moved(at, order[2], step), order[:2])
            keep(full[k].at[spot], dst.at[spot], 33 + 4 * (k - 3) + step)
        y = lax.rem(at["y"] + step, 4)
        here, there = lax.div(y, 2), lax.rem(y, 2)

        @pl.when(here == core)
        def _():
            out = down_half.at[(there, *REST[:3], slice(None), columns(core))]
            pltpu.make_async_copy(full[5].at[y], out, local.at[41 + step]).start()

        @pl.when(here != core)
        def _():
            remote(full[5].at[y], landed.at[there], sends, recvs, sibling, 15 * count + step).start()

    def feed_land(step):
        y = lax.rem(at["y"] + step, 4)
        here, there = lax.div(y, 2), lax.rem(y, 2)

        @pl.when(here == core)
        def _():
            arrived(landed.at[there], 15 * count + step)
            out = down_half.at[(there, *REST[:3], slice(None), columns(1 - core))]
            pltpu.make_async_copy(landed.at[there], out, local.at[45 + step]).start()

    def feed_end(step):
        y = lax.rem(at["y"] + step, 4)
        here, there = lax.div(y, 2), lax.rem(y, 2)

        @pl.when(here == core)
        def _():
            out = down_half.at[(there, *REST[:3], slice(None), columns(core))]
            pltpu.make_async_copy(full[5].at[y], out, local.at[41 + step]).wait()
            out = down_half.at[(there, *REST[:3], slice(None), columns(1 - core))]
            pltpu.make_async_copy(landed.at[there], out, local.at[45 + step]).wait()

        @pl.when(here != core)
        def _():
            remote(
                full[5].at[y], landed.at[there], sends, recvs, sibling, 15 * count + step
            ).wait_send()

    for step in (0, 1, 3):
        feed_out(step)
    arrived(mix2, 13 * count + 3)

    def norm_two(c, rows):
        r = toks[c, rows, :] + (mix[c, rows, :] + mix2[c, rows, :])
        res[c, rows, :] = r
        hid2[c, rows, :] = (r * rms_inverse(r) * small[1:2, :]).astype(BF16)

    row_blocks(norm_two)
    hand_over(0, 2)
    for step in (0, 1, 3):
        feed_land(step)
    each(complete, FEED, 2)
    feed_out(2)
    feed_land(2)
    for step in range(4):
        feed_end(step)
    for copy in sent:
        copy.wait_send()
    for copy in kept:
        copy.wait()


def gather(shards, tok, cot):
    count = len(ARRAYS)
    hbm, vmem = pl.BlockSpec(memory_space=pl.ANY), pl.BlockSpec(memory_space=pltpu.VMEM)
    shape = jax.ShapeDtypeStruct
    pair = (2, ROWS, WIDTH)
    outs = [shape((*CHIPS, 16, HALF), BF16)] * 3 + [shape((2, 2, 2, 4, 2, 16, HALF), BF16)]
    outs += [shape((*CHIPS, *ARRAYS[k][0]), BF16) for k in (3, 4)]
    outs += [shape((2, 2, 4, 2, 72, WIDTH), BF16), shape(pair, F32), shape(pair, F32)]
    held = [
        shape(pair, F32),
        shape(pair, BF16),
        shape(pair, BF16),
        shape((2, ROWS, HALF), F32),
        shape((2, ROWS + 8, HALF), F32),
        shape((2, ROWS, HALF), F32),
        shape((2, ROWS + 8, HALF), F32),
        shape((2, ROWS, HALF), BF16),
        shape(pair, BF16),
    ]
    outs += held
    in_hbm = len(outs)
    outs += [shape((16, WIDTH), F32)]
    blocks = [pltpu.VMEM(array, BF16) for array, _ in ARRAYS]
    return pl.pallas_call(
        gather_kernel,
        out_shape=outs,
        in_specs=[vmem] * len(shards) + [hbm] * 2,
        out_specs=[hbm] * in_hbm + [vmem],
        scratch_shapes=[
            *blocks,
            *blocks,
            *blocks,
            pltpu.VMEM((72, WIDTH), F32),
            *[pltpu.VMEM((*CHIPS, *array), BF16) for array, _ in ARRAYS],
            *[pltpu.VMEM(pair, F32)] * 3,
            pltpu.VMEM((2, 2, 2, 4, 2, 16, HALF), BF16),
            pltpu.VMEM((2, 8, HALF), F32),
            pltpu.VMEM(pair, F32),
            pltpu.VMEM((2, 2, 4, 2, 72, HALF), BF16),
            *[pltpu.VMEM(value.shape, value.dtype) for value in held],
            pltpu.SemaphoreType.DMA((16 * count,)),
            pltpu.SemaphoreType.DMA((16 * count,)),
            pltpu.SemaphoreType.DMA((50,)),
        ],
        compiler_params=pltpu.CompilerParams(
            collective_id=0, has_side_effects=True, vmem_limit_bytes=60 * 2**20
        ),
        name="gather_and_mix",
    )(*shards, tok, cot)


def reduce_kernel(factor, *refs):
    count = len(ARRAYS)
    refs = list(refs)

    def take(n):
        taken = refs[:n]
        del refs[:n]
        return taken

    g_gate, g_up, g_down, d_hid2, out_part, in_hbm = *take(5), take(14)
    block_out, input_grad, in_grads, out_grads, gate_grads, up_grads, down_grads, small_grads = take(8)
    totals = take(count)
    data, arriving = take(count), take(12 * count)
    cot, res, hid1, b_mat, c_mat, x_mat, gated, y_mat, outw, small = held = take(10)
    dh, dh2, d1r, dres, g_out, halo, ffn_own, ffn_other = take(8)
    d_proj, (g_small,) = take(3), take(1)
    sends, recvs, local = refs
    at, core = position()
    sibling = device(at, 1 - core)
    enter(at, core)
    sent = []

    def send(src, dst, target, sem):
        copy = remote(src, dst, sends, recvs, target, sem)
        copy.start()
        sent.append(copy)

    def arrived(ref, sem):
        remote(ref, ref, sends, recvs, sibling, sem).wait_recv()

    def load(src, dst, sem):
        copy = pltpu.make_async_copy(src, dst, local.at[sem])
        copy.start()
        return copy

    def buffer(k, phase, which):
        return arriving[12 * k + 4 * phase + which]

    def add(k, phase, where, sources, columns, total=None):
        sizes = sources[0].shape[:4]

        def body(t):
            i3 = lax.rem(t, sizes[3])
            t3 = lax.div(t, sizes[3])
            i2 = lax.rem(t3, sizes[2])
            t2 = lax.div(t3, sizes[2])
            i1 = lax.rem(t2, sizes[1])
            i0 = lax.div(t2, sizes[1])
            spot = tuple(i + b for i, b in zip((i0, i1, i2, i3), where))
            value = data[k][(*spot, slice(None), columns)].astype(F32)
            for source in sources:
                value = value + source[i0, i1, i2, i3].astype(F32)
            if total is None:
                data[k][(*spot, slice(None), columns)] = value.astype(BF16)
            else:
                total[...] = value

        steps(math.prod(sizes), body)

    def start_of(place, whole):
        y = 0 if "y" in whole else place["y"]
        z = 0 if "z" in whole else place["z"]
        if "x" in whole:
            return (y, 0, z, 0)
        return (y, lax.rem(place["x"], 2), z, lax.div(place["x"], 2))

    def begin(k, phase):
        (_, columns), order = ARRAYS[k]
        axis, whole = order[2 - phase], order[: 2 - phase]
        across = chip_index(moved(at, axis, 2), whole)
        for part, which, by in zip(halves(columns), (0, 1), (1, 3)):
            send(
                data[k].at[(*across, slice(None), part)],
                buffer(k, phase, which),
                device(moved(at, axis, by), core),
                12 * k + 4 * phase + which,
            )

    def pass_on(k, phase):
        (_, columns), order = ARRAYS[k]
        axis, whole = order[2 - phase], order[: 2 - phase]
        base = 12 * k + 4 * phase
        for part, which, by in zip(halves(columns), (0, 1), (1, 3)):
            near = moved(at, axis, by)
            arrived(buffer(k, phase, which), base + which)
            add(k, phase, start_of(near, whole), [buffer(k, phase, which)], part)
            send(
                data[k].at[chip_index(near, whole)],
                buffer(k, phase, 2 + which),
                device(near, core),
                base + 2 + which,
            )

    def complete(k, phase):
        whole = ARRAYS[k][1][: 2 - phase]
        base = 12 * k + 4 * phase
        both = [buffer(k, phase, 2), buffer(k, phase, 3)]
        arrived(both[0], base + 2)
        arrived(both[1], base + 3)
        total = totals[k].at[core] if phase == 2 else None
        add(k, phase, start_of(at, whole), both, slice(None), total)
        if phase < 2:
            begin(k, phase + 1)
        else:
            send(total, total, sibling, 13 * count + k)

    def each(step, arrays, phase):
        for k in arrays:
            step(k, phase)

    def slab(step, start):
        y = lax.rem(at["y"] + step, 4)
        here, there = lax.div(y, 2), lax.rem(y, 2)

        def of(half):
            return g_down.at[(there, *REST[:3], slice(None), tile(half, HALF))]

        own = pltpu.make_async_copy(of(core), data[5].at[y], local.at[21 + step])
        given = remote(of(1 - core), data[5].at[y], sends, recvs, sibling, 15 * count + step)

        @pl.when(here == core)
        def _():
            if start:
                given.start()
                own.start()
            else:
                own.wait()

        @pl.when(here != core)
        def _():
            if not start:
                given.wait_recv()

    def slab_sent(step):
        y = lax.rem(at["y"] + step, 4)
        there = lax.rem(y, 2)
        src = g_down.at[(there, *REST[:3], slice(None), tile(1 - core, HALF))]

        @pl.when(lax.div(y, 2) == core)
        def _():
            remote(src, data[5].at[y], sends, recvs, sibling, 15 * count + step).wait_send()

    ring = (2, 1, 3, 0)
    feed_loads = {}
    for step in ring:
        for k, src in ((3, g_gate), (4, g_up)):
            order = ARRAYS[k][1]
            spot = chip_index(moved(at, order[2], step), order[:2])
            feed_loads[k, step] = load(src.at[spot], data[k].at[spot], 25 + 4 * (k - 3) + step)
        slab(step, True)
    send(d_hid2, dh2, sibling, 12 * count)
    send(out_part.at[1 - core], ffn_other, sibling, 12 * count + 2)
    first_loads = [load(d_hid2, dh, 6)]
    first_loads += [load(in_hbm[i], held[i], 7 + i) for i in (0, 1, 9)]
    rest_loads = [load(in_hbm[i], held[i], 7 + i) for i in range(2, 9)]
    left = slice(0, HALF)
    for k in MIXER:
        dst = data[k].at[(*REST, slice(None), left)]
        rest_loads.append(load(in_hbm[10 + k], dst, 17 + k))
    for k in (3, 4):
        feed_loads[k, 2].wait()
        begin(k, 0)
    slab(2, False)
    begin(5, 0)
    ffn_load = load(out_part.at[core], ffn_own, 33)
    for copy in first_loads:
        copy.wait()
    arrived(dh2, 12 * count)
    g_small[...] = jnp.zeros_like(g_small)

    def norm_two(c, rows):
        r = res[c, rows, :]
        inv = rms_inverse(r)
        normed = r * inv
        d = dh[c, rows, :] + dh2[c, rows, :]
        g_small[1:2, :] += 0.5 * jnp.sum(d * normed, axis=0, keepdims=True)
        scaled = d * small[1:2, :]
        mean = jnp.mean(scaled * normed, axis=-1, keepdims=True)
        out = cot[c, rows, :] + inv * (scaled - normed * mean)
        cot[c, rows, :] = out
        dres[c, rows, :] = out.astype(BF16)

    row_blocks(norm_two)
    ffn_load.wait()
    arrived(ffn_other, 12 * count + 2)

    def add_ffn(i):
        rows = tile(i, 32)
        block_out[rows, :] = res[core, rows, :] + (ffn_own[rows, :] + ffn_other[rows, :])

    steps(ROWS // 32, add_ffn)
    tok_load = load(in_hbm[13], res, 20)
    for step in ring[1:]:
        feed_loads[3, step].wait()
        feed_loads[4, step].wait()
        slab(step, False)
    each(pass_on, FEED, 0)
    for copy in rest_loads:
        copy.wait()

    taps = [small[2 + i : 3 + i, tile(core, HALF)] for i in range(3)]
    for c in range(2):
        for j in range(2):
            cols = slice(256 * j, 256 * j + 256)
            d_y = dot_t(dres[c, :, 0:HALF], flat(outw[0, j]))
            d_y = d_y + dot_t(dres[c, :, HALF:WIDTH], flat(outw[1, j]))
            conv = sum(taps[i][:, cols] * gated[c, 6 + i : 6 + i + ROWS, cols] for i in range(3))
            d_proj[1][c, :, cols] = (d_y * conv).astype(BF16)
            c_mat[c, 0:ROWS, cols] = d_y * c_mat[c, 0:ROWS, cols]
    send(c_mat.at[:, pl.ds(0, 8), :], halo, next_block(31), 12 * count + 3)

    def out_grad(i):
        f = i
        for j in range(2):
            other = sum(
                t_dot(y_mat[c, :, tile(f)], dres[c, :, tile(2 - 2 * core + j)]) for c in range(2)
            )
            g_out[f, :, :, :, :, 256 * j : 256 * j + 256] = other.astype(BF16).reshape(
                2, 4, 2, 16, 256
            )
            own = sum(
                t_dot(y_mat[c, :, tile(f)], dres[c, :, tile(2 * core + j)]) for c in range(2)
            )
            data[1 + j][2 * core + f, :, :, :, :, HALF : HALF + 256] = own.astype(BF16).reshape(
                2, 4, 2, 16, 256
            )

    steps(2, out_grad)
    right = slice(HALF, HALF + 256)
    for j in range(2):
        send(
            g_out.at[(slice(None), *REST, slice(256 * j, 256 * j + 256))],
            data[1 + j].at[(pl.ds(2 * core, 2), *REST, right)],
            sibling,
            14 * count + j,
        )
    arrived(halo, 12 * count + 3)
    ends = lax.axis_index("seq") == 31
    for c in range(2):
        c_mat[c, ROWS : ROWS + 8, :] = jnp.where(ends, 0.0, halo[c])
        for r in range(0, ROWS, 64):
            d_conv = c_mat[c, r : r + 64, :]
            for i in range(3):
                part = jnp.sum(
                    d_conv * gated[c, r + 6 + i : r + 70 + i, :], axis=0, keepdims=True
                )
                g_small[2 + i : 3 + i, tile(core, HALF)] += part
            d_gated = taps[0] * c_mat[c, r + 2 : r + 66, :]
            d_gated = d_gated + taps[1] * c_mat[c, r + 1 : r + 65, :] + taps[2] * d_conv
            d_proj[0][c, r : r + 64, :] = (d_gated * x_mat[c, r : r + 64, :]).astype(BF16)
            d_proj[2][c, r : r + 64, :] = (d_gated * b_mat[c, r : r + 64, :]).astype(BF16)

    def back(i):
        c, y = lax.div(i, 4), lax.rem(i, 4)
        value = None
        for k in MIXER:
            part = dot_t(d_proj[k][c], flat(data[k][y, :, :, :, :, 0:HALF]))
            value = part if value is None else value + part
        dh[c, :, tile(y)] = value

    steps(8, back)
    send(dh.at[1 - core], d1r, sibling, 12 * count + 1)

    def in_grad(i):
        y, j = lax.div(i, 2), tile(lax.rem(i, 2))
        for k in MIXER:
            value = sum(t_dot(hid1[c, :, tile(y)], d_proj[k][c, :, j]) for c in range(2))
            data[k][y, :, :, :, :, j] = value.astype(BF16).reshape(2, 4, 2, 16, 256)

    steps(8, in_grad)
    tok_load.wait()

    def gain_one(c, rows):
        t = res[c, rows, :]
        g_small[0:1, :] += jnp.sum(dh[c, rows, :] * (t * rms_inverse(t)), axis=0, keepdims=True)

    row_blocks(gain_one)
    turned = t_dot(g_small[...].astype(BF16), picker()).astype(BF16)
    data[0][:, :, :, :, :, HALF : HALF + 128] = turned.reshape(*CHIPS, 16, 128)
    for j in range(2):
        arrived(data[1 + j].at[(pl.ds(2 - 2 * core, 2), *REST, right)], 14 * count + j)
    each(begin, MIXER, 0)
    each(complete, FEED, 0)
    each(pass_on, MIXER, 0)
    each(pass_on, FEED, 1)
    arrived(d1r, 12 * count + 1)

    def norm_one(i):
        rows = tile(i, 32)
        t = res[core, rows, :]
        inv = rms_inverse(t)
        normed = t * inv
        scaled = (dh[core, rows, :] + d1r[rows, :]) * small[0:1, :]
        mean = jnp.mean(scaled * normed, axis=-1, keepdims=True)
        input_grad[rows, :] = cot[core, rows, :] + inv * (scaled - normed * mean)

    steps(ROWS // 32, norm_one)
    each(complete, MIXER, 0)
    each(complete, FEED, 1)
    each(pass_on, MIXER, 1)
    each(pass_on, FEED, 2)
    each(complete, MIXER, 1)
    each(complete, FEED, 2)
    each(pass_on, MIXER, 2)
    each(complete, MIXER, 2)
    for k in range(count):
        arrived(totals[k].at[1 - core], 13 * count + k)
    mine = pl.ds(pl.multiple_of(8 * core, 8), 8)
    for h in range(2):
        at_half = slice(HALF * h, HALF * h + HALF)
        for k in MIXER:
            in_grads[:, WIDTH * k + HALF * h : WIDTH * k + HALF * h + HALF] = (
                totals[k][h, mine, 0:HALF] * factor
            )
        for k in (1, 2):
            first = HALF * h + 256 * (k - 1)
            out_grads[:, first : first + 256] = totals[k][h, mine, HALF : HALF + 256] * factor
        for k, dst in ((3, gate_grads), (4, up_grads)):
            dst[:, 2304 * h : 2304 * h + 2304] = totals[k][h, mine, :] * factor
        down_grads[:, at_half] = factor * jnp.where(
            core == 0, totals[5][h, 0:36, :], totals[5][h, 36:72, :]
        )
    small_grads[...] = factor * (
        totals[0][0, mine, HALF : HALF + 128] + totals[0][1, mine, HALF : HALF + 128]
    )
    for step in ring:
        slab_sent(step)
    for copy in sent:
        copy.wait_send()


def reduce(factor, g_gate, g_up, g_down, d_hid2, out_part, *rest):
    count = len(ARRAYS)
    hbm, vmem = pl.BlockSpec(memory_space=pl.ANY), pl.BlockSpec(memory_space=pltpu.VMEM)
    buffers = []
    for (rows, columns), order in ARRAYS:
        for phase in range(3):
            whole = order[: 2 - phase]
            lead = (
                4 if "y" in whole else 1,
                2 if "x" in whole else 1,
                4 if "z" in whole else 1,
                2 if "x" in whole else 1,
            )
            for part in halves(columns):
                buffers.append(pltpu.VMEM((*lead, rows, part.stop - part.start), BF16))
            buffers += [pltpu.VMEM((*lead, rows, columns), BF16)] * 2
    pair = pltpu.VMEM((2, ROWS, WIDTH), F32)
    operands = (g_gate, g_up, g_down, d_hid2, out_part, *rest)
    return pl.pallas_call(
        functools.partial(reduce_kernel, factor),
        out_shape=[
            jax.ShapeDtypeStruct(shape, F32)
            for shape in (
                (ROWS, WIDTH),
                (ROWS, WIDTH),
                (8, 3 * WIDTH),
                (8, WIDTH),
                (8, 4608),
                (8, 4608),
                (36, WIDTH),
                (8, 128),
            )
        ],
        in_specs=[hbm] * len(operands),
        out_specs=[vmem] * 8,
        scratch_shapes=[
            *[pltpu.VMEM((2, *shape), F32) for shape, _ in ARRAYS],
            *[pltpu.VMEM((*CHIPS, *shape), BF16) for shape, _ in ARRAYS],
            *buffers,
            *[pltpu.VMEM(value.shape, value.dtype) for value in rest[:10]],
            pair,
            pair,
            pltpu.VMEM((ROWS, WIDTH), F32),
            pltpu.VMEM((2, ROWS, WIDTH), BF16),
            pltpu.VMEM((2, 2, 4, 2, 16, HALF), BF16),
            pltpu.VMEM((2, 8, HALF), F32),
            pltpu.VMEM((ROWS, WIDTH), F32),
            pltpu.VMEM((ROWS, WIDTH), F32),
            *[pltpu.VMEM((2, ROWS, HALF), BF16)] * 3,
            pltpu.VMEM((16, WIDTH), F32),
            pltpu.SemaphoreType.DMA((16 * count,)),
            pltpu.SemaphoreType.DMA((16 * count,)),
            pltpu.SemaphoreType.DMA((34,)),
        ],
        compiler_params=pltpu.CompilerParams(
            collective_id=1, has_side_effects=True, vmem_limit_bytes=63 * 2**20
        ),
        name="sum_gradients",
    )(*operands)


def finish_kernel(*refs):
    count = (len(refs) - 1) // 2
    copies = [
        pltpu.make_async_copy(refs[i], refs[count + i], refs[-1].at[i]) for i in range(count)
    ]
    for copy in copies:
        copy.start()
    for copy in copies:
        copy.wait()


def finish(*values):
    hbm, vmem = pl.BlockSpec(memory_space=pl.ANY), pl.BlockSpec(memory_space=pltpu.VMEM)
    return pl.pallas_call(
        finish_kernel,
        out_shape=[jax.ShapeDtypeStruct(v.shape, v.dtype) for v in values],
        in_specs=[vmem] * len(values),
        out_specs=[hbm] * len(values),
        scratch_shapes=[pltpu.SemaphoreType.DMA((len(values),))],
        name="finish",
    )(*values)


def shards(
    tokens,
    cotangent,
    norm1_gain,
    in_weight,
    conv_taps,
    out_weight,
    norm2_gain,
    gate_weight,
    up_weight,
    down_weight,
):
    width = tokens.shape[-1]
    inputs = tokens.reshape(-1, width)
    upstream = cotangent.reshape(-1, width)
    rows = inputs.shape[0]
    total_rows = rows * lax.axis_size("seq") * lax.axis_size("fsdp")
    factor = 1.0 / math.sqrt(total_rows)
    core = lax.rem(lax.axis_index("fsdp"), 2)

    small = jnp.concatenate(
        [norm1_gain[:, None], norm2_gain[:, None], conv_taps.T, jnp.zeros((8, 123), BF16)], axis=1
    )

    pieces = (small, in_weight, out_weight, gate_weight, up_weight, down_weight)
    w_b, w_c, w_x, w_out, w_gate, w_up, w_down, tok, cot, *kept = gather(pieces, inputs, upstream)
    resid, hidden_one, hidden_two, b_mat, c_mat, x_mat, gated, y_mat, cot_half, small = kept
    w_gate = w_gate.reshape(width, -1)
    w_up = w_up.reshape(width, -1)
    w_down = w_down.reshape(-1, width)
    hid2 = hidden_two.reshape(-1, width)
    gate, up_vals = dot(hid2, w_gate), dot(hid2, w_up)
    sigma = jax.nn.sigmoid(gate)
    act = (gate * sigma * up_vals).astype(BF16)
    out_part = dot(act, w_down)
    cot_half = cot_half.reshape(-1, width)
    g_down = t_dot(act, cot_half).astype(BF16)
    d_act = dot_t(cot_half, w_down)
    d_gate = (d_act * up_vals * sigma * (1.0 + gate * (1.0 - sigma))).astype(BF16)
    d_up = (d_act * gate * sigma).astype(BF16)
    g_gate = t_dot(hid2, d_gate).astype(BF16)
    g_up = t_dot(hid2, d_up).astype(BF16)
    d_hid2 = dot_t(d_gate, w_gate) + dot_t(d_up, w_up)
    block_out, input_grad, g_in, g_out, g_gate, g_up, g_down, g_small = reduce(
        factor,
        g_gate.reshape(*CHIPS, 16, 2304),
        g_up.reshape(*CHIPS, 16, 2304),
        g_down.reshape(2, 2, 4, 2, 72, width),
        d_hid2.reshape(2, rows, width),
        out_part.reshape(2, rows, width),
        cot,
        resid,
        hidden_one,
        b_mat,
        c_mat,
        x_mat,
        gated,
        y_mat,
        w_out,
        small,
        w_b,
        w_c,
        w_x,
        tok,
    )

    block_out, input_grad, g_in, g_out, g_gate, g_up, g_down = finish(
        block_out, input_grad, g_in, g_out, g_gate, g_up, g_down
    )
    return (
        block_out.reshape(tokens.shape),
        input_grad.reshape(tokens.shape),
        g_small[:, 0],
        g_in,
        g_small[:, 2:5].T,
        g_out,
        g_small[:, 1],
        g_gate,
        g_up,
        g_down,
    )


def solution(mesh):
    tokens = P("fsdp", "seq", None)
    vector, matrix, taps = P(("seq", "fsdp")), P(("seq", "fsdp"), None), P(None, ("seq", "fsdp"))
    weights = (vector, matrix, taps, matrix, vector, matrix, matrix, matrix)
    return jax.shard_map(
        shards,
        mesh=mesh,
        in_specs=(tokens, tokens, *weights),
        out_specs=(tokens, tokens, *weights),
        check_vma=False,
    )
```

```python
import functools
import math

import jax
import jax.numpy as jnp
from jax import lax
from jax.experimental import pallas as pl
from jax.experimental.pallas import tpu as pltpu
from jax.sharding import PartitionSpec as P

norm_eps = 1e-05
MESH = pl.DeviceIdType.MESH
F32, BF16 = jnp.float32, jnp.bfloat16

CHIPS = (4, 2, 4, 2)
ARRAYS = (
    ((16, 640), "xyz"),
    ((16, 768), "yzx"),
    ((16, 768), "zxy"),
    ((16, 2304), "xyz"),
    ((16, 2304), "yzx"),
    ((72, 512), "zxy"),
)


def position():
    s, f = lax.axis_index("seq"), lax.axis_index("fsdp")
    y, x_lo, z = lax.div(s, 8), lax.rem(lax.div(s, 4), 2), lax.rem(s, 4)
    x_hi, core = lax.div(f, 2), lax.rem(f, 2)
    return {"x": x_hi * 2 + x_lo, "y": y, "z": z}, core


def device(at, core):
    x_lo, x_hi = lax.rem(at["x"], 2), lax.div(at["x"], 2)
    return ((at["y"] * 2 + x_lo) * 4 + at["z"], x_hi * 2 + core)


def moved(at, axis, by):
    return {**at, axis: lax.rem(at[axis] + by, 4)}


def chip_index(at, whole):
    y = slice(None) if "y" in whole else pl.ds(at["y"], 1)
    z = slice(None) if "z" in whole else pl.ds(at["z"], 1)
    if "x" in whole:
        x_lo = x_hi = slice(None)
    else:
        x_lo, x_hi = pl.ds(lax.rem(at["x"], 2), 1), pl.ds(lax.div(at["x"], 2), 1)
    return (y, x_lo, z, x_hi)


def halves(columns):
    first = (columns // 128 + 1) // 2 * 128
    return slice(0, first), slice(first, columns)


def enter(at, core):
    barrier = pltpu.get_barrier_semaphore()
    for axis in "xyz":
        for by in (1, 3):
            pl.semaphore_signal(
                barrier, inc=1, device_id=device(moved(at, axis, by), core), device_id_type=MESH
            )
    for other in (device(at, 1 - core), next_block(1), next_block(31)):
        pl.semaphore_signal(barrier, inc=1, device_id=other, device_id_type=MESH)
    pl.semaphore_wait(barrier, 9)


def next_block(by):
    return (lax.rem(lax.axis_index("seq") + by, 32), lax.axis_index("fsdp"))


def remote(src, dst, sends, recvs, target, sem):
    return pltpu.make_async_remote_copy(
        src_ref=src,
        dst_ref=dst,
        send_sem=sends.at[sem],
        recv_sem=recvs.at[sem],
        device_id=target,
        device_id_type=MESH,
    )


def dot(a, b):
    return jnp.dot(a, b, preferred_element_type=F32)


def dot_t(a, b):
    return lax.dot_general(a, b, (((1,), (1,)), ((), ())), preferred_element_type=F32)


def t_dot(a, b):
    return lax.dot_general(a, b, (((0,), (0,)), ((), ())), preferred_element_type=F32)


def flat(value):
    return value.reshape(-1, value.shape[-1])


def tile(j, size=256):
    return pl.ds(pl.multiple_of(j * size, size), size)


def rms_inverse(values):
    return lax.rsqrt(jnp.mean(values * values, axis=-1, keepdims=True) + norm_eps)


def steps(count, body):
    def run(i, carry):
        body(i)
        return carry

    lax.fori_loop(0, count, run, 0)


REST = (slice(None),) * 4
MIXER, FEED = (0, 1, 2), (3, 4, 5)
ROWS, WIDTH, HALF = 256, 1024, 512


def row_blocks(body, size=32):
    per = ROWS // size

    def run(i):
        body(lax.div(i, per), tile(lax.rem(i, per), size))

    steps(2 * per, run)


def picker():
    shape = (16, 128)
    same = lax.broadcasted_iota(jnp.int32, shape, 0) == lax.broadcasted_iota(jnp.int32, shape, 1)
    return jnp.where(same, 1.0, 0.0).astype(BF16)


def gather_kernel(*refs):
    count = len(ARRAYS)
    refs = list(refs)

    def take(n):
        taken = refs[:n]
        del refs[:n]
        return taken

    gain1, gain2, tap_rows, in_rows, out_rows, gate_rows, up_rows, down_rows, tok, cot = take(10)
    w_b, w_c, w_x, out_half, gate_full, up_full, down_half, tok_pair, cot_pair = take(9)
    results = take(9)
    (small,) = take(1)
    given, theirs, block = take(count), take(count), take(count)
    down32, small32 = take(2)
    full = take(count)
    toks, mix, mix2, outw, halo, cots, landed = take(7)
    res, hid1, hid2, b_mat, c_mat, x_mat, gated, y_mat, cot16 = held = take(9)
    sends, recvs, local = refs
    at, core = position()
    sibling = device(at, 1 - core)
    enter(at, core)
    sent, kept = [], []

    def start(copy):
        copy.start()
        return copy

    def send(src, dst, target, sem):
        sent.append(start(remote(src, dst, sends, recvs, target, sem)))

    def arrived(ref, sem):
        remote(ref, ref, sends, recvs, sibling, sem).wait_recv()

    def keep(src, dst, sem):
        kept.append(start(pltpu.make_async_copy(src, dst, local.at[sem])))
        return kept[-1]

    down32[...] = jnp.zeros_like(down32)
    for c in range(2):

        @pl.when(core == c)
        def _():
            down32[36 * c : 36 * c + 36, :] = down_rows[...].astype(F32)

    small32[...] = jnp.zeros_like(small32)
    small32[0:1, 0:8] = gain1[...].astype(F32)
    small32[1:2, 0:8] = gain2[...].astype(F32)
    small32[2:5, 0:8] = tap_rows[...].astype(F32)
    small_rows = t_dot(small32[...].astype(BF16), picker())[0:8, :]

    def spread(rows):
        both = jnp.concatenate([rows.astype(F32)] * 2, axis=0)
        mine = lax.broadcasted_iota(jnp.int32, both.shape, 0) // 8 == core
        return jnp.where(mine, both, 0.0).astype(BF16)

    def fill(k, half, dst):
        def columns(ref, first, size):
            return ref[:, pl.ds(pl.multiple_of(first, 128), size)]

        if k < 3:
            dst[:, 0:HALF] = spread(columns(in_rows, k * WIDTH + half * HALF, HALF))
        if k == 0:
            dst[:, HALF : HALF + 128] = spread(small_rows)
        elif k < 3:
            dst[:, HALF : HALF + 256] = spread(
                columns(out_rows, half * HALF + 256 * (k - 1), 256)
            )
        elif k < 5:
            dst[...] = spread(columns(gate_rows if k == 3 else up_rows, half * 2304, 2304))
        else:
            dst[...] = columns(down32, half * HALF, HALF).astype(BF16)

    for k in range(count):
        fill(k, 1 - core, given[k])
        send(given[k], theirs[k], sibling, 12 * count + k)
    for k in range(count):
        fill(k, core, block[k])
    own_copies = []
    here = (at["y"], lax.rem(at["x"], 2), at["z"], lax.div(at["x"], 2))
    for k in range(count):
        arrived(theirs[k], 12 * count + k)
        block[k][...] = block[k][...] + theirs[k][...]
        own_copies.append(
            start(pltpu.make_async_copy(block[k], full[k].at[here], local.at[k]))
        )
        for by, sem in ((1, 0), (3, 1)):
            send(
                block[k],
                full[k].at[here],
                device(moved(at, ARRAYS[k][1][0], by), core),
                12 * k + sem,
            )
    send(tok, toks.at[core], sibling, 13 * count)
    own_tok = start(pltpu.make_async_copy(tok, toks.at[core], local.at[count]))
    send(cot, cots.at[core], sibling, 13 * count + 1)
    own_cot = start(pltpu.make_async_copy(cot, cots.at[core], local.at[count + 1]))

    def piece_index(place, whole, late):
        spot = list(chip_index(place, whole))
        spot[0 if "y" in whole else 2] = pl.ds(3, 1) if late else pl.ds(0, 3)
        return tuple(spot)

    def begin_feed(late):
        for k in FEED:
            order = ARRAYS[k][1]
            mine = full[k].at[piece_index(at, order[:2], late)]
            for by, sem in ((1, 0), (3, 1)):
                index = 16 * count + 2 * (k - 3) + sem if late else 12 * k + 8 + sem
                send(mine, mine, device(moved(at, order[2], by), core), index)

    def pass_on(k, phase):
        (_, columns), order = ARRAYS[k]
        axis, whole, base = order[phase], order[:phase], 12 * k + 4 * phase
        right, left = moved(at, axis, 1), moved(at, axis, 3)
        for source, part, target, sem in zip((left, right), halves(columns), (right, left), (0, 1)):
            if phase == 2 and k in FEED:
                for late in range(2):
                    spot = piece_index(source, whole, late)
                    arrived(full[k].at[spot], 16 * count + 2 * (k - 3) + sem if late else base + sem)
            else:
                arrived(full[k].at[chip_index(source, whole)], base + sem)
            piece = full[k].at[(*chip_index(source, whole), slice(None), part)]
            send(piece, piece, device(target, core), base + 2 + sem)

    def complete(k, phase):
        (_, columns), order = ARRAYS[k]
        whole, base = order[:phase], 12 * k + 4 * phase
        across = moved(at, order[phase], 2)
        for part, sem in zip(halves(columns), (2, 3)):
            arrived(full[k].at[(*chip_index(across, whole), slice(None), part)], base + sem)
        if phase == 0:
            own_copies[k].wait()

    def begin(k, phase):
        order = ARRAYS[k][1]
        mine = full[k].at[chip_index(at, order[:phase])]
        for by, sem in ((1, 0), (3, 1)):
            send(mine, mine, device(moved(at, order[phase], by), core), 12 * k + 4 * phase + sem)

    def give_half(k, dst, columns, sem):
        mine = full[k].at[(pl.ds(2 * core, 2), *REST, columns)]
        other = full[k].at[(pl.ds(2 - 2 * core, 2), *REST, columns)]
        send(other, dst, sibling, sem)
        return start(pltpu.make_async_copy(mine, dst, local.at[10 + k]))

    def each(step, arrays, phase):
        for k in arrays:
            step(k, phase)

    each(pass_on, MIXER, 0)
    each(pass_on, FEED, 0)
    each(complete, MIXER, 0)
    each(begin, MIXER, 1)
    each(complete, FEED, 0)
    each(begin, FEED, 1)
    each(pass_on, MIXER, 1)
    each(complete, MIXER, 1)
    each(begin, MIXER, 2)
    each(pass_on, FEED, 1)
    each(complete, FEED, 1)
    each(pass_on, MIXER, 2)
    begin_feed(False)
    each(complete, MIXER, 2)
    own_out = [
        give_half(
            k,
            outw.at[(core, *REST, slice(None), slice(256 * k - 256, 256 * k))],
            slice(HALF, HALF + 256),
            14 * count + k,
        )
        for k in (1, 2)
    ]
    own_cot.wait()
    arrived(cots.at[1 - core], 13 * count + 1)
    keep(cots, cot_pair, 23)

    def round_cot(c, rows):
        cot16[c, rows, :] = cots[c, rows, :].astype(BF16)

    row_blocks(round_cot)
    left = slice(0, 512)

    def hand_over(*which):
        for i in which:
            keep(held[i], results[i], 24 + i)

    hand_over(8)
    keep(full[0].at[(*REST, slice(None), left)], w_b, 18)
    keep(full[1].at[(*REST, slice(None), left)], w_c, 19)
    keep(full[2].at[(*REST, slice(None), left)], w_x, 20)

    small[...] = dot_t(picker(), flat(full[0][:, :, :, :, :, 512:640]))
    own_tok.wait()
    arrived(toks.at[1 - core], 13 * count)
    keep(toks, tok_pair, 21)

    def norm_one(c, rows):
        t = toks[c, rows, :]
        hid1[c, rows, :] = (t * rms_inverse(t) * small[0:1, :]).astype(BF16)

    row_blocks(norm_one)

    def project(i):
        c, j = lax.div(i, 2), tile(lax.rem(i, 2))
        h = hid1[c]
        b = dot(h, flat(full[0][:, :, :, :, :, j]))
        x = dot(h, flat(full[2][:, :, :, :, :, j]))
        b_mat[c, :, j] = b
        x_mat[c, :, j] = x
        gated[c, pl.ds(8, ROWS), j] = b * x
        c_mat[c, pl.ds(0, ROWS), j] = dot(h, flat(full[1][:, :, :, :, :, j]))

    steps(4, project)
    send(gated.at[:, pl.ds(ROWS, 8), :], halo, next_block(1), 13 * count + 4)
    begin_feed(True)
    hand_over(1, 3, 4, 5)
    arrived(halo, 13 * count + 4)
    each(pass_on, FEED, 2)
    starts = lax.axis_index("seq") == 0
    taps = [small[2 + i : 3 + i, tile(core, HALF)] for i in range(3)]
    for c in range(2):
        gated[c, 0:8, :] = jnp.where(starts, 0.0, halo[c])
        for r in range(0, ROWS, 64):
            conv = taps[0] * gated[c, r + 6 : r + 70, :]
            conv = conv + taps[1] * gated[c, r + 7 : r + 71, :]
            conv = conv + taps[2] * gated[c, r + 8 : r + 72, :]
            y_mat[c, r : r + 64, :] = (c_mat[c, r : r + 64, :] * conv).astype(BF16)

    hand_over(6, 7)

    for k in (1, 2):
        own_out[k - 1].wait()
        part = (1 - core, *REST, slice(None), slice(256 * k - 256, 256 * k))
        arrived(outw.at[part], 14 * count + k)
    keep(outw, out_half, 22)

    def mixing(i):
        c, h, j = lax.div(i, 4), lax.rem(lax.div(i, 2), 2), lax.rem(i, 2)
        weight = outw[h, :, :, :, :, :, tile(j)]
        mix[c, :, tile(2 * h + j)] = dot(y_mat[c], flat(weight))

    steps(8, mixing)
    send(mix, mix2, sibling, 13 * count + 3)

    def columns(half):
        return tile(half, HALF)

    def feed_out(step):
        for k, dst in ((3, gate_full), (4, up_full)):
            order = ARRAYS[k][1]
            spot = chip_index(moved(at, order[2], step), order[:2])
            keep(full[k].at[spot], dst.at[spot], 33 + 4 * (k - 3) + step)
        y = lax.rem(at["y"] + step, 4)
        here, there = lax.div(y, 2), lax.rem(y, 2)

        @pl.when(here == core)
        def _():
            out = down_half.at[(there, *REST[:3], slice(None), columns(core))]
            pltpu.make_async_copy(full[5].at[y], out, local.at[41 + step]).start()

        @pl.when(here != core)
        def _():
            remote(full[5].at[y], landed.at[there], sends, recvs, sibling, 15 * count + step).start()

    def feed_land(step):
        y = lax.rem(at["y"] + step, 4)
        here, there = lax.div(y, 2), lax.rem(y, 2)

        @pl.when(here == core)
        def _():
            arrived(landed.at[there], 15 * count + step)
            out = down_half.at[(there, *REST[:3], slice(None), columns(1 - core))]
            pltpu.make_async_copy(landed.at[there], out, local.at[45 + step]).start()

    def feed_end(step):
        y = lax.rem(at["y"] + step, 4)
        here, there = lax.div(y, 2), lax.rem(y, 2)

        @pl.when(here == core)
        def _():
            out = down_half.at[(there, *REST[:3], slice(None), columns(core))]
            pltpu.make_async_copy(full[5].at[y], out, local.at[41 + step]).wait()
            out = down_half.at[(there, *REST[:3], slice(None), columns(1 - core))]
            pltpu.make_async_copy(landed.at[there], out, local.at[45 + step]).wait()

        @pl.when(here != core)
        def _():
            remote(
                full[5].at[y], landed.at[there], sends, recvs, sibling, 15 * count + step
            ).wait_send()

    for step in (0, 1, 3):
        feed_out(step)
    arrived(mix2, 13 * count + 3)

    def norm_two(c, rows):
        r = toks[c, rows, :] + (mix[c, rows, :] + mix2[c, rows, :])
        res[c, rows, :] = r
        hid2[c, rows, :] = (r * rms_inverse(r) * small[1:2, :]).astype(BF16)

    row_blocks(norm_two)
    hand_over(0, 2)
    for step in (0, 1, 3):
        feed_land(step)
    each(complete, FEED, 2)
    feed_out(2)
    feed_land(2)
    for step in range(4):
        feed_end(step)
    for copy in sent:
        copy.wait_send()
    for copy in kept:
        copy.wait()


def gather(shards, tok, cot):
    count = len(ARRAYS)
    hbm, vmem = pl.BlockSpec(memory_space=pl.ANY), pl.BlockSpec(memory_space=pltpu.VMEM)
    shape = jax.ShapeDtypeStruct
    pair = (2, ROWS, WIDTH)
    outs = [shape((*CHIPS, 16, HALF), BF16)] * 3 + [shape((2, 2, 2, 4, 2, 16, HALF), BF16)]
    outs += [shape((*CHIPS, *ARRAYS[k][0]), BF16) for k in (3, 4)]
    outs += [shape((2, 2, 4, 2, 72, WIDTH), BF16), shape(pair, F32), shape(pair, F32)]
    held = [
        shape(pair, F32),
        shape(pair, BF16),
        shape(pair, BF16),
        shape((2, ROWS, HALF), F32),
        shape((2, ROWS + 8, HALF), F32),
        shape((2, ROWS, HALF), F32),
        shape((2, ROWS + 8, HALF), F32),
        shape((2, ROWS, HALF), BF16),
        shape(pair, BF16),
    ]
    outs += held
    in_hbm = len(outs)
    outs += [shape((16, WIDTH), F32)]
    blocks = [pltpu.VMEM(array, BF16) for array, _ in ARRAYS]
    return pl.pallas_call(
        gather_kernel,
        out_shape=outs,
        in_specs=[vmem] * len(shards) + [hbm] * 2,
        out_specs=[hbm] * in_hbm + [vmem],
        scratch_shapes=[
            *blocks,
            *blocks,
            *blocks,
            pltpu.VMEM((72, WIDTH), F32),
            pltpu.VMEM((16, 128), F32),
            *[pltpu.VMEM((*CHIPS, *array), BF16) for array, _ in ARRAYS],
            *[pltpu.VMEM(pair, F32)] * 3,
            pltpu.VMEM((2, 2, 2, 4, 2, 16, HALF), BF16),
            pltpu.VMEM((2, 8, HALF), F32),
            pltpu.VMEM(pair, F32),
            pltpu.VMEM((2, 2, 4, 2, 72, HALF), BF16),
            *[pltpu.VMEM(value.shape, value.dtype) for value in held],
            pltpu.SemaphoreType.DMA((17 * count,)),
            pltpu.SemaphoreType.DMA((17 * count,)),
            pltpu.SemaphoreType.DMA((50,)),
        ],
        compiler_params=pltpu.CompilerParams(
            collective_id=0, has_side_effects=True, vmem_limit_bytes=60 * 2**20
        ),
        name="gather_and_mix",
    )(*shards, tok, cot)


def reduce_kernel(factor, *refs):
    count = len(ARRAYS)
    refs = list(refs)

    def take(n):
        taken = refs[:n]
        del refs[:n]
        return taken

    g_gate, g_up, g_down, d_hid2, out_part, in_hbm = *take(5), take(14)
    block_out, input_grad, in_grads, out_grads, gate_grads, up_grads, down_grads, small_grads = take(8)
    totals = take(count)
    data, arriving = take(count), take(12 * count)
    cot, res, hid1, b_mat, c_mat, x_mat, gated, y_mat, outw, small = held = take(10)
    dh, dh2, d1r, dres, g_out, halo, ffn_own, ffn_other = take(8)
    d_proj, (g_small, small_sum) = take(3), take(2)
    sends, recvs, local = refs
    at, core = position()
    sibling = device(at, 1 - core)
    enter(at, core)
    sent = []

    def send(src, dst, target, sem):
        copy = remote(src, dst, sends, recvs, target, sem)
        copy.start()
        sent.append(copy)

    def arrived(ref, sem):
        remote(ref, ref, sends, recvs, sibling, sem).wait_recv()

    def load(src, dst, sem):
        copy = pltpu.make_async_copy(src, dst, local.at[sem])
        copy.start()
        return copy

    def buffer(k, phase, which):
        return arriving[12 * k + 4 * phase + which]

    def add(k, phase, where, sources, columns, total=None):
        sizes = sources[0].shape[:4]

        def body(t):
            i3 = lax.rem(t, sizes[3])
            t3 = lax.div(t, sizes[3])
            i2 = lax.rem(t3, sizes[2])
            t2 = lax.div(t3, sizes[2])
            i1 = lax.rem(t2, sizes[1])
            i0 = lax.div(t2, sizes[1])
            spot = tuple(i + b for i, b in zip((i0, i1, i2, i3), where))
            value = data[k][(*spot, slice(None), columns)].astype(F32)
            for source in sources:
                value = value + source[i0, i1, i2, i3].astype(F32)
            if total is None:
                data[k][(*spot, slice(None), columns)] = value.astype(BF16)
            else:
                total[...] = value

        steps(math.prod(sizes), body)

    def start_of(place, whole):
        y = 0 if "y" in whole else place["y"]
        z = 0 if "z" in whole else place["z"]
        if "x" in whole:
            return (y, 0, z, 0)
        return (y, lax.rem(place["x"], 2), z, lax.div(place["x"], 2))

    def begin(k, phase):
        (_, columns), order = ARRAYS[k]
        axis, whole = order[2 - phase], order[: 2 - phase]
        across = chip_index(moved(at, axis, 2), whole)
        for part, which, by in zip(halves(columns), (0, 1), (1, 3)):
            send(
                data[k].at[(*across, slice(None), part)],
                buffer(k, phase, which),
                device(moved(at, axis, by), core),
                12 * k + 4 * phase + which,
            )

    def pass_on(k, phase):
        (_, columns), order = ARRAYS[k]
        axis, whole = order[2 - phase], order[: 2 - phase]
        base = 12 * k + 4 * phase
        for part, which, by in zip(halves(columns), (0, 1), (1, 3)):
            near = moved(at, axis, by)
            arrived(buffer(k, phase, which), base + which)
            add(k, phase, start_of(near, whole), [buffer(k, phase, which)], part)
            send(
                data[k].at[chip_index(near, whole)],
                buffer(k, phase, 2 + which),
                device(near, core),
                base + 2 + which,
            )

    def complete(k, phase):
        whole = ARRAYS[k][1][: 2 - phase]
        base = 12 * k + 4 * phase
        both = [buffer(k, phase, 2), buffer(k, phase, 3)]
        arrived(both[0], base + 2)
        arrived(both[1], base + 3)
        total = totals[k].at[core] if phase == 2 else None
        add(k, phase, start_of(at, whole), both, slice(None), total)
        if phase < 2:
            begin(k, phase + 1)
        else:
            send(total, total, sibling, 13 * count + k)

    def each(step, arrays, phase):
        for k in arrays:
            step(k, phase)

    def slab(step, start):
        y = lax.rem(at["y"] + step, 4)
        here, there = lax.div(y, 2), lax.rem(y, 2)

        def of(half):
            return g_down.at[(there, *REST[:3], slice(None), tile(half, HALF))]

        own = pltpu.make_async_copy(of(core), data[5].at[y], local.at[21 + step])
        given = remote(of(1 - core), data[5].at[y], sends, recvs, sibling, 15 * count + step)

        @pl.when(here == core)
        def _():
            if start:
                given.start()
                own.start()
            else:
                own.wait()

        @pl.when(here != core)
        def _():
            if not start:
                given.wait_recv()

    def slab_sent(step):
        y = lax.rem(at["y"] + step, 4)
        there = lax.rem(y, 2)
        src = g_down.at[(there, *REST[:3], slice(None), tile(1 - core, HALF))]

        @pl.when(lax.div(y, 2) == core)
        def _():
            remote(src, data[5].at[y], sends, recvs, sibling, 15 * count + step).wait_send()

    ring = (2, 1, 3, 0)
    feed_loads = {}
    for step in ring:
        for k, src in ((3, g_gate), (4, g_up)):
            order = ARRAYS[k][1]
            spot = chip_index(moved(at, order[2], step), order[:2])
            feed_loads[k, step] = load(src.at[spot], data[k].at[spot], 25 + 4 * (k - 3) + step)
        slab(step, True)
    send(d_hid2, dh2, sibling, 12 * count)
    send(out_part.at[1 - core], ffn_other, sibling, 12 * count + 2)
    first_loads = [load(d_hid2, dh, 6)]
    first_loads += [load(in_hbm[i], held[i], 7 + i) for i in (0, 1, 9)]
    rest_loads = [load(in_hbm[i], held[i], 7 + i) for i in range(2, 9)]
    left = slice(0, HALF)
    for k in MIXER:
        dst = data[k].at[(*REST, slice(None), left)]
        rest_loads.append(load(in_hbm[10 + k], dst, 17 + k))
    for k in (3, 4):
        feed_loads[k, 2].wait()
        begin(k, 0)
    slab(2, False)
    begin(5, 0)
    ffn_load = load(out_part.at[core], ffn_own, 33)
    for copy in first_loads:
        copy.wait()
    arrived(dh2, 12 * count)
    g_small[...] = jnp.zeros_like(g_small)

    def norm_two(c, rows):
        r = res[c, rows, :]
        inv = rms_inverse(r)
        normed = r * inv
        d = dh[c, rows, :] + dh2[c, rows, :]
        g_small[1:2, :] += 0.5 * jnp.sum(d * normed, axis=0, keepdims=True)
        scaled = d * small[1:2, :]
        mean = jnp.mean(scaled * normed, axis=-1, keepdims=True)
        out = cot[c, rows, :] + inv * (scaled - normed * mean)
        cot[c, rows, :] = out
        dres[c, rows, :] = out.astype(BF16)

    row_blocks(norm_two)
    ffn_load.wait()
    arrived(ffn_other, 12 * count + 2)

    def add_ffn(i):
        rows = tile(i, 32)
        block_out[rows, :] = res[core, rows, :] + (ffn_own[rows, :] + ffn_other[rows, :])

    steps(ROWS // 32, add_ffn)
    tok_load = load(in_hbm[13], res, 20)
    for copy in rest_loads:
        copy.wait()

    taps = [small[2 + i : 3 + i, tile(core, HALF)] for i in range(3)]
    for c in range(2):
        for j in range(2):
            cols = slice(256 * j, 256 * j + 256)
            d_y = dot_t(dres[c, :, 0:HALF], flat(outw[0, j]))
            d_y = d_y + dot_t(dres[c, :, HALF:WIDTH], flat(outw[1, j]))
            conv = sum(taps[i][:, cols] * gated[c, 6 + i : 6 + i + ROWS, cols] for i in range(3))
            d_proj[1][c, :, cols] = (d_y * conv).astype(BF16)
            c_mat[c, 0:ROWS, cols] = d_y * c_mat[c, 0:ROWS, cols]
    send(c_mat.at[:, pl.ds(0, 8), :], halo, next_block(31), 12 * count + 3)
    for step in ring[1:]:
        feed_loads[3, step].wait()
        feed_loads[4, step].wait()
        slab(step, False)
    each(pass_on, FEED, 0)

    def out_grad(i):
        f = i
        for j in range(2):
            other = sum(
                t_dot(y_mat[c, :, tile(f)], dres[c, :, tile(2 - 2 * core + j)]) for c in range(2)
            )
            g_out[f, :, :, :, :, 256 * j : 256 * j + 256] = other.astype(BF16).reshape(
                2, 4, 2, 16, 256
            )
            own = sum(
                t_dot(y_mat[c, :, tile(f)], dres[c, :, tile(2 * core + j)]) for c in range(2)
            )
            data[1 + j][2 * core + f, :, :, :, :, HALF : HALF + 256] = own.astype(BF16).reshape(
                2, 4, 2, 16, 256
            )

    steps(2, out_grad)
    right = slice(HALF, HALF + 256)
    for j in range(2):
        send(
            g_out.at[(slice(None), *REST, slice(256 * j, 256 * j + 256))],
            data[1 + j].at[(pl.ds(2 * core, 2), *REST, right)],
            sibling,
            14 * count + j,
        )
    arrived(halo, 12 * count + 3)
    ends = lax.axis_index("seq") == 31
    for c in range(2):
        c_mat[c, ROWS : ROWS + 8, :] = jnp.where(ends, 0.0, halo[c])
        for r in range(0, ROWS, 64):
            d_conv = c_mat[c, r : r + 64, :]
            for i in range(3):
                part = jnp.sum(
                    d_conv * gated[c, r + 6 + i : r + 70 + i, :], axis=0, keepdims=True
                )
                g_small[2 + i : 3 + i, tile(core, HALF)] += part
            d_gated = taps[0] * c_mat[c, r + 2 : r + 66, :]
            d_gated = d_gated + taps[1] * c_mat[c, r + 1 : r + 65, :] + taps[2] * d_conv
            d_proj[0][c, r : r + 64, :] = (d_gated * x_mat[c, r : r + 64, :]).astype(BF16)
            d_proj[2][c, r : r + 64, :] = (d_gated * b_mat[c, r : r + 64, :]).astype(BF16)

    def back(i):
        c, y = lax.div(i, 4), lax.rem(i, 4)
        value = None
        for k in MIXER:
            part = dot_t(d_proj[k][c], flat(data[k][y, :, :, :, :, 0:HALF]))
            value = part if value is None else value + part
        dh[c, :, tile(y)] = value

    steps(8, back)
    send(dh.at[1 - core], d1r, sibling, 12 * count + 1)

    def in_grad(i):
        y, j = lax.div(i, 2), tile(lax.rem(i, 2))
        for k in MIXER:
            value = sum(t_dot(hid1[c, :, tile(y)], d_proj[k][c, :, j]) for c in range(2))
            data[k][y, :, :, :, :, j] = value.astype(BF16).reshape(2, 4, 2, 16, 256)

    steps(8, in_grad)
    tok_load.wait()

    def gain_one(c, rows):
        t = res[c, rows, :]
        g_small[0:1, :] += jnp.sum(dh[c, rows, :] * (t * rms_inverse(t)), axis=0, keepdims=True)

    row_blocks(gain_one)
    turned = t_dot(g_small[...].astype(BF16), picker()).astype(BF16)
    data[0][:, :, :, :, :, HALF : HALF + 128] = turned.reshape(*CHIPS, 16, 128)
    for j in range(2):
        arrived(data[1 + j].at[(pl.ds(2 - 2 * core, 2), *REST, right)], 14 * count + j)
    each(begin, MIXER, 0)
    each(complete, FEED, 0)
    each(pass_on, MIXER, 0)
    each(pass_on, FEED, 1)
    arrived(d1r, 12 * count + 1)

    def norm_one(i):
        rows = tile(i, 32)
        t = res[core, rows, :]
        inv = rms_inverse(t)
        normed = t * inv
        scaled = (dh[core, rows, :] + d1r[rows, :]) * small[0:1, :]
        mean = jnp.mean(scaled * normed, axis=-1, keepdims=True)
        input_grad[rows, :] = cot[core, rows, :] + inv * (scaled - normed * mean)

    steps(ROWS // 32, norm_one)
    each(complete, MIXER, 0)
    each(complete, FEED, 1)
    each(pass_on, MIXER, 1)
    each(pass_on, FEED, 2)
    each(complete, MIXER, 1)
    each(complete, FEED, 2)
    each(pass_on, MIXER, 2)
    each(complete, MIXER, 2)
    for k in range(count):
        arrived(totals[k].at[1 - core], 13 * count + k)
    mine = pl.ds(pl.multiple_of(8 * core, 8), 8)
    for h in range(2):
        at_half = slice(HALF * h, HALF * h + HALF)
        for k in MIXER:
            in_grads[:, WIDTH * k + HALF * h : WIDTH * k + HALF * h + HALF] = (
                totals[k][h, mine, 0:HALF] * factor
            )
        for k in (1, 2):
            first = HALF * h + 256 * (k - 1)
            out_grads[:, first : first + 256] = totals[k][h, mine, HALF : HALF + 256] * factor
        for k, dst in ((3, gate_grads), (4, up_grads)):
            dst[:, 2304 * h : 2304 * h + 2304] = totals[k][h, mine, :] * factor
        down_grads[:, at_half] = factor * jnp.where(
            core == 0, totals[5][h, 0:36, :], totals[5][h, 36:72, :]
        )
    small_sum[...] = jnp.zeros_like(small_sum)
    small_sum[0:8, :] = factor * (
        totals[0][0, mine, HALF : HALF + 128] + totals[0][1, mine, HALF : HALF + 128]
    )
    small_grads[...] = small_sum[...].T[0:8, :]
    for step in ring:
        slab_sent(step)
    for copy in sent:
        copy.wait_send()


def reduce(factor, g_gate, g_up, g_down, d_hid2, out_part, *rest):
    count = len(ARRAYS)
    hbm, vmem = pl.BlockSpec(memory_space=pl.ANY), pl.BlockSpec(memory_space=pltpu.VMEM)
    buffers = []
    for (rows, columns), order in ARRAYS:
        for phase in range(3):
            whole = order[: 2 - phase]
            lead = (
                4 if "y" in whole else 1,
                2 if "x" in whole else 1,
                4 if "z" in whole else 1,
                2 if "x" in whole else 1,
            )
            for part in halves(columns):
                buffers.append(pltpu.VMEM((*lead, rows, part.stop - part.start), BF16))
            buffers += [pltpu.VMEM((*lead, rows, columns), BF16)] * 2
    pair = pltpu.VMEM((2, ROWS, WIDTH), F32)
    operands = (g_gate, g_up, g_down, d_hid2, out_part, *rest)
    return pl.pallas_call(
        functools.partial(reduce_kernel, factor),
        out_shape=[
            jax.ShapeDtypeStruct(shape, F32)
            for shape in (
                (ROWS, WIDTH),
                (ROWS, WIDTH),
                (8, 3 * WIDTH),
                (8, WIDTH),
                (8, 4608),
                (8, 4608),
                (36, WIDTH),
                (8, 128),
            )
        ],
        in_specs=[hbm] * len(operands),
        out_specs=[vmem] * 8,
        scratch_shapes=[
            *[pltpu.VMEM((2, *shape), F32) for shape, _ in ARRAYS],
            *[pltpu.VMEM((*CHIPS, *shape), BF16) for shape, _ in ARRAYS],
            *buffers,
            *[pltpu.VMEM(value.shape, value.dtype) for value in rest[:10]],
            pair,
            pair,
            pltpu.VMEM((ROWS, WIDTH), F32),
            pltpu.VMEM((2, ROWS, WIDTH), BF16),
            pltpu.VMEM((2, 2, 4, 2, 16, HALF), BF16),
            pltpu.VMEM((2, 8, HALF), F32),
            pltpu.VMEM((ROWS, WIDTH), F32),
            pltpu.VMEM((ROWS, WIDTH), F32),
            *[pltpu.VMEM((2, ROWS, HALF), BF16)] * 3,
            pltpu.VMEM((16, WIDTH), F32),
            pltpu.VMEM((128, 128), F32),
            pltpu.SemaphoreType.DMA((16 * count,)),
            pltpu.SemaphoreType.DMA((16 * count,)),
            pltpu.SemaphoreType.DMA((34,)),
        ],
        compiler_params=pltpu.CompilerParams(
            collective_id=1, has_side_effects=True, vmem_limit_bytes=63 * 2**20
        ),
        name="sum_gradients",
    )(*operands)


def finish_kernel(*refs):
    count = (len(refs) - 5) // 2
    small, (one, taps, two) = refs[count], refs[2 * count + 1 : 2 * count + 4]
    copies = [
        pltpu.make_async_copy(refs[i], refs[count + 1 + i], refs[-1].at[i]) for i in range(count)
    ]
    for copy in copies:
        copy.start()
    one[...] = small[0:1, 0:8]
    two[...] = small[1:2, 0:8]
    taps[...] = small[2:5, 0:8]
    for copy in copies:
        copy.wait()


def finish(*values):
    hbm, vmem = pl.BlockSpec(memory_space=pl.ANY), pl.BlockSpec(memory_space=pltpu.VMEM)
    outs = [jax.ShapeDtypeStruct(v.shape, v.dtype) for v in values[:-1]]
    rows = [jax.ShapeDtypeStruct((r, 8), F32) for r in (1, 3, 1)]
    return pl.pallas_call(
        finish_kernel,
        out_shape=outs + rows,
        in_specs=[vmem] * len(values),
        out_specs=[hbm] * len(outs) + [vmem] * 3,
        scratch_shapes=[pltpu.SemaphoreType.DMA((len(values),))],
        name="finish",
    )(*values)


def shards(
    tokens,
    cotangent,
    norm1_gain,
    in_weight,
    conv_taps,
    out_weight,
    norm2_gain,
    gate_weight,
    up_weight,
    down_weight,
):
    width = tokens.shape[-1]
    inputs = tokens.reshape(-1, width)
    upstream = cotangent.reshape(-1, width)
    rows = inputs.shape[0]
    total_rows = rows * lax.axis_size("seq") * lax.axis_size("fsdp")
    factor = 1.0 / math.sqrt(total_rows)
    core = lax.rem(lax.axis_index("fsdp"), 2)

    pieces = (
        norm1_gain.reshape(1, -1),
        norm2_gain.reshape(1, -1),
        conv_taps,
        in_weight,
        out_weight,
        gate_weight,
        up_weight,
        down_weight,
    )
    w_b, w_c, w_x, w_out, w_gate, w_up, w_down, tok, cot, *kept = gather(pieces, inputs, upstream)
    resid, hidden_one, hidden_two, b_mat, c_mat, x_mat, gated, y_mat, cot_half, small = kept
    w_gate = w_gate.reshape(width, -1)
    w_up = w_up.reshape(width, -1)
    w_down = w_down.reshape(-1, width)
    hid2 = hidden_two.reshape(-1, width)
    gate, up_vals = dot(hid2, w_gate), dot(hid2, w_up)
    sigma = jax.nn.sigmoid(gate)
    act = (gate * sigma * up_vals).astype(BF16)
    out_part = dot(act, w_down)
    cot_half = cot_half.reshape(-1, width)
    g_down = t_dot(act, cot_half).astype(BF16)
    d_act = dot_t(cot_half, w_down)
    d_gate = (d_act * up_vals * sigma * (1.0 + gate * (1.0 - sigma))).astype(BF16)
    d_up = (d_act * gate * sigma).astype(BF16)
    g_gate = t_dot(hid2, d_gate).astype(BF16)
    g_up = t_dot(hid2, d_up).astype(BF16)
    d_hid2 = dot_t(d_gate, w_gate) + dot_t(d_up, w_up)
    block_out, input_grad, g_in, g_out, g_gate, g_up, g_down, g_small = reduce(
        factor,
        g_gate.reshape(*CHIPS, 16, 2304),
        g_up.reshape(*CHIPS, 16, 2304),
        g_down.reshape(2, 2, 4, 2, 72, width),
        d_hid2.reshape(2, rows, width),
        out_part.reshape(2, rows, width),
        cot,
        resid,
        hidden_one,
        b_mat,
        c_mat,
        x_mat,
        gated,
        y_mat,
        w_out,
        small,
        w_b,
        w_c,
        w_x,
        tok,
    )

    block_out, input_grad, g_in, g_out, g_gate, g_up, g_down, g_one, g_taps, g_two = finish(
        block_out, input_grad, g_in, g_out, g_gate, g_up, g_down, g_small
    )
    return (
        block_out.reshape(tokens.shape),
        input_grad.reshape(tokens.shape),
        g_one.reshape(-1),
        g_in,
        g_taps,
        g_out,
        g_two.reshape(-1),
        g_gate,
        g_up,
        g_down,
    )


def solution(mesh):
    tokens = P("fsdp", "seq", None)
    vector, matrix, taps = P(("seq", "fsdp")), P(("seq", "fsdp"), None), P(None, ("seq", "fsdp"))
    weights = (vector, matrix, taps, matrix, vector, matrix, matrix, matrix)
    return jax.shard_map(
        shards,
        mesh=mesh,
        in_specs=(tokens, tokens, *weights),
        out_specs=(tokens, tokens, *weights),
        check_vma=False,
    )
```

```python
import functools
import math

import jax
import jax.numpy as jnp
from jax import lax
from jax.experimental import pallas as pl
from jax.experimental.pallas import tpu as pltpu
from jax.sharding import PartitionSpec as P

norm_eps = 1e-05
MESH = pl.DeviceIdType.MESH
F32, BF16 = jnp.float32, jnp.bfloat16

CHIPS = (4, 2, 4, 2)
ARRAYS = (
    ((16, 640), "xyz"),
    ((16, 768), "yzx"),
    ((16, 768), "zxy"),
    ((16, 2304), "xyz"),
    ((16, 2304), "yzx"),
    ((72, 512), "zxy"),
)


def position():
    s, f = lax.axis_index("seq"), lax.axis_index("fsdp")
    y, x_lo, z = lax.div(s, 8), lax.rem(lax.div(s, 4), 2), lax.rem(s, 4)
    x_hi, core = lax.div(f, 2), lax.rem(f, 2)
    return {"x": x_hi * 2 + x_lo, "y": y, "z": z}, core


def device(at, core):
    x_lo, x_hi = lax.rem(at["x"], 2), lax.div(at["x"], 2)
    return ((at["y"] * 2 + x_lo) * 4 + at["z"], x_hi * 2 + core)


def moved(at, axis, by):
    return {**at, axis: lax.rem(at[axis] + by, 4)}


def chip_index(at, whole):
    y = slice(None) if "y" in whole else pl.ds(at["y"], 1)
    z = slice(None) if "z" in whole else pl.ds(at["z"], 1)
    if "x" in whole:
        x_lo = x_hi = slice(None)
    else:
        x_lo, x_hi = pl.ds(lax.rem(at["x"], 2), 1), pl.ds(lax.div(at["x"], 2), 1)
    return (y, x_lo, z, x_hi)


def halves(columns):
    first = (columns // 128 + 1) // 2 * 128
    return slice(0, first), slice(first, columns)


def arrive(at, core):
    barrier = pltpu.get_barrier_semaphore()
    for axis in "xyz":
        for by in (1, 2, 3):
            pl.semaphore_signal(
                barrier, inc=1, device_id=device(moved(at, axis, by), core), device_id_type=MESH
            )
    for other in (device(at, 1 - core), next_block(1), next_block(31)):
        pl.semaphore_signal(barrier, inc=1, device_id=other, device_id_type=MESH)


def meet():
    pl.semaphore_wait(pltpu.get_barrier_semaphore(), 12)


def next_block(by):
    return (lax.rem(lax.axis_index("seq") + by, 32), lax.axis_index("fsdp"))


def remote(src, dst, sends, recvs, target, sem):
    return pltpu.make_async_remote_copy(
        src_ref=src,
        dst_ref=dst,
        send_sem=sends.at[sem],
        recv_sem=recvs.at[sem],
        device_id=target,
        device_id_type=MESH,
    )


def dot(a, b):
    return jnp.dot(a, b, preferred_element_type=F32)


def dot_t(a, b):
    return lax.dot_general(a, b, (((1,), (1,)), ((), ())), preferred_element_type=F32)


def t_dot(a, b):
    return lax.dot_general(a, b, (((0,), (0,)), ((), ())), preferred_element_type=F32)


def flat(value):
    return value.reshape(-1, value.shape[-1])


def tile(j, size=256):
    return pl.ds(pl.multiple_of(j * size, size), size)


def rms_inverse(values):
    return lax.rsqrt(jnp.mean(values * values, axis=-1, keepdims=True) + norm_eps)


def steps(count, body):
    def run(i, carry):
        body(i)
        return carry

    lax.fori_loop(0, count, run, 0)


REST = (slice(None),) * 4
MIXER, FEED = (0, 1, 2), (3, 4, 5)
ROWS, WIDTH, HALF = 256, 1024, 512


def row_blocks(body, size=32):
    per = ROWS // size

    def run(i):
        body(lax.div(i, per), tile(lax.rem(i, per), size))

    steps(2 * per, run)


def picker():
    shape = (16, 128)
    same = lax.broadcasted_iota(jnp.int32, shape, 0) == lax.broadcasted_iota(jnp.int32, shape, 1)
    return jnp.where(same, 1.0, 0.0).astype(BF16)


def gather_kernel(*refs):
    count = len(ARRAYS)
    refs = list(refs)

    def take(n):
        taken = refs[:n]
        del refs[:n]
        return taken

    gain1, gain2, tap_rows, in_rows, out_rows, gate_rows, up_rows, down_rows, tok, cot = take(10)
    w_b, w_c, w_x, out_half, gate_full, up_full, down_half, tok_pair, cot_pair = take(9)
    results = take(9)
    (small,) = take(1)
    given, theirs, block = take(count), take(count), take(count)
    down32, small32 = take(2)
    full = take(count)
    toks, mix, mix2, outw, halo, cots, landed = take(7)
    res, hid1, hid2, b_mat, c_mat, x_mat, gated, y_mat, cot16 = held = take(9)
    sends, recvs, local = refs
    at, core = position()
    sibling = device(at, 1 - core)
    arrive(at, core)
    sent, kept = [], []

    def start(copy):
        copy.start()
        return copy

    def send(src, dst, target, sem):
        sent.append(start(remote(src, dst, sends, recvs, target, sem)))

    def arrived(ref, sem):
        remote(ref, ref, sends, recvs, sibling, sem).wait_recv()

    def keep(src, dst, sem):
        kept.append(start(pltpu.make_async_copy(src, dst, local.at[sem])))
        return kept[-1]

    down32[...] = jnp.zeros_like(down32)
    for c in range(2):

        @pl.when(core == c)
        def _():
            down32[36 * c : 36 * c + 36, :] = down_rows[...].astype(F32)

    small32[...] = jnp.zeros_like(small32)
    small32[0:1, 0:8] = gain1[...].astype(F32)
    small32[1:2, 0:8] = gain2[...].astype(F32)
    small32[2:5, 0:8] = tap_rows[...].astype(F32)
    small_rows = t_dot(small32[...].astype(BF16), picker())[0:8, :]

    def spread(rows):
        both = jnp.concatenate([rows.astype(F32)] * 2, axis=0)
        mine = lax.broadcasted_iota(jnp.int32, both.shape, 0) // 8 == core
        return jnp.where(mine, both, 0.0).astype(BF16)

    def fill(k, half, dst):
        def columns(ref, first, size):
            return ref[:, pl.ds(pl.multiple_of(first, 128), size)]

        if k < 3:
            dst[:, 0:HALF] = spread(columns(in_rows, k * WIDTH + half * HALF, HALF))
        if k == 0:
            dst[:, HALF : HALF + 128] = spread(small_rows)
        elif k < 3:
            dst[:, HALF : HALF + 256] = spread(
                columns(out_rows, half * HALF + 256 * (k - 1), 256)
            )
        elif k < 5:
            dst[...] = spread(columns(gate_rows if k == 3 else up_rows, half * 2304, 2304))
        else:
            dst[...] = columns(down32, half * HALF, HALF).astype(BF16)

    for k in range(count):
        fill(k, 1 - core, given[k])
        fill(k, core, block[k])
    meet()
    for k in range(count):
        send(given[k], theirs[k], sibling, 12 * count + k)
    own_copies = []
    here = (at["y"], lax.rem(at["x"], 2), at["z"], lax.div(at["x"], 2))
    for k in range(count):
        arrived(theirs[k], 12 * count + k)
        block[k][...] = block[k][...] + theirs[k][...]
        own_copies.append(
            start(pltpu.make_async_copy(block[k], full[k].at[here], local.at[k]))
        )
        for by, sem in ((1, 0), (3, 1), (2, 2)):
            send(
                block[k],
                full[k].at[here],
                device(moved(at, ARRAYS[k][1][0], by), core),
                12 * k + sem,
            )
    send(tok, toks.at[core], sibling, 13 * count)
    own_tok = start(pltpu.make_async_copy(tok, toks.at[core], local.at[count]))
    send(cot, cots.at[core], sibling, 13 * count + 1)
    own_cot = start(pltpu.make_async_copy(cot, cots.at[core], local.at[count + 1]))

    def piece_index(place, whole, late):
        spot = list(chip_index(place, whole))
        spot[0 if "y" in whole else 2] = pl.ds(3, 1) if late else pl.ds(0, 3)
        return tuple(spot)

    def begin_feed(late):
        for k in FEED:
            order = ARRAYS[k][1]
            mine = full[k].at[piece_index(at, order[:2], late)]
            for by, sem in ((1, 0), (3, 1)):
                index = 16 * count + 2 * (k - 3) + sem if late else 12 * k + 8 + sem
                send(mine, mine, device(moved(at, order[2], by), core), index)

    def pass_on(k, phase):
        (_, columns), order = ARRAYS[k]
        axis, whole, base = order[phase], order[:phase], 12 * k + 4 * phase
        right, left = moved(at, axis, 1), moved(at, axis, 3)
        for source, part, target, sem in zip((left, right), halves(columns), (right, left), (0, 1)):
            if phase == 2 and k in FEED:
                for late in range(2):
                    spot = piece_index(source, whole, late)
                    arrived(full[k].at[spot], 16 * count + 2 * (k - 3) + sem if late else base + sem)
            else:
                arrived(full[k].at[chip_index(source, whole)], base + sem)
            piece = full[k].at[(*chip_index(source, whole), slice(None), part)]
            send(piece, piece, device(target, core), base + 2 + sem)

    def complete(k, phase):
        (_, columns), order = ARRAYS[k]
        whole, base = order[:phase], 12 * k + 4 * phase
        if phase == 0:
            for by, sem in ((3, 0), (1, 1), (2, 2)):
                arrived(full[k].at[chip_index(moved(at, order[0], by), whole)], base + sem)
            own_copies[k].wait()
            return
        across = moved(at, order[phase], 2)
        for part, sem in zip(halves(columns), (2, 3)):
            arrived(full[k].at[(*chip_index(across, whole), slice(None), part)], base + sem)

    def begin(k, phase):
        order = ARRAYS[k][1]
        mine = full[k].at[chip_index(at, order[:phase])]
        for by, sem in ((1, 0), (3, 1)):
            send(mine, mine, device(moved(at, order[phase], by), core), 12 * k + 4 * phase + sem)

    def give_half(k, dst, columns, sem):
        mine = full[k].at[(pl.ds(2 * core, 2), *REST, columns)]
        other = full[k].at[(pl.ds(2 - 2 * core, 2), *REST, columns)]
        send(other, dst, sibling, sem)
        return start(pltpu.make_async_copy(mine, dst, local.at[10 + k]))

    def each(step, arrays, phase):
        for k in arrays:
            step(k, phase)

    each(complete, MIXER, 0)
    each(begin, MIXER, 1)
    each(complete, FEED, 0)
    each(begin, FEED, 1)
    each(pass_on, MIXER, 1)
    each(complete, MIXER, 1)
    each(begin, MIXER, 2)
    each(pass_on, FEED, 1)
    each(complete, FEED, 1)
    each(pass_on, MIXER, 2)
    begin_feed(False)
    each(complete, MIXER, 2)
    own_out = [
        give_half(
            k,
            outw.at[(core, *REST, slice(None), slice(256 * k - 256, 256 * k))],
            slice(HALF, HALF + 256),
            14 * count + k,
        )
        for k in (1, 2)
    ]
    own_cot.wait()
    arrived(cots.at[1 - core], 13 * count + 1)
    keep(cots, cot_pair, 23)

    def round_cot(c, rows):
        cot16[c, rows, :] = cots[c, rows, :].astype(BF16)

    row_blocks(round_cot)
    left = slice(0, 512)

    def hand_over(*which):
        for i in which:
            keep(held[i], results[i], 24 + i)

    hand_over(8)
    keep(full[0].at[(*REST, slice(None), left)], w_b, 18)
    keep(full[1].at[(*REST, slice(None), left)], w_c, 19)
    keep(full[2].at[(*REST, slice(None), left)], w_x, 20)

    small[...] = dot_t(picker(), flat(full[0][:, :, :, :, :, 512:640]))
    own_tok.wait()
    arrived(toks.at[1 - core], 13 * count)
    keep(toks, tok_pair, 21)

    def norm_one(c, rows):
        t = toks[c, rows, :]
        hid1[c, rows, :] = (t * rms_inverse(t) * small[0:1, :]).astype(BF16)

    row_blocks(norm_one)

    def project(i):
        c, j = lax.div(i, 2), tile(lax.rem(i, 2))
        h = hid1[c]
        b = dot(h, flat(full[0][:, :, :, :, :, j]))
        x = dot(h, flat(full[2][:, :, :, :, :, j]))
        b_mat[c, :, j] = b
        x_mat[c, :, j] = x
        gated[c, pl.ds(8, ROWS), j] = b * x
        c_mat[c, pl.ds(0, ROWS), j] = dot(h, flat(full[1][:, :, :, :, :, j]))

    steps(4, project)
    send(gated.at[:, pl.ds(ROWS, 8), :], halo, next_block(1), 13 * count + 4)
    begin_feed(True)
    hand_over(1, 3, 4, 5)
    arrived(halo, 13 * count + 4)
    each(pass_on, FEED, 2)
    starts = lax.axis_index("seq") == 0
    taps = [small[2 + i : 3 + i, tile(core, HALF)] for i in range(3)]
    for c in range(2):
        gated[c, 0:8, :] = jnp.where(starts, 0.0, halo[c])
        for r in range(0, ROWS, 64):
            conv = taps[0] * gated[c, r + 6 : r + 70, :]
            conv = conv + taps[1] * gated[c, r + 7 : r + 71, :]
            conv = conv + taps[2] * gated[c, r + 8 : r + 72, :]
            y_mat[c, r : r + 64, :] = (c_mat[c, r : r + 64, :] * conv).astype(BF16)

    hand_over(6, 7)

    for k in (1, 2):
        own_out[k - 1].wait()
        part = (1 - core, *REST, slice(None), slice(256 * k - 256, 256 * k))
        arrived(outw.at[part], 14 * count + k)
    keep(outw, out_half, 22)

    def mixing(i):
        c, h, j = lax.div(i, 4), lax.rem(lax.div(i, 2), 2), lax.rem(i, 2)
        weight = outw[h, :, :, :, :, :, tile(j)]
        mix[c, :, tile(2 * h + j)] = dot(y_mat[c], flat(weight))

    steps(8, mixing)
    send(mix, mix2, sibling, 13 * count + 3)

    def columns(half):
        return tile(half, HALF)

    def feed_out(step):
        for k, dst in ((3, gate_full), (4, up_full)):
            order = ARRAYS[k][1]
            spot = chip_index(moved(at, order[2], step), order[:2])
            keep(full[k].at[spot], dst.at[spot], 33 + 4 * (k - 3) + step)
        y = lax.rem(at["y"] + step, 4)
        here, there = lax.div(y, 2), lax.rem(y, 2)

        @pl.when(here == core)
        def _():
            out = down_half.at[(there, *REST[:3], slice(None), columns(core))]
            pltpu.make_async_copy(full[5].at[y], out, local.at[41 + step]).start()

        @pl.when(here != core)
        def _():
            remote(full[5].at[y], landed.at[there], sends, recvs, sibling, 15 * count + step).start()

    def feed_land(step):
        y = lax.rem(at["y"] + step, 4)
        here, there = lax.div(y, 2), lax.rem(y, 2)

        @pl.when(here == core)
        def _():
            arrived(landed.at[there], 15 * count + step)
            out = down_half.at[(there, *REST[:3], slice(None), columns(1 - core))]
            pltpu.make_async_copy(landed.at[there], out, local.at[45 + step]).start()

    def feed_end(step):
        y = lax.rem(at["y"] + step, 4)
        here, there = lax.div(y, 2), lax.rem(y, 2)

        @pl.when(here == core)
        def _():
            out = down_half.at[(there, *REST[:3], slice(None), columns(core))]
            pltpu.make_async_copy(full[5].at[y], out, local.at[41 + step]).wait()
            out = down_half.at[(there, *REST[:3], slice(None), columns(1 - core))]
            pltpu.make_async_copy(landed.at[there], out, local.at[45 + step]).wait()

        @pl.when(here != core)
        def _():
            remote(
                full[5].at[y], landed.at[there], sends, recvs, sibling, 15 * count + step
            ).wait_send()

    for step in (0, 1, 3):
        feed_out(step)
    arrived(mix2, 13 * count + 3)

    def norm_two(c, rows):
        r = toks[c, rows, :] + (mix[c, rows, :] + mix2[c, rows, :])
        res[c, rows, :] = r
        hid2[c, rows, :] = (r * rms_inverse(r) * small[1:2, :]).astype(BF16)

    row_blocks(norm_two)
    hand_over(0, 2)
    for step in (0, 1, 3):
        feed_land(step)
    each(complete, FEED, 2)
    feed_out(2)
    feed_land(2)
    for step in range(4):
        feed_end(step)
    for copy in sent:
        copy.wait_send()
    for copy in kept:
        copy.wait()


def gather(shards, tok, cot):
    count = len(ARRAYS)
    hbm, vmem = pl.BlockSpec(memory_space=pl.ANY), pl.BlockSpec(memory_space=pltpu.VMEM)
    shape = jax.ShapeDtypeStruct
    pair = (2, ROWS, WIDTH)
    outs = [shape((*CHIPS, 16, HALF), BF16)] * 3 + [shape((2, 2, 2, 4, 2, 16, HALF), BF16)]
    outs += [shape((*CHIPS, *ARRAYS[k][0]), BF16) for k in (3, 4)]
    outs += [shape((2, 2, 4, 2, 72, WIDTH), BF16), shape(pair, F32), shape(pair, F32)]
    held = [
        shape(pair, F32),
        shape(pair, BF16),
        shape(pair, BF16),
        shape((2, ROWS, HALF), F32),
        shape((2, ROWS + 8, HALF), F32),
        shape((2, ROWS, HALF), F32),
        shape((2, ROWS + 8, HALF), F32),
        shape((2, ROWS, HALF), BF16),
        shape(pair, BF16),
    ]
    outs += held
    in_hbm = len(outs)
    outs += [shape((16, WIDTH), F32)]
    blocks = [pltpu.VMEM(array, BF16) for array, _ in ARRAYS]
    return pl.pallas_call(
        gather_kernel,
        out_shape=outs,
        in_specs=[vmem] * len(shards) + [hbm] * 2,
        out_specs=[hbm] * in_hbm + [vmem],
        scratch_shapes=[
            *blocks,
            *blocks,
            *blocks,
            pltpu.VMEM((72, WIDTH), F32),
            pltpu.VMEM((16, 128), F32),
            *[pltpu.VMEM((*CHIPS, *array), BF16) for array, _ in ARRAYS],
            *[pltpu.VMEM(pair, F32)] * 3,
            pltpu.VMEM((2, 2, 2, 4, 2, 16, HALF), BF16),
            pltpu.VMEM((2, 8, HALF), F32),
            pltpu.VMEM(pair, F32),
            pltpu.VMEM((2, 2, 4, 2, 72, HALF), BF16),
            *[pltpu.VMEM(value.shape, value.dtype) for value in held],
            pltpu.SemaphoreType.DMA((17 * count,)),
            pltpu.SemaphoreType.DMA((17 * count,)),
            pltpu.SemaphoreType.DMA((50,)),
        ],
        compiler_params=pltpu.CompilerParams(
            collective_id=0, has_side_effects=True, vmem_limit_bytes=60 * 2**20
        ),
        name="gather_and_mix",
    )(*shards, tok, cot)


def reduce_kernel(factor, *refs):
    count = len(ARRAYS)
    refs = list(refs)

    def take(n):
        taken = refs[:n]
        del refs[:n]
        return taken

    g_gate, g_up, g_down, d_hid2, out_part, in_hbm = *take(5), take(14)
    block_out, input_grad, in_grads, out_grads, gate_grads, up_grads, down_grads, small_grads = take(8)
    totals = take(count)
    data, arriving = take(count), take(12 * count)
    cot, res, hid1, b_mat, c_mat, x_mat, gated, y_mat, outw, small = held = take(10)
    dh, dh2, d1r, dres, g_out, halo, ffn_own, ffn_other = take(8)
    d_proj, (g_small, small_sum) = take(3), take(2)
    sends, recvs, local = refs
    at, core = position()
    sibling = device(at, 1 - core)
    arrive(at, core)
    sent = []

    def send(src, dst, target, sem):
        copy = remote(src, dst, sends, recvs, target, sem)
        copy.start()
        sent.append(copy)

    def arrived(ref, sem):
        remote(ref, ref, sends, recvs, sibling, sem).wait_recv()

    def load(src, dst, sem):
        copy = pltpu.make_async_copy(src, dst, local.at[sem])
        copy.start()
        return copy

    def buffer(k, phase, which):
        return arriving[12 * k + 4 * phase + which]

    def add(k, phase, where, sources, columns, total=None):
        sizes = sources[0].shape[:4]

        def body(t):
            i3 = lax.rem(t, sizes[3])
            t3 = lax.div(t, sizes[3])
            i2 = lax.rem(t3, sizes[2])
            t2 = lax.div(t3, sizes[2])
            i1 = lax.rem(t2, sizes[1])
            i0 = lax.div(t2, sizes[1])
            spot = tuple(i + b for i, b in zip((i0, i1, i2, i3), where))
            value = data[k][(*spot, slice(None), columns)].astype(F32)
            for source in sources:
                value = value + source[i0, i1, i2, i3].astype(F32)
            if total is None:
                data[k][(*spot, slice(None), columns)] = value.astype(BF16)
            else:
                total[...] = value

        steps(math.prod(sizes), body)

    def start_of(place, whole):
        y = 0 if "y" in whole else place["y"]
        z = 0 if "z" in whole else place["z"]
        if "x" in whole:
            return (y, 0, z, 0)
        return (y, lax.rem(place["x"], 2), z, lax.div(place["x"], 2))

    def begin(k, phase):
        (_, columns), order = ARRAYS[k]
        axis, whole = order[2 - phase], order[: 2 - phase]
        if phase == 2:
            for by, which in ((1, 0), (3, 1), (2, 2)):
                other = moved(at, axis, by)
                src = data[k].at[chip_index(other, whole)]
                send(src, buffer(k, 2, which), device(other, core), 12 * k + 8 + which)
            return
        across = chip_index(moved(at, axis, 2), whole)
        for part, which, by in zip(halves(columns), (0, 1), (1, 3)):
            send(
                data[k].at[(*across, slice(None), part)],
                buffer(k, phase, which),
                device(moved(at, axis, by), core),
                12 * k + 4 * phase + which,
            )

    def pass_on(k, phase):
        (_, columns), order = ARRAYS[k]
        axis, whole = order[2 - phase], order[: 2 - phase]
        base = 12 * k + 4 * phase
        for part, which, by in zip(halves(columns), (0, 1), (1, 3)):
            near = moved(at, axis, by)
            arrived(buffer(k, phase, which), base + which)
            add(k, phase, start_of(near, whole), [buffer(k, phase, which)], part)
            send(
                data[k].at[chip_index(near, whole)],
                buffer(k, phase, 2 + which),
                device(near, core),
                base + 2 + which,
            )

    def complete(k, phase):
        whole = ARRAYS[k][1][: 2 - phase]
        base = 12 * k + 4 * phase
        which = (0, 1, 2) if phase == 2 else (2, 3)
        both = [buffer(k, phase, w) for w in which]
        for w, source in zip(which, both):
            arrived(source, base + w)
        total = totals[k].at[core] if phase == 2 else None
        add(k, phase, start_of(at, whole), both, slice(None), total)
        if phase < 2:
            begin(k, phase + 1)
        else:
            send(total, total, sibling, 13 * count + k)

    def each(step, arrays, phase):
        for k in arrays:
            step(k, phase)

    def slab(step, action):
        y = lax.rem(at["y"] + step, 4)
        here, there = lax.div(y, 2), lax.rem(y, 2)

        def of(half):
            return g_down.at[(there, *REST[:3], slice(None), tile(half, HALF))]

        own = pltpu.make_async_copy(of(core), data[5].at[y], local.at[21 + step])
        given = remote(of(1 - core), data[5].at[y], sends, recvs, sibling, 15 * count + step)

        @pl.when(here == core)
        def _():
            if action == "load":
                own.start()
            elif action == "give":
                given.start()
            else:
                own.wait()

        @pl.when(here != core)
        def _():
            if action == "wait":
                given.wait_recv()

    def slab_sent(step):
        y = lax.rem(at["y"] + step, 4)
        there = lax.rem(y, 2)
        src = g_down.at[(there, *REST[:3], slice(None), tile(1 - core, HALF))]

        @pl.when(lax.div(y, 2) == core)
        def _():
            remote(src, data[5].at[y], sends, recvs, sibling, 15 * count + step).wait_send()

    ring = (2, 1, 3, 0)
    feed_loads = {}
    for step in ring:
        for k, src in ((3, g_gate), (4, g_up)):
            order = ARRAYS[k][1]
            spot = chip_index(moved(at, order[2], step), order[:2])
            feed_loads[k, step] = load(src.at[spot], data[k].at[spot], 25 + 4 * (k - 3) + step)
        slab(step, "load")
    first_loads = [load(d_hid2, dh, 6)]
    first_loads += [load(in_hbm[i], held[i], 7 + i) for i in (0, 1, 9)]
    rest_loads = [load(in_hbm[i], held[i], 7 + i) for i in range(2, 9)]
    left = slice(0, HALF)
    for k in MIXER:
        dst = data[k].at[(*REST, slice(None), left)]
        rest_loads.append(load(in_hbm[10 + k], dst, 17 + k))
    meet()
    slab(2, "give")
    for k in (3, 4):
        feed_loads[k, 2].wait()
        begin(k, 0)
    send(d_hid2, dh2, sibling, 12 * count)
    slab(2, "wait")
    begin(5, 0)
    for step in ring[1:]:
        slab(step, "give")
    send(out_part.at[1 - core], ffn_other, sibling, 12 * count + 2)
    ffn_load = load(out_part.at[core], ffn_own, 33)
    for copy in first_loads:
        copy.wait()
    arrived(dh2, 12 * count)
    g_small[...] = jnp.zeros_like(g_small)

    def norm_two(c, rows):
        r = res[c, rows, :]
        inv = rms_inverse(r)
        normed = r * inv
        d = dh[c, rows, :] + dh2[c, rows, :]
        g_small[1:2, :] += 0.5 * jnp.sum(d * normed, axis=0, keepdims=True)
        scaled = d * small[1:2, :]
        mean = jnp.mean(scaled * normed, axis=-1, keepdims=True)
        out = cot[c, rows, :] + inv * (scaled - normed * mean)
        cot[c, rows, :] = out
        dres[c, rows, :] = out.astype(BF16)

    row_blocks(norm_two)
    ffn_load.wait()
    arrived(ffn_other, 12 * count + 2)

    def add_ffn(i):
        rows = tile(i, 32)
        block_out[rows, :] = res[core, rows, :] + (ffn_own[rows, :] + ffn_other[rows, :])

    steps(ROWS // 32, add_ffn)
    tok_load = load(in_hbm[13], res, 20)
    for copy in rest_loads:
        copy.wait()

    taps = [small[2 + i : 3 + i, tile(core, HALF)] for i in range(3)]
    for c in range(2):
        for j in range(2):
            cols = slice(256 * j, 256 * j + 256)
            d_y = dot_t(dres[c, :, 0:HALF], flat(outw[0, j]))
            d_y = d_y + dot_t(dres[c, :, HALF:WIDTH], flat(outw[1, j]))
            conv = sum(taps[i][:, cols] * gated[c, 6 + i : 6 + i + ROWS, cols] for i in range(3))
            d_proj[1][c, :, cols] = (d_y * conv).astype(BF16)
            c_mat[c, 0:ROWS, cols] = d_y * c_mat[c, 0:ROWS, cols]
    send(c_mat.at[:, pl.ds(0, 8), :], halo, next_block(31), 12 * count + 3)
    for step in ring[1:]:
        feed_loads[3, step].wait()
        feed_loads[4, step].wait()
        slab(step, "wait")
    each(pass_on, FEED, 0)

    def out_grad(i):
        f = i
        for j in range(2):
            other = sum(
                t_dot(y_mat[c, :, tile(f)], dres[c, :, tile(2 - 2 * core + j)]) for c in range(2)
            )
            g_out[f, :, :, :, :, 256 * j : 256 * j + 256] = other.astype(BF16).reshape(
                2, 4, 2, 16, 256
            )
            own = sum(
                t_dot(y_mat[c, :, tile(f)], dres[c, :, tile(2 * core + j)]) for c in range(2)
            )
            data[1 + j][2 * core + f, :, :, :, :, HALF : HALF + 256] = own.astype(BF16).reshape(
                2, 4, 2, 16, 256
            )

    steps(2, out_grad)
    right = slice(HALF, HALF + 256)
    for j in range(2):
        send(
            g_out.at[(slice(None), *REST, slice(256 * j, 256 * j + 256))],
            data[1 + j].at[(pl.ds(2 * core, 2), *REST, right)],
            sibling,
            14 * count + j,
        )
    arrived(halo, 12 * count + 3)
    ends = lax.axis_index("seq") == 31
    for c in range(2):
        c_mat[c, ROWS : ROWS + 8, :] = jnp.where(ends, 0.0, halo[c])
        for r in range(0, ROWS, 64):
            d_conv = c_mat[c, r : r + 64, :]
            for i in range(3):
                part = jnp.sum(
                    d_conv * gated[c, r + 6 + i : r + 70 + i, :], axis=0, keepdims=True
                )
                g_small[2 + i : 3 + i, tile(core, HALF)] += part
            d_gated = taps[0] * c_mat[c, r + 2 : r + 66, :]
            d_gated = d_gated + taps[1] * c_mat[c, r + 1 : r + 65, :] + taps[2] * d_conv
            d_proj[0][c, r : r + 64, :] = (d_gated * x_mat[c, r : r + 64, :]).astype(BF16)
            d_proj[2][c, r : r + 64, :] = (d_gated * b_mat[c, r : r + 64, :]).astype(BF16)

    def back(i):
        c, y = lax.div(i, 4), lax.rem(i, 4)
        value = None
        for k in MIXER:
            part = dot_t(d_proj[k][c], flat(data[k][y, :, :, :, :, 0:HALF]))
            value = part if value is None else value + part
        dh[c, :, tile(y)] = value

    steps(8, back)
    send(dh.at[1 - core], d1r, sibling, 12 * count + 1)

    def in_grad(i):
        y, j = lax.div(i, 2), tile(lax.rem(i, 2))
        for k in MIXER:
            value = sum(t_dot(hid1[c, :, tile(y)], d_proj[k][c, :, j]) for c in range(2))
            data[k][y, :, :, :, :, j] = value.astype(BF16).reshape(2, 4, 2, 16, 256)

    steps(8, in_grad)
    tok_load.wait()

    def gain_one(c, rows):
        t = res[c, rows, :]
        g_small[0:1, :] += jnp.sum(dh[c, rows, :] * (t * rms_inverse(t)), axis=0, keepdims=True)

    row_blocks(gain_one)
    turned = t_dot(g_small[...].astype(BF16), picker()).astype(BF16)
    data[0][:, :, :, :, :, HALF : HALF + 128] = turned.reshape(*CHIPS, 16, 128)
    for j in range(2):
        arrived(data[1 + j].at[(pl.ds(2 - 2 * core, 2), *REST, right)], 14 * count + j)
    each(begin, MIXER, 0)
    each(complete, FEED, 0)
    each(pass_on, MIXER, 0)
    each(pass_on, FEED, 1)
    arrived(d1r, 12 * count + 1)

    def norm_one(i):
        rows = tile(i, 32)
        t = res[core, rows, :]
        inv = rms_inverse(t)
        normed = t * inv
        scaled = (dh[core, rows, :] + d1r[rows, :]) * small[0:1, :]
        mean = jnp.mean(scaled * normed, axis=-1, keepdims=True)
        input_grad[rows, :] = cot[core, rows, :] + inv * (scaled - normed * mean)

    steps(ROWS // 32, norm_one)
    each(complete, MIXER, 0)
    each(complete, FEED, 1)
    each(pass_on, MIXER, 1)
    each(complete, MIXER, 1)
    each(complete, FEED, 2)
    each(complete, MIXER, 2)
    for k in range(count):
        arrived(totals[k].at[1 - core], 13 * count + k)
    mine = pl.ds(pl.multiple_of(8 * core, 8), 8)
    for h in range(2):
        at_half = slice(HALF * h, HALF * h + HALF)
        for k in MIXER:
            in_grads[:, WIDTH * k + HALF * h : WIDTH * k + HALF * h + HALF] = (
                totals[k][h, mine, 0:HALF] * factor
            )
        for k in (1, 2):
            first = HALF * h + 256 * (k - 1)
            out_grads[:, first : first + 256] = totals[k][h, mine, HALF : HALF + 256] * factor
        for k, dst in ((3, gate_grads), (4, up_grads)):
            dst[:, 2304 * h : 2304 * h + 2304] = totals[k][h, mine, :] * factor
        down_grads[:, at_half] = factor * jnp.where(
            core == 0, totals[5][h, 0:36, :], totals[5][h, 36:72, :]
        )
    small_sum[...] = jnp.zeros_like(small_sum)
    small_sum[0:8, :] = factor * (
        totals[0][0, mine, HALF : HALF + 128] + totals[0][1, mine, HALF : HALF + 128]
    )
    small_grads[...] = small_sum[...].T[0:8, :]
    for step in ring:
        slab_sent(step)
    for copy in sent:
        copy.wait_send()


def reduce(factor, g_gate, g_up, g_down, d_hid2, out_part, *rest):
    count = len(ARRAYS)
    hbm, vmem = pl.BlockSpec(memory_space=pl.ANY), pl.BlockSpec(memory_space=pltpu.VMEM)
    buffers = []
    for (rows, columns), order in ARRAYS:
        for phase in range(3):
            whole = order[: 2 - phase]
            lead = (
                4 if "y" in whole else 1,
                2 if "x" in whole else 1,
                4 if "z" in whole else 1,
                2 if "x" in whole else 1,
            )
            if phase == 2:
                buffers += [pltpu.VMEM((*lead, rows, columns), BF16)] * 3
                buffers.append(pltpu.VMEM((16, 128), BF16))
                continue
            for part in halves(columns):
                buffers.append(pltpu.VMEM((*lead, rows, part.stop - part.start), BF16))
            buffers += [pltpu.VMEM((*lead, rows, columns), BF16)] * 2
    pair = pltpu.VMEM((2, ROWS, WIDTH), F32)
    operands = (g_gate, g_up, g_down, d_hid2, out_part, *rest)
    return pl.pallas_call(
        functools.partial(reduce_kernel, factor),
        out_shape=[
            jax.ShapeDtypeStruct(shape, F32)
            for shape in (
                (ROWS, WIDTH),
                (ROWS, WIDTH),
                (8, 3 * WIDTH),
                (8, WIDTH),
                (8, 4608),
                (8, 4608),
                (36, WIDTH),
                (8, 128),
            )
        ],
        in_specs=[hbm] * len(operands),
        out_specs=[vmem] * 8,
        scratch_shapes=[
            *[pltpu.VMEM((2, *shape), F32) for shape, _ in ARRAYS],
            *[pltpu.VMEM((*CHIPS, *shape), BF16) for shape, _ in ARRAYS],
            *buffers,
            *[pltpu.VMEM(value.shape, value.dtype) for value in rest[:10]],
            pair,
            pair,
            pltpu.VMEM((ROWS, WIDTH), F32),
            pltpu.VMEM((2, ROWS, WIDTH), BF16),
            pltpu.VMEM((2, 2, 4, 2, 16, HALF), BF16),
            pltpu.VMEM((2, 8, HALF), F32),
            pltpu.VMEM((ROWS, WIDTH), F32),
            pltpu.VMEM((ROWS, WIDTH), F32),
            *[pltpu.VMEM((2, ROWS, HALF), BF16)] * 3,
            pltpu.VMEM((16, WIDTH), F32),
            pltpu.VMEM((128, 128), F32),
            pltpu.SemaphoreType.DMA((16 * count,)),
            pltpu.SemaphoreType.DMA((16 * count,)),
            pltpu.SemaphoreType.DMA((34,)),
        ],
        compiler_params=pltpu.CompilerParams(
            collective_id=1, has_side_effects=True, vmem_limit_bytes=63 * 2**20
        ),
        name="sum_gradients",
    )(*operands)


def finish_kernel(*refs):
    count = (len(refs) - 5) // 2
    small, (one, taps, two) = refs[count], refs[2 * count + 1 : 2 * count + 4]
    copies = [
        pltpu.make_async_copy(refs[i], refs[count + 1 + i], refs[-1].at[i]) for i in range(count)
    ]
    for copy in copies:
        copy.start()
    one[...] = small[0:1, 0:8]
    two[...] = small[1:2, 0:8]
    taps[...] = small[2:5, 0:8]
    for copy in copies:
        copy.wait()


def finish(*values):
    hbm, vmem = pl.BlockSpec(memory_space=pl.ANY), pl.BlockSpec(memory_space=pltpu.VMEM)
    outs = [jax.ShapeDtypeStruct(v.shape, v.dtype) for v in values[:-1]]
    rows = [jax.ShapeDtypeStruct((r, 8), F32) for r in (1, 3, 1)]
    return pl.pallas_call(
        finish_kernel,
        out_shape=outs + rows,
        in_specs=[vmem] * len(values),
        out_specs=[hbm] * len(outs) + [vmem] * 3,
        scratch_shapes=[pltpu.SemaphoreType.DMA((len(values),))],
        name="finish",
    )(*values)


def shards(
    tokens,
    cotangent,
    norm1_gain,
    in_weight,
    conv_taps,
    out_weight,
    norm2_gain,
    gate_weight,
    up_weight,
    down_weight,
):
    width = tokens.shape[-1]
    inputs = tokens.reshape(-1, width)
    upstream = cotangent.reshape(-1, width)
    rows = inputs.shape[0]
    total_rows = rows * lax.axis_size("seq") * lax.axis_size("fsdp")
    factor = 1.0 / math.sqrt(total_rows)
    core = lax.rem(lax.axis_index("fsdp"), 2)

    pieces = (
        norm1_gain.reshape(1, -1),
        norm2_gain.reshape(1, -1),
        conv_taps,
        in_weight,
        out_weight,
        gate_weight,
        up_weight,
        down_weight,
    )
    w_b, w_c, w_x, w_out, w_gate, w_up, w_down, tok, cot, *kept = gather(pieces, inputs, upstream)
    resid, hidden_one, hidden_two, b_mat, c_mat, x_mat, gated, y_mat, cot_half, small = kept
    w_gate = w_gate.reshape(width, -1)
    w_up = w_up.reshape(width, -1)
    w_down = w_down.reshape(-1, width)
    hid2 = hidden_two.reshape(-1, width)
    gate, up_vals = dot(hid2, w_gate), dot(hid2, w_up)
    sigma = jax.nn.sigmoid(gate)
    act = (gate * sigma * up_vals).astype(BF16)
    out_part = dot(act, w_down)
    cot_half = cot_half.reshape(-1, width)
    g_down = t_dot(act, cot_half).astype(BF16)
    d_act = dot_t(cot_half, w_down)
    d_gate = (d_act * up_vals * sigma * (1.0 + gate * (1.0 - sigma))).astype(BF16)
    d_up = (d_act * gate * sigma).astype(BF16)
    g_gate = t_dot(hid2, d_gate).astype(BF16)
    g_up = t_dot(hid2, d_up).astype(BF16)
    d_hid2 = dot_t(d_gate, w_gate) + dot_t(d_up, w_up)
    block_out, input_grad, g_in, g_out, g_gate, g_up, g_down, g_small = reduce(
        factor,
        g_gate.reshape(*CHIPS, 16, 2304),
        g_up.reshape(*CHIPS, 16, 2304),
        g_down.reshape(2, 2, 4, 2, 72, width),
        d_hid2.reshape(2, rows, width),
        out_part.reshape(2, rows, width),
        cot,
        resid,
        hidden_one,
        b_mat,
        c_mat,
        x_mat,
        gated,
        y_mat,
        w_out,
        small,
        w_b,
        w_c,
        w_x,
        tok,
    )

    block_out, input_grad, g_in, g_out, g_gate, g_up, g_down, g_one, g_taps, g_two = finish(
        block_out, input_grad, g_in, g_out, g_gate, g_up, g_down, g_small
    )
    return (
        block_out.reshape(tokens.shape),
        input_grad.reshape(tokens.shape),
        g_one.reshape(-1),
        g_in,
        g_taps,
        g_out,
        g_two.reshape(-1),
        g_gate,
        g_up,
        g_down,
    )


def solution(mesh):
    tokens = P("fsdp", "seq", None)
    vector, matrix, taps = P(("seq", "fsdp")), P(("seq", "fsdp"), None), P(None, ("seq", "fsdp"))
    weights = (vector, matrix, taps, matrix, vector, matrix, matrix, matrix)
    return jax.shard_map(
        shards,
        mesh=mesh,
        in_specs=(tokens, tokens, *weights),
        out_specs=(tokens, tokens, *weights),
        check_vma=False,
    )
```

```python
import functools
import math

import jax
import jax.numpy as jnp
from jax import lax
from jax.experimental import pallas as pl
from jax.experimental.pallas import tpu as pltpu
from jax.sharding import PartitionSpec as P

norm_eps = 1e-05
MESH = pl.DeviceIdType.MESH
F32, BF16 = jnp.float32, jnp.bfloat16

CHIPS = (4, 2, 4, 2)
ARRAYS = (
    ((16, 640), "xyz"),
    ((16, 768), "yzx"),
    ((16, 768), "zxy"),
    ((16, 2304), "xyz"),
    ((16, 2304), "yzx"),
    ((72, 512), "zxy"),
)


def position():
    s, f = lax.axis_index("seq"), lax.axis_index("fsdp")
    y, x_lo, z = lax.div(s, 8), lax.rem(lax.div(s, 4), 2), lax.rem(s, 4)
    x_hi, core = lax.div(f, 2), lax.rem(f, 2)
    return {"x": x_hi * 2 + x_lo, "y": y, "z": z}, core


def device(at, core):
    x_lo, x_hi = lax.rem(at["x"], 2), lax.div(at["x"], 2)
    return ((at["y"] * 2 + x_lo) * 4 + at["z"], x_hi * 2 + core)


def moved(at, axis, by):
    return {**at, axis: lax.rem(at[axis] + by, 4)}


def chip_index(at, whole):
    y = slice(None) if "y" in whole else pl.ds(at["y"], 1)
    z = slice(None) if "z" in whole else pl.ds(at["z"], 1)
    if "x" in whole:
        x_lo = x_hi = slice(None)
    else:
        x_lo, x_hi = pl.ds(lax.rem(at["x"], 2), 1), pl.ds(lax.div(at["x"], 2), 1)
    return (y, x_lo, z, x_hi)


def halves(columns):
    first = (columns // 128 + 1) // 2 * 128
    return slice(0, first), slice(first, columns)


def arrive(at, core):
    barrier = pltpu.get_barrier_semaphore()
    for axis in "xyz":
        for by in (1, 2, 3):
            pl.semaphore_signal(
                barrier, inc=1, device_id=device(moved(at, axis, by), core), device_id_type=MESH
            )
    for other in (device(at, 1 - core), next_block(1), next_block(31)):
        pl.semaphore_signal(barrier, inc=1, device_id=other, device_id_type=MESH)


def meet():
    pl.semaphore_wait(pltpu.get_barrier_semaphore(), 12)


def next_block(by):
    return (lax.rem(lax.axis_index("seq") + by, 32), lax.axis_index("fsdp"))


def remote(src, dst, sends, recvs, target, sem):
    return pltpu.make_async_remote_copy(
        src_ref=src,
        dst_ref=dst,
        send_sem=sends.at[sem],
        recv_sem=recvs.at[sem],
        device_id=target,
        device_id_type=MESH,
    )


def dot(a, b):
    return jnp.dot(a, b, preferred_element_type=F32)


def dot_t(a, b):
    return lax.dot_general(a, b, (((1,), (1,)), ((), ())), preferred_element_type=F32)


def t_dot(a, b):
    return lax.dot_general(a, b, (((0,), (0,)), ((), ())), preferred_element_type=F32)


def flat(value):
    return value.reshape(-1, value.shape[-1])


def tile(j, size=256):
    return pl.ds(pl.multiple_of(j * size, size), size)


def rms_inverse(values):
    return lax.rsqrt(jnp.mean(values * values, axis=-1, keepdims=True) + norm_eps)


def steps(count, body):
    def run(i, carry):
        body(i)
        return carry

    lax.fori_loop(0, count, run, 0)


REST = (slice(None),) * 4
MIXER, FEED = (0, 1, 2), (3, 4, 5)
ROWS, WIDTH, HALF = 256, 1024, 512


def row_blocks(body, size=32):
    per = ROWS // size

    def run(i):
        body(lax.div(i, per), tile(lax.rem(i, per), size))

    steps(2 * per, run)


def picker():
    shape = (16, 128)
    same = lax.broadcasted_iota(jnp.int32, shape, 0) == lax.broadcasted_iota(jnp.int32, shape, 1)
    return jnp.where(same, 1.0, 0.0).astype(BF16)


def gather_kernel(*refs):
    count = len(ARRAYS)
    refs = list(refs)

    def take(n):
        taken = refs[:n]
        del refs[:n]
        return taken

    gain1, gain2, tap_rows, in_rows, out_rows, gate_rows, up_rows, down_rows, tok, cot = take(10)
    w_b, w_c, w_x, out_half, gate_full, up_full, down_half, tok_pair, cot_pair = take(9)
    results = take(9)
    (small,) = take(1)
    given, theirs, block = take(count), take(count), take(count)
    down32, small32 = take(2)
    full = take(count)
    toks, mix, mix2, outw, halo, cots, landed = take(7)
    res, hid1, hid2, b_mat, c_mat, x_mat, gated, y_mat, cot16 = held = take(9)
    sends, recvs, local = refs
    at, core = position()
    sibling = device(at, 1 - core)
    arrive(at, core)
    sent, kept = [], []

    def start(copy):
        copy.start()
        return copy

    def send(src, dst, target, sem):
        sent.append(start(remote(src, dst, sends, recvs, target, sem)))

    def arrived(ref, sem):
        remote(ref, ref, sends, recvs, sibling, sem).wait_recv()

    def keep(src, dst, sem):
        kept.append(start(pltpu.make_async_copy(src, dst, local.at[sem])))
        return kept[-1]

    down32[...] = jnp.zeros_like(down32)
    for c in range(2):

        @pl.when(core == c)
        def _():
            down32[36 * c : 36 * c + 36, :] = down_rows[...].astype(F32)

    small32[...] = jnp.zeros_like(small32)
    small32[0:1, 0:8] = gain1[...].astype(F32)
    small32[1:2, 0:8] = gain2[...].astype(F32)
    small32[2:5, 0:8] = tap_rows[...].astype(F32)
    small_rows = t_dot(small32[...].astype(BF16), picker())[0:8, :]

    def spread(rows):
        both = jnp.concatenate([rows.astype(F32)] * 2, axis=0)
        mine = lax.broadcasted_iota(jnp.int32, both.shape, 0) // 8 == core
        return jnp.where(mine, both, 0.0).astype(BF16)

    def fill(k, half, dst):
        def columns(ref, first, size):
            return ref[:, pl.ds(pl.multiple_of(first, 128), size)]

        if k < 3:
            dst[:, 0:HALF] = spread(columns(in_rows, k * WIDTH + half * HALF, HALF))
        if k == 0:
            dst[:, HALF : HALF + 128] = spread(small_rows)
        elif k < 3:
            dst[:, HALF : HALF + 256] = spread(
                columns(out_rows, half * HALF + 256 * (k - 1), 256)
            )
        elif k < 5:
            dst[...] = spread(columns(gate_rows if k == 3 else up_rows, half * 2304, 2304))
        else:
            dst[...] = columns(down32, half * HALF, HALF).astype(BF16)

    for k in range(count):
        fill(k, 1 - core, given[k])
        fill(k, core, block[k])
    meet()
    for k in range(count):
        send(given[k], theirs[k], sibling, 12 * count + k)
    own_copies = []
    here = (at["y"], lax.rem(at["x"], 2), at["z"], lax.div(at["x"], 2))
    for k in range(count):
        arrived(theirs[k], 12 * count + k)
        block[k][...] = block[k][...] + theirs[k][...]
        own_copies.append(
            start(pltpu.make_async_copy(block[k], full[k].at[here], local.at[k]))
        )
        for by, sem in ((1, 0), (3, 1), (2, 2)):
            send(
                block[k],
                full[k].at[here],
                device(moved(at, ARRAYS[k][1][0], by), core),
                12 * k + sem,
            )
    send(tok, toks.at[core], sibling, 13 * count)
    own_tok = start(pltpu.make_async_copy(tok, toks.at[core], local.at[count]))
    send(cot, cots.at[core], sibling, 13 * count + 1)
    own_cot = start(pltpu.make_async_copy(cot, cots.at[core], local.at[count + 1]))

    def piece_index(place, whole, late):
        spot = list(chip_index(place, whole))
        spot[0 if "y" in whole else 2] = pl.ds(2, 2) if late else pl.ds(0, 2)
        return tuple(spot)

    def begin_feed(late):
        for k in FEED:
            order = ARRAYS[k][1]
            mine = full[k].at[piece_index(at, order[:2], late)]
            for by, sem in ((1, 0), (3, 1)):
                index = 16 * count + 2 * (k - 3) + sem if late else 12 * k + 8 + sem
                send(mine, mine, device(moved(at, order[2], by), core), index)

    def pass_on(k, phase):
        (_, columns), order = ARRAYS[k]
        axis, whole, base = order[phase], order[:phase], 12 * k + 4 * phase
        right, left = moved(at, axis, 1), moved(at, axis, 3)
        for source, part, target, sem in zip((left, right), halves(columns), (right, left), (0, 1)):
            if phase == 2 and k in FEED:
                for late in range(2):
                    spot = piece_index(source, whole, late)
                    arrived(full[k].at[spot], 16 * count + 2 * (k - 3) + sem if late else base + sem)
            else:
                arrived(full[k].at[chip_index(source, whole)], base + sem)
            piece = full[k].at[(*chip_index(source, whole), slice(None), part)]
            send(piece, piece, device(target, core), base + 2 + sem)

    def complete(k, phase):
        (_, columns), order = ARRAYS[k]
        whole, base = order[:phase], 12 * k + 4 * phase
        if phase == 0:
            for by, sem in ((3, 0), (1, 1), (2, 2)):
                arrived(full[k].at[chip_index(moved(at, order[0], by), whole)], base + sem)
            own_copies[k].wait()
            return
        across = moved(at, order[phase], 2)
        for part, sem in zip(halves(columns), (2, 3)):
            arrived(full[k].at[(*chip_index(across, whole), slice(None), part)], base + sem)

    def begin(k, phase):
        order = ARRAYS[k][1]
        mine = full[k].at[chip_index(at, order[:phase])]
        for by, sem in ((1, 0), (3, 1)):
            send(mine, mine, device(moved(at, order[phase], by), core), 12 * k + 4 * phase + sem)

    def give_half(k, dst, columns, sem):
        mine = full[k].at[(pl.ds(2 * core, 2), *REST, columns)]
        other = full[k].at[(pl.ds(2 - 2 * core, 2), *REST, columns)]
        send(other, dst, sibling, sem)
        return start(pltpu.make_async_copy(mine, dst, local.at[10 + k]))

    def each(step, arrays, phase):
        for k in arrays:
            step(k, phase)

    each(complete, MIXER, 0)
    each(begin, MIXER, 1)
    each(complete, FEED, 0)
    each(begin, FEED, 1)
    each(pass_on, MIXER, 1)
    each(complete, MIXER, 1)
    each(pass_on, FEED, 1)
    each(begin, MIXER, 2)
    each(complete, FEED, 1)
    each(pass_on, MIXER, 2)
    begin_feed(False)
    each(complete, MIXER, 2)
    own_out = [
        give_half(
            k,
            outw.at[(core, *REST, slice(None), slice(256 * k - 256, 256 * k))],
            slice(HALF, HALF + 256),
            14 * count + k,
        )
        for k in (1, 2)
    ]
    own_cot.wait()
    arrived(cots.at[1 - core], 13 * count + 1)
    keep(cots, cot_pair, 23)

    def round_cot(c, rows):
        cot16[c, rows, :] = cots[c, rows, :].astype(BF16)

    row_blocks(round_cot)
    left = slice(0, 512)

    def hand_over(*which):
        for i in which:
            keep(held[i], results[i], 24 + i)

    hand_over(8)
    keep(full[0].at[(*REST, slice(None), left)], w_b, 18)
    keep(full[1].at[(*REST, slice(None), left)], w_c, 19)
    keep(full[2].at[(*REST, slice(None), left)], w_x, 20)

    small[...] = dot_t(picker(), flat(full[0][:, :, :, :, :, 512:640]))
    own_tok.wait()
    arrived(toks.at[1 - core], 13 * count)
    keep(toks, tok_pair, 21)

    def norm_one(c, rows):
        t = toks[c, rows, :]
        hid1[c, rows, :] = (t * rms_inverse(t) * small[0:1, :]).astype(BF16)

    row_blocks(norm_one)

    def project(i):
        c, j = lax.div(i, 2), tile(lax.rem(i, 2))
        h = hid1[c]
        b = dot(h, flat(full[0][:, :, :, :, :, j]))
        x = dot(h, flat(full[2][:, :, :, :, :, j]))
        b_mat[c, :, j] = b
        x_mat[c, :, j] = x
        gated[c, pl.ds(8, ROWS), j] = b * x
        c_mat[c, pl.ds(0, ROWS), j] = dot(h, flat(full[1][:, :, :, :, :, j]))

    steps(4, project)
    send(gated.at[:, pl.ds(ROWS, 8), :], halo, next_block(1), 13 * count + 4)
    begin_feed(True)
    hand_over(1, 3, 4, 5)
    arrived(halo, 13 * count + 4)
    each(pass_on, FEED, 2)
    starts = lax.axis_index("seq") == 0
    taps = [small[2 + i : 3 + i, tile(core, HALF)] for i in range(3)]
    for c in range(2):
        gated[c, 0:8, :] = jnp.where(starts, 0.0, halo[c])
        for r in range(0, ROWS, 64):
            conv = taps[0] * gated[c, r + 6 : r + 70, :]
            conv = conv + taps[1] * gated[c, r + 7 : r + 71, :]
            conv = conv + taps[2] * gated[c, r + 8 : r + 72, :]
            y_mat[c, r : r + 64, :] = (c_mat[c, r : r + 64, :] * conv).astype(BF16)

    hand_over(6, 7)

    for k in (1, 2):
        own_out[k - 1].wait()
        part = (1 - core, *REST, slice(None), slice(256 * k - 256, 256 * k))
        arrived(outw.at[part], 14 * count + k)
    keep(outw, out_half, 22)

    def mixing(i):
        c, h, j = lax.div(i, 4), lax.rem(lax.div(i, 2), 2), lax.rem(i, 2)
        weight = outw[h, :, :, :, :, :, tile(j)]
        mix[c, :, tile(2 * h + j)] = dot(y_mat[c], flat(weight))

    steps(8, mixing)
    send(mix, mix2, sibling, 13 * count + 3)

    def columns(half):
        return tile(half, HALF)

    def feed_out(step):
        for k, dst in ((3, gate_full), (4, up_full)):
            order = ARRAYS[k][1]
            spot = chip_index(moved(at, order[2], step), order[:2])
            keep(full[k].at[spot], dst.at[spot], 33 + 4 * (k - 3) + step)
        y = lax.rem(at["y"] + step, 4)
        here, there = lax.div(y, 2), lax.rem(y, 2)

        @pl.when(here == core)
        def _():
            out = down_half.at[(there, *REST[:3], slice(None), columns(core))]
            pltpu.make_async_copy(full[5].at[y], out, local.at[41 + step]).start()

        @pl.when(here != core)
        def _():
            remote(full[5].at[y], landed.at[there], sends, recvs, sibling, 15 * count + step).start()

    def feed_land(step):
        y = lax.rem(at["y"] + step, 4)
        here, there = lax.div(y, 2), lax.rem(y, 2)

        @pl.when(here == core)
        def _():
            arrived(landed.at[there], 15 * count + step)
            out = down_half.at[(there, *REST[:3], slice(None), columns(1 - core))]
            pltpu.make_async_copy(landed.at[there], out, local.at[45 + step]).start()

    def feed_end(step):
        y = lax.rem(at["y"] + step, 4)
        here, there = lax.div(y, 2), lax.rem(y, 2)

        @pl.when(here == core)
        def _():
            out = down_half.at[(there, *REST[:3], slice(None), columns(core))]
            pltpu.make_async_copy(full[5].at[y], out, local.at[41 + step]).wait()
            out = down_half.at[(there, *REST[:3], slice(None), columns(1 - core))]
            pltpu.make_async_copy(landed.at[there], out, local.at[45 + step]).wait()

        @pl.when(here != core)
        def _():
            remote(
                full[5].at[y], landed.at[there], sends, recvs, sibling, 15 * count + step
            ).wait_send()

    for step in (0, 1, 3):
        feed_out(step)
    arrived(mix2, 13 * count + 3)

    def norm_two(c, rows):
        r = toks[c, rows, :] + (mix[c, rows, :] + mix2[c, rows, :])
        res[c, rows, :] = r
        hid2[c, rows, :] = (r * rms_inverse(r) * small[1:2, :]).astype(BF16)

    row_blocks(norm_two)
    hand_over(0, 2)
    for step in (0, 1, 3):
        feed_land(step)
    each(complete, FEED, 2)
    feed_out(2)
    feed_land(2)
    for step in range(4):
        feed_end(step)
    for copy in sent:
        copy.wait_send()
    for copy in kept:
        copy.wait()


def gather(shards, tok, cot):
    count = len(ARRAYS)
    hbm, vmem = pl.BlockSpec(memory_space=pl.ANY), pl.BlockSpec(memory_space=pltpu.VMEM)
    shape = jax.ShapeDtypeStruct
    pair = (2, ROWS, WIDTH)
    outs = [shape((*CHIPS, 16, HALF), BF16)] * 3 + [shape((2, 2, 2, 4, 2, 16, HALF), BF16)]
    outs += [shape((*CHIPS, *ARRAYS[k][0]), BF16) for k in (3, 4)]
    outs += [shape((2, 2, 4, 2, 72, WIDTH), BF16), shape(pair, F32), shape(pair, F32)]
    held = [
        shape(pair, F32),
        shape(pair, BF16),
        shape(pair, BF16),
        shape((2, ROWS, HALF), F32),
        shape((2, ROWS + 8, HALF), F32),
        shape((2, ROWS, HALF), F32),
        shape((2, ROWS + 8, HALF), F32),
        shape((2, ROWS, HALF), BF16),
        shape(pair, BF16),
    ]
    outs += held
    in_hbm = len(outs)
    outs += [shape((16, WIDTH), F32)]
    blocks = [pltpu.VMEM(array, BF16) for array, _ in ARRAYS]
    return pl.pallas_call(
        gather_kernel,
        out_shape=outs,
        in_specs=[vmem] * len(shards) + [hbm] * 2,
        out_specs=[hbm] * in_hbm + [vmem],
        scratch_shapes=[
            *blocks,
            *blocks,
            *blocks,
            pltpu.VMEM((72, WIDTH), F32),
            pltpu.VMEM((16, 128), F32),
            *[pltpu.VMEM((*CHIPS, *array), BF16) for array, _ in ARRAYS],
            *[pltpu.VMEM(pair, F32)] * 3,
            pltpu.VMEM((2, 2, 2, 4, 2, 16, HALF), BF16),
            pltpu.VMEM((2, 8, HALF), F32),
            pltpu.VMEM(pair, F32),
            pltpu.VMEM((2, 2, 4, 2, 72, HALF), BF16),
            *[pltpu.VMEM(value.shape, value.dtype) for value in held],
            pltpu.SemaphoreType.DMA((17 * count,)),
            pltpu.SemaphoreType.DMA((17 * count,)),
            pltpu.SemaphoreType.DMA((50,)),
        ],
        compiler_params=pltpu.CompilerParams(
            collective_id=0, has_side_effects=True, vmem_limit_bytes=60 * 2**20
        ),
        name="gather_and_mix",
    )(*shards, tok, cot)


def reduce_kernel(factor, *refs):
    count = len(ARRAYS)
    refs = list(refs)

    def take(n):
        taken = refs[:n]
        del refs[:n]
        return taken

    g_gate, g_up, g_down, d_hid2, out_part, in_hbm = *take(5), take(14)
    block_out, input_grad, in_grads, out_grads, gate_grads, up_grads, down_grads, small_grads = take(8)
    totals = take(count)
    data, arriving = take(count), take(12 * count)
    cot, res, hid1, b_mat, c_mat, x_mat, gated, y_mat, outw, small = held = take(10)
    dh, dh2, d1r, dres, g_out, halo, ffn_own, ffn_other = take(8)
    d_proj, (g_small, small_sum) = take(3), take(2)
    sends, recvs, local = refs
    at, core = position()
    sibling = device(at, 1 - core)
    arrive(at, core)
    sent = []

    def send(src, dst, target, sem):
        copy = remote(src, dst, sends, recvs, target, sem)
        copy.start()
        sent.append(copy)

    def arrived(ref, sem):
        remote(ref, ref, sends, recvs, sibling, sem).wait_recv()

    def load(src, dst, sem):
        copy = pltpu.make_async_copy(src, dst, local.at[sem])
        copy.start()
        return copy

    def buffer(k, phase, which):
        return arriving[12 * k + 4 * phase + which]

    def add(k, phase, where, sources, columns, total=None):
        sizes = sources[0].shape[:4]

        def body(t):
            i3 = lax.rem(t, sizes[3])
            t3 = lax.div(t, sizes[3])
            i2 = lax.rem(t3, sizes[2])
            t2 = lax.div(t3, sizes[2])
            i1 = lax.rem(t2, sizes[1])
            i0 = lax.div(t2, sizes[1])
            spot = tuple(i + b for i, b in zip((i0, i1, i2, i3), where))
            value = data[k][(*spot, slice(None), columns)].astype(F32)
            for source in sources:
                value = value + source[i0, i1, i2, i3].astype(F32)
            if total is None:
                data[k][(*spot, slice(None), columns)] = value.astype(BF16)
            else:
                total[...] = value

        steps(math.prod(sizes), body)

    def start_of(place, whole):
        y = 0 if "y" in whole else place["y"]
        z = 0 if "z" in whole else place["z"]
        if "x" in whole:
            return (y, 0, z, 0)
        return (y, lax.rem(place["x"], 2), z, lax.div(place["x"], 2))

    def begin(k, phase):
        (_, columns), order = ARRAYS[k]
        axis, whole = order[2 - phase], order[: 2 - phase]
        if phase == 2:
            for by, which in ((1, 0), (3, 1), (2, 2)):
                other = moved(at, axis, by)
                src = data[k].at[chip_index(other, whole)]
                send(src, buffer(k, 2, which), device(other, core), 12 * k + 8 + which)
            return
        across = chip_index(moved(at, axis, 2), whole)
        for part, which, by in zip(halves(columns), (0, 1), (1, 3)):
            send(
                data[k].at[(*across, slice(None), part)],
                buffer(k, phase, which),
                device(moved(at, axis, by), core),
                12 * k + 4 * phase + which,
            )

    def pass_on(k, phase):
        (_, columns), order = ARRAYS[k]
        axis, whole = order[2 - phase], order[: 2 - phase]
        base = 12 * k + 4 * phase
        for part, which, by in zip(halves(columns), (0, 1), (1, 3)):
            near = moved(at, axis, by)
            arrived(buffer(k, phase, which), base + which)
            add(k, phase, start_of(near, whole), [buffer(k, phase, which)], part)
            send(
                data[k].at[chip_index(near, whole)],
                buffer(k, phase, 2 + which),
                device(near, core),
                base + 2 + which,
            )

    def complete(k, phase):
        whole = ARRAYS[k][1][: 2 - phase]
        base = 12 * k + 4 * phase
        which = (0, 1, 2) if phase == 2 else (2, 3)
        both = [buffer(k, phase, w) for w in which]
        for w, source in zip(which, both):
            arrived(source, base + w)
        total = totals[k].at[core] if phase == 2 else None
        add(k, phase, start_of(at, whole), both, slice(None), total)
        if phase < 2:
            begin(k, phase + 1)
        else:
            send(total, total, sibling, 13 * count + k)

    def each(step, arrays, phase):
        for k in arrays:
            step(k, phase)

    def slab(step, action):
        y = lax.rem(at["y"] + step, 4)
        here, there = lax.div(y, 2), lax.rem(y, 2)

        def of(half):
            return g_down.at[(there, *REST[:3], slice(None), tile(half, HALF))]

        own = pltpu.make_async_copy(of(core), data[5].at[y], local.at[21 + step])
        given = remote(of(1 - core), data[5].at[y], sends, recvs, sibling, 15 * count + step)

        @pl.when(here == core)
        def _():
            if action == "load":
                own.start()
            elif action == "give":
                given.start()
            else:
                own.wait()

        @pl.when(here != core)
        def _():
            if action == "wait":
                given.wait_recv()

    def slab_sent(step):
        y = lax.rem(at["y"] + step, 4)
        there = lax.rem(y, 2)
        src = g_down.at[(there, *REST[:3], slice(None), tile(1 - core, HALF))]

        @pl.when(lax.div(y, 2) == core)
        def _():
            remote(src, data[5].at[y], sends, recvs, sibling, 15 * count + step).wait_send()

    ring = (2, 1, 3, 0)
    feed_loads = {}
    for step in ring:
        for k, src in ((3, g_gate), (4, g_up)):
            order = ARRAYS[k][1]
            spot = chip_index(moved(at, order[2], step), order[:2])
            feed_loads[k, step] = load(src.at[spot], data[k].at[spot], 25 + 4 * (k - 3) + step)
        slab(step, "load")
    first_loads = [load(d_hid2, dh, 6)]
    first_loads += [load(in_hbm[i], held[i], 7 + i) for i in (0, 1, 9)]
    rest_loads = [load(in_hbm[i], held[i], 7 + i) for i in range(2, 9)]
    left = slice(0, HALF)
    for k in MIXER:
        dst = data[k].at[(*REST, slice(None), left)]
        rest_loads.append(load(in_hbm[10 + k], dst, 17 + k))
    meet()
    slab(2, "give")
    for k in (3, 4):
        feed_loads[k, 2].wait()
        begin(k, 0)
    send(d_hid2, dh2, sibling, 12 * count)
    slab(2, "wait")
    begin(5, 0)
    for step in ring[1:]:
        slab(step, "give")
    send(out_part.at[1 - core], ffn_other, sibling, 12 * count + 2)
    ffn_load = load(out_part.at[core], ffn_own, 33)
    for copy in first_loads:
        copy.wait()
    arrived(dh2, 12 * count)
    g_small[...] = jnp.zeros_like(g_small)

    def norm_two(c, rows):
        r = res[c, rows, :]
        inv = rms_inverse(r)
        normed = r * inv
        d = dh[c, rows, :] + dh2[c, rows, :]
        g_small[1:2, :] += 0.5 * jnp.sum(d * normed, axis=0, keepdims=True)
        scaled = d * small[1:2, :]
        mean = jnp.mean(scaled * normed, axis=-1, keepdims=True)
        out = cot[c, rows, :] + inv * (scaled - normed * mean)
        cot[c, rows, :] = out
        dres[c, rows, :] = out.astype(BF16)

    row_blocks(norm_two)
    ffn_load.wait()
    arrived(ffn_other, 12 * count + 2)

    def add_ffn(i):
        rows = tile(i, 32)
        block_out[rows, :] = res[core, rows, :] + (ffn_own[rows, :] + ffn_other[rows, :])

    steps(ROWS // 32, add_ffn)
    tok_load = load(in_hbm[13], res, 20)
    for copy in rest_loads:
        copy.wait()

    taps = [small[2 + i : 3 + i, tile(core, HALF)] for i in range(3)]
    for c in range(2):
        for j in range(2):
            cols = slice(256 * j, 256 * j + 256)
            d_y = dot_t(dres[c, :, 0:HALF], flat(outw[0, j]))
            d_y = d_y + dot_t(dres[c, :, HALF:WIDTH], flat(outw[1, j]))
            conv = sum(taps[i][:, cols] * gated[c, 6 + i : 6 + i + ROWS, cols] for i in range(3))
            d_proj[1][c, :, cols] = (d_y * conv).astype(BF16)
            c_mat[c, 0:ROWS, cols] = d_y * c_mat[c, 0:ROWS, cols]
    send(c_mat.at[:, pl.ds(0, 8), :], halo, next_block(31), 12 * count + 3)
    for step in ring[1:]:
        feed_loads[3, step].wait()
        feed_loads[4, step].wait()
        slab(step, "wait")
    each(pass_on, FEED, 0)

    def out_grad(i):
        f = i
        for j in range(2):
            other = sum(
                t_dot(y_mat[c, :, tile(f)], dres[c, :, tile(2 - 2 * core + j)]) for c in range(2)
            )
            g_out[f, :, :, :, :, 256 * j : 256 * j + 256] = other.astype(BF16).reshape(
                2, 4, 2, 16, 256
            )
            own = sum(
                t_dot(y_mat[c, :, tile(f)], dres[c, :, tile(2 * core + j)]) for c in range(2)
            )
            data[1 + j][2 * core + f, :, :, :, :, HALF : HALF + 256] = own.astype(BF16).reshape(
                2, 4, 2, 16, 256
            )

    steps(2, out_grad)
    right = slice(HALF, HALF + 256)
    for j in range(2):
        send(
            g_out.at[(slice(None), *REST, slice(256 * j, 256 * j + 256))],
            data[1 + j].at[(pl.ds(2 * core, 2), *REST, right)],
            sibling,
            14 * count + j,
        )
    arrived(halo, 12 * count + 3)
    ends = lax.axis_index("seq") == 31
    for c in range(2):
        c_mat[c, ROWS : ROWS + 8, :] = jnp.where(ends, 0.0, halo[c])
        for r in range(0, ROWS, 64):
            d_conv = c_mat[c, r : r + 64, :]
            for i in range(3):
                part = jnp.sum(
                    d_conv * gated[c, r + 6 + i : r + 70 + i, :], axis=0, keepdims=True
                )
                g_small[2 + i : 3 + i, tile(core, HALF)] += part
            d_gated = taps[0] * c_mat[c, r + 2 : r + 66, :]
            d_gated = d_gated + taps[1] * c_mat[c, r + 1 : r + 65, :] + taps[2] * d_conv
            d_proj[0][c, r : r + 64, :] = (d_gated * x_mat[c, r : r + 64, :]).astype(BF16)
            d_proj[2][c, r : r + 64, :] = (d_gated * b_mat[c, r : r + 64, :]).astype(BF16)

    def back(i):
        c, y = lax.div(i, 4), lax.rem(i, 4)
        value = None
        for k in MIXER:
            part = dot_t(d_proj[k][c], flat(data[k][y, :, :, :, :, 0:HALF]))
            value = part if value is None else value + part
        dh[c, :, tile(y)] = value

    steps(8, back)
    send(dh.at[1 - core], d1r, sibling, 12 * count + 1)

    def in_grad(i):
        y, j = lax.div(i, 2), tile(lax.rem(i, 2))
        for k in MIXER:
            value = sum(t_dot(hid1[c, :, tile(y)], d_proj[k][c, :, j]) for c in range(2))
            data[k][y, :, :, :, :, j] = value.astype(BF16).reshape(2, 4, 2, 16, 256)

    steps(8, in_grad)
    tok_load.wait()

    def gain_one(c, rows):
        t = res[c, rows, :]
        g_small[0:1, :] += jnp.sum(dh[c, rows, :] * (t * rms_inverse(t)), axis=0, keepdims=True)

    row_blocks(gain_one)
    turned = t_dot(g_small[...].astype(BF16), picker()).astype(BF16)
    data[0][:, :, :, :, :, HALF : HALF + 128] = turned.reshape(*CHIPS, 16, 128)
    for j in range(2):
        arrived(data[1 + j].at[(pl.ds(2 - 2 * core, 2), *REST, right)], 14 * count + j)
    each(begin, MIXER, 0)
    each(complete, FEED, 0)
    each(pass_on, MIXER, 0)
    each(pass_on, FEED, 1)
    arrived(d1r, 12 * count + 1)

    def norm_one(i):
        rows = tile(i, 32)
        t = res[core, rows, :]
        inv = rms_inverse(t)
        normed = t * inv
        scaled = (dh[core, rows, :] + d1r[rows, :]) * small[0:1, :]
        mean = jnp.mean(scaled * normed, axis=-1, keepdims=True)
        input_grad[rows, :] = cot[core, rows, :] + inv * (scaled - normed * mean)

    steps(ROWS // 32, norm_one)
    each(complete, MIXER, 0)
    each(complete, FEED, 1)
    each(pass_on, MIXER, 1)
    each(complete, MIXER, 1)
    each(complete, FEED, 2)
    each(complete, MIXER, 2)
    for k in range(count):
        arrived(totals[k].at[1 - core], 13 * count + k)
    mine = pl.ds(pl.multiple_of(8 * core, 8), 8)
    for h in range(2):
        at_half = slice(HALF * h, HALF * h + HALF)
        for k in MIXER:
            in_grads[:, WIDTH * k + HALF * h : WIDTH * k + HALF * h + HALF] = (
                totals[k][h, mine, 0:HALF] * factor
            )
        for k in (1, 2):
            first = HALF * h + 256 * (k - 1)
            out_grads[:, first : first + 256] = totals[k][h, mine, HALF : HALF + 256] * factor
        for k, dst in ((3, gate_grads), (4, up_grads)):
            dst[:, 2304 * h : 2304 * h + 2304] = totals[k][h, mine, :] * factor
        down_grads[:, at_half] = factor * jnp.where(
            core == 0, totals[5][h, 0:36, :], totals[5][h, 36:72, :]
        )
    small_sum[...] = jnp.zeros_like(small_sum)
    small_sum[0:8, :] = factor * (
        totals[0][0, mine, HALF : HALF + 128] + totals[0][1, mine, HALF : HALF + 128]
    )
    small_grads[...] = small_sum[...].T[0:8, :]
    for step in ring:
        slab_sent(step)
    for copy in sent:
        copy.wait_send()


def reduce(factor, g_gate, g_up, g_down, d_hid2, out_part, *rest):
    count = len(ARRAYS)
    hbm, vmem = pl.BlockSpec(memory_space=pl.ANY), pl.BlockSpec(memory_space=pltpu.VMEM)
    buffers = []
    for (rows, columns), order in ARRAYS:
        for phase in range(3):
            whole = order[: 2 - phase]
            lead = (
                4 if "y" in whole else 1,
                2 if "x" in whole else 1,
                4 if "z" in whole else 1,
                2 if "x" in whole else 1,
            )
            if phase == 2:
                buffers += [pltpu.VMEM((*lead, rows, columns), BF16)] * 3
                buffers.append(pltpu.VMEM((16, 128), BF16))
                continue
            for part in halves(columns):
                buffers.append(pltpu.VMEM((*lead, rows, part.stop - part.start), BF16))
            buffers += [pltpu.VMEM((*lead, rows, columns), BF16)] * 2
    pair = pltpu.VMEM((2, ROWS, WIDTH), F32)
    operands = (g_gate, g_up, g_down, d_hid2, out_part, *rest)
    return pl.pallas_call(
        functools.partial(reduce_kernel, factor),
        out_shape=[
            jax.ShapeDtypeStruct(shape, F32)
            for shape in (
                (ROWS, WIDTH),
                (ROWS, WIDTH),
                (8, 3 * WIDTH),
                (8, WIDTH),
                (8, 4608),
                (8, 4608),
                (36, WIDTH),
                (8, 128),
            )
        ],
        in_specs=[hbm] * len(operands),
        out_specs=[vmem] * 8,
        scratch_shapes=[
            *[pltpu.VMEM((2, *shape), F32) for shape, _ in ARRAYS],
            *[pltpu.VMEM((*CHIPS, *shape), BF16) for shape, _ in ARRAYS],
            *buffers,
            *[pltpu.VMEM(value.shape, value.dtype) for value in rest[:10]],
            pair,
            pair,
            pltpu.VMEM((ROWS, WIDTH), F32),
            pltpu.VMEM((2, ROWS, WIDTH), BF16),
            pltpu.VMEM((2, 2, 4, 2, 16, HALF), BF16),
            pltpu.VMEM((2, 8, HALF), F32),
            pltpu.VMEM((ROWS, WIDTH), F32),
            pltpu.VMEM((ROWS, WIDTH), F32),
            *[pltpu.VMEM((2, ROWS, HALF), BF16)] * 3,
            pltpu.VMEM((16, WIDTH), F32),
            pltpu.VMEM((128, 128), F32),
            pltpu.SemaphoreType.DMA((16 * count,)),
            pltpu.SemaphoreType.DMA((16 * count,)),
            pltpu.SemaphoreType.DMA((34,)),
        ],
        compiler_params=pltpu.CompilerParams(
            collective_id=1, has_side_effects=True, vmem_limit_bytes=63 * 2**20
        ),
        name="sum_gradients",
    )(*operands)


def finish_kernel(*refs):
    count = (len(refs) - 5) // 2
    small, (one, taps, two) = refs[count], refs[2 * count + 1 : 2 * count + 4]
    copies = [
        pltpu.make_async_copy(refs[i], refs[count + 1 + i], refs[-1].at[i]) for i in range(count)
    ]
    for copy in copies:
        copy.start()
    one[...] = small[0:1, 0:8]
    two[...] = small[1:2, 0:8]
    taps[...] = small[2:5, 0:8]
    for copy in copies:
        copy.wait()


def finish(*values):
    hbm, vmem = pl.BlockSpec(memory_space=pl.ANY), pl.BlockSpec(memory_space=pltpu.VMEM)
    outs = [jax.ShapeDtypeStruct(v.shape, v.dtype) for v in values[:-1]]
    rows = [jax.ShapeDtypeStruct((r, 8), F32) for r in (1, 3, 1)]
    return pl.pallas_call(
        finish_kernel,
        out_shape=outs + rows,
        in_specs=[vmem] * len(values),
        out_specs=[hbm] * len(outs) + [vmem] * 3,
        scratch_shapes=[pltpu.SemaphoreType.DMA((len(values),))],
        name="finish",
    )(*values)


def shards(
    tokens,
    cotangent,
    norm1_gain,
    in_weight,
    conv_taps,
    out_weight,
    norm2_gain,
    gate_weight,
    up_weight,
    down_weight,
):
    width = tokens.shape[-1]
    inputs = tokens.reshape(-1, width)
    upstream = cotangent.reshape(-1, width)
    rows = inputs.shape[0]
    total_rows = rows * lax.axis_size("seq") * lax.axis_size("fsdp")
    factor = 1.0 / math.sqrt(total_rows)
    core = lax.rem(lax.axis_index("fsdp"), 2)

    pieces = (
        norm1_gain.reshape(1, -1),
        norm2_gain.reshape(1, -1),
        conv_taps,
        in_weight,
        out_weight,
        gate_weight,
        up_weight,
        down_weight,
    )
    w_b, w_c, w_x, w_out, w_gate, w_up, w_down, tok, cot, *kept = gather(pieces, inputs, upstream)
    resid, hidden_one, hidden_two, b_mat, c_mat, x_mat, gated, y_mat, cot_half, small = kept
    w_gate = w_gate.reshape(width, -1)
    w_up = w_up.reshape(width, -1)
    w_down = w_down.reshape(-1, width)
    hid2 = hidden_two.reshape(-1, width)
    gate, up_vals = dot(hid2, w_gate), dot(hid2, w_up)
    sigma = jax.nn.sigmoid(gate)
    act = (gate * sigma * up_vals).astype(BF16)
    out_part = dot(act, w_down)
    cot_half = cot_half.reshape(-1, width)
    g_down = t_dot(act, cot_half).astype(BF16)
    d_act = dot_t(cot_half, w_down)
    d_gate = (d_act * up_vals * sigma * (1.0 + gate * (1.0 - sigma))).astype(BF16)
    d_up = (d_act * gate * sigma).astype(BF16)
    g_gate = t_dot(hid2, d_gate).astype(BF16)
    g_up = t_dot(hid2, d_up).astype(BF16)
    d_hid2 = dot_t(d_gate, w_gate) + dot_t(d_up, w_up)
    block_out, input_grad, g_in, g_out, g_gate, g_up, g_down, g_small = reduce(
        factor,
        g_gate.reshape(*CHIPS, 16, 2304),
        g_up.reshape(*CHIPS, 16, 2304),
        g_down.reshape(2, 2, 4, 2, 72, width),
        d_hid2.reshape(2, rows, width),
        out_part.reshape(2, rows, width),
        cot,
        resid,
        hidden_one,
        b_mat,
        c_mat,
        x_mat,
        gated,
        y_mat,
        w_out,
        small,
        w_b,
        w_c,
        w_x,
        tok,
    )

    block_out, input_grad, g_in, g_out, g_gate, g_up, g_down, g_one, g_taps, g_two = finish(
        block_out, input_grad, g_in, g_out, g_gate, g_up, g_down, g_small
    )
    return (
        block_out.reshape(tokens.shape),
        input_grad.reshape(tokens.shape),
        g_one.reshape(-1),
        g_in,
        g_taps,
        g_out,
        g_two.reshape(-1),
        g_gate,
        g_up,
        g_down,
    )


def solution(mesh):
    tokens = P("fsdp", "seq", None)
    vector, matrix, taps = P(("seq", "fsdp")), P(("seq", "fsdp"), None), P(None, ("seq", "fsdp"))
    weights = (vector, matrix, taps, matrix, vector, matrix, matrix, matrix)
    return jax.shard_map(
        shards,
        mesh=mesh,
        in_specs=(tokens, tokens, *weights),
        out_specs=(tokens, tokens, *weights),
        check_vma=False,
    )
```
